256 devices in a mesh: var: 32 (over y_hi, z, core), tok: 8 (over y_lo, x).
Axes of the slice: x: 4, y: 4 (y_hi: 2, y_lo: 2; y = y_hi * 2 + y_lo), z: 8, core: 2. Of those that a mesh axis runs over, the one named last changes fastest.
Arguments:
- patches: bfloat16 [64, 16, 4096], P('var', 'tok'), may hold values from -6 to 6
- embed_w: bfloat16 [64, 16, 1024], P('var'), may hold values from -1.5 to 1.5
- embed_b: bfloat16 [64, 1024], P('var'), may hold values from -3 to 3
- query: bfloat16 [1024], replicated, may hold values from -64 to 64
- kv_w: bfloat16 [1024, 2048], replicated, may hold values from -0.1875 to 0.1875
- out_w: bfloat16 [1024, 1024], replicated, may hold values from -0.1875 to 0.1875
- cotangent: bfloat16 [16, 256, 1024], P('tok', 'var'), may hold values from -0.08984375 to 0.08984375
Outputs:
- aggregated: bfloat16 [16, 256, 1024], P('tok', 'var')
- grad_kv: float32 [1024, 2048], P(('var', 'tok'))
- grad_embed_w: float32 [64, 16, 1024], P('var')
- grad_embed_b: float32 [64, 1024], P('var')
The draws below stay inside these ranges and needn't reach their ends.
All inputs are finite; a program needn't handle non-finite values.
Results may differ from the reference program's by a relative error of at most 0.013.
The reference program's roundings to bfloat16 on the way (of `embedded`, `keyvals`, `weights`, `context`, `context_grad`, `value_grad`, `key_grad` and `embedded_grad`) count: a program that leaves them out, or rounds other values in their place, can miss the bound.
Values may be sent and summed in bfloat16 or wider, within the bound.
A program may use at most 128 MiB of HBM per device.

```python
import math
import jax
import jax.numpy as jnp
from jax import lax

D = 1024
HEADS = 16
HEAD_DIM = 64
P_SIZE = 16
V = 64
LON = 256
LAT = 16


def draw_query(key, part):
    key = jax.random.fold_in(key, 7)
    values = jax.random.normal(key, (D,), jnp.float32)
    values = jnp.clip(values, -6.0, 6.0)
    return values.astype(jnp.bfloat16)


def shard_levels(stream_key, shape, cuts, smallest, largest):
    def one(dim, shards_of):
        draws = jax.random.uniform(jax.random.fold_in(jax.random.fold_in(stream_key, 6), dim), (shards_of,), jnp.float32, smallest / len(cuts), largest / len(cuts))
        return jnp.repeat(jnp.exp(draws), shape[dim] // shards_of).reshape((-1,) + (1,) * (len(shape) - dim - 1))

    loudness = one(*cuts[0])
    for cut in cuts[1:]:
        loudness = loudness * one(*cut)
    return loudness


def gaussian(stream_key, shape, deviation, reach, pieces=(), dtype=jnp.bfloat16):
    drawn = deviation * jax.random.normal(stream_key, shape, jnp.float32)
    if pieces:
        drawn = drawn * shard_levels(stream_key, shape, pieces, -0.22, 0.18)
    return jnp.clip(drawn, -reach, reach).astype(dtype)


def setup_inputs(seed: int = 0) -> dict:
    arg_keys = jax.random.split(jax.random.key(seed), 8)
    return {
        "patches": gaussian(arg_keys[0], (V, LAT, LON * P_SIZE), 1.0, 6.0, ((0, 32), (1, 8))),
        "embed_w": gaussian(arg_keys[1], (V, P_SIZE, D), P_SIZE ** -0.5, 1.5, ((0, 32),)),
        "embed_b": gaussian(arg_keys[2], (V, D), 0.5, 3.0, ((0, 32),)),
        "query": draw_query(jax.random.fold_in(arg_keys[7], 71), 0),
        "kv_w": gaussian(arg_keys[4], (D, 2 * D), D ** -0.5, 0.1875),
        "out_w": gaussian(arg_keys[5], (D, D), D ** -0.5, 0.1875),
        "cotangent": gaussian(arg_keys[6], (LAT, LON, D), (1.0 / 64), 0.08984375, ((0, 8), (1, 32))),
    }


def reference(patches, embed_w, embed_b, query, kv_w, out_w, cotangent):
    score_scale = 1.0 / math.sqrt(HEAD_DIM)
    head_query = query.astype(jnp.float32).reshape(HEADS, HEAD_DIM)
    table_f = embed_w.astype(jnp.float32)
    bias_f = embed_b.astype(jnp.float32)

    def row_step(totals, inputs):
        grad_kv, grad_w, grad_b = totals
        patch_row, cot_row = inputs
        pixels_row = patch_row.reshape(V, LON, P_SIZE).astype(jnp.float32)
        embedded = (jnp.einsum('vnp,vpd->vnd', pixels_row, table_f) + bias_f[:, None, :]).astype(jnp.bfloat16)
        flat_rows = embedded.reshape(-1, D)
        keyvals = jnp.dot(flat_rows, kv_w, preferred_element_type=jnp.float32).astype(jnp.bfloat16)
        keyvals = keyvals.reshape(V, LON, 2, HEADS, HEAD_DIM)
        keys_f = keyvals[:, :, 0].astype(jnp.float32)
        values_f = keyvals[:, :, 1].astype(jnp.float32)
        scores = jnp.einsum('vnhd,hd->nhv', keys_f, head_query) * score_scale
        weights_f = jax.nn.softmax(scores, axis=-1)
        weights = lax.optimization_barrier(weights_f.astype(jnp.bfloat16)).astype(jnp.float32)
        context = jnp.einsum('nhv,vnhd->nhd', weights, values_f).astype(jnp.bfloat16).reshape(LON, D)
        output_row = jnp.dot(context, out_w, preferred_element_type=jnp.float32).astype(jnp.bfloat16)
        context_grad = jnp.dot(cot_row, out_w.T, preferred_element_type=jnp.float32).astype(jnp.bfloat16)
        context_grad = lax.optimization_barrier(context_grad).reshape(LON, HEADS, HEAD_DIM).astype(jnp.float32)
        weight_grad = jnp.einsum('nhd,vnhd->nhv', context_grad, values_f)
        value_grad = jnp.einsum('nhv,nhd->vnhd', weights, context_grad).astype(jnp.bfloat16)
        score_grad = weights_f * (weight_grad - lax.optimization_barrier(jnp.sum(weights_f * weight_grad, axis=-1, keepdims=True))) * score_scale
        key_grad = jnp.einsum('nhv,hd->vnhd', score_grad, head_query).astype(jnp.bfloat16)
        both_grad = jnp.stack([key_grad, value_grad], axis=2).reshape(-1, 2 * D)
        embedded_grad = jnp.dot(both_grad, kv_w.T, preferred_element_type=jnp.float32).astype(jnp.bfloat16)
        embedded_grad = lax.optimization_barrier(embedded_grad).reshape(V, LON, D).astype(jnp.float32)
        grad_kv = grad_kv + jnp.dot(flat_rows.T, both_grad, preferred_element_type=jnp.float32)
        grad_w = grad_w + jnp.einsum('vnp,vnd->vpd', pixels_row, embedded_grad)
        grad_b = grad_b + lax.optimization_barrier(jnp.sum(embedded_grad, axis=1))
        return ((grad_kv, grad_w, grad_b), output_row)
    start = (jnp.zeros((D, 2 * D), jnp.float32), jnp.zeros((V, P_SIZE, D), jnp.float32), jnp.zeros((V, D), jnp.float32))
    totals, aggregated = lax.scan(row_step, start, (jnp.moveaxis(patches, 1, 0), cotangent))
    return (aggregated, totals[0], totals[1], totals[2])
```

```python
import functools

import jax
import jax.numpy as jnp
from jax import lax
from jax.experimental import pallas as pl
from jax.experimental.pallas import tpu as pltpu
from jax.sharding import PartitionSpec as P

MESH = pl.DeviceIdType.MESH
F32 = jnp.float32
BF16 = jnp.bfloat16
LANES = 128
PIX = 16
OWN = 16
HEADS = 16
HEAD_DIM = 64
GROWS = 40


def dot(a, b):
    return jnp.dot(a, b, preferred_element_type=F32)


def dot_nt(a, b):
    return lax.dot_general(a, b, (((1,), (1,)), ((), ())), preferred_element_type=F32)


def iota(shape, dim):
    return lax.broadcasted_iota(jnp.int32, shape, dim)


def ones_at(cond):
    return jnp.where(cond, 1.0, 0.0).astype(BF16)


def split(x):
    high = x.astype(BF16)
    return high, (x - high.astype(F32)).astype(BF16)


def kernel(
    nv, nt,
    p_ref, w_ref, b_ref, q_ref, cot_ref, kv_hbm, ow_hbm,
    agg_ref, gkv_ref, gw_ref, gb_ref,
    kv, ow, pt, px, wf, bt, cgs, emb, val, sc, wgs, d4, rd, gs, gr, gj, gt, gv, gk, gx, rb, os_, or_,
    load_sem, pix_send, pix_recv, w_send, w_recv, wt_send, wt_recv, bt_send, bt_recv, wc_send, wc_recv,
    cg_send, cg_recv, cc_send, cc_recv, d_send, d_recv, gs_send, gs_recv, gt_send, gt_recv, gv_send, gv_recv,
    o_send, o_recv,
):
    me = lax.axis_index("var")
    row = lax.axis_index("tok")
    core = lax.rem(me, 2)
    chip = me // 2
    sib = chip * 2 + 1 - core
    nc = nv // 2
    gi = min(16, nv)
    groups = nv // gi
    rows = gi * OWN
    cpi = (nt * LANES) // nv
    rpd = cpi // nt
    width = nt * LANES
    scale = HEAD_DIM ** -0.5

    def var_peer(o):
        return lax.rem(me + o, nv)

    def tok_peer(o):
        return lax.rem(row + o, nt)

    load_ow = pltpu.make_async_copy(ow_hbm, ow, load_sem.at[0])
    load_kv = pltpu.make_async_copy(kv_hbm, kv, load_sem.at[1])
    load_ow.start()
    load_kv.start()

    barrier = pltpu.get_barrier_semaphore()

    @pl.loop(1, nv)
    def _(o):
        pl.semaphore_signal(barrier, inc=1, device_id=(var_peer(o), row), device_id_type=MESH)

    @pl.loop(1, nt)
    def _(o):
        pl.semaphore_signal(barrier, inc=1, device_id=(me, tok_peer(o)), device_id_type=MESH)

    block = pl.ds(pl.multiple_of(row * LANES, LANES), LANES)
    biases = b_ref[:, block].astype(F32)
    for k in range(nv):
        lanes = slice(k * LANES, (k + 1) * LANES)
        pt[k] = jnp.concatenate(
            [p_ref[0, :, lanes].astype(F32), p_ref[1, :, lanes].astype(F32), biases, jnp.zeros((10, LANES), F32)],
            axis=0,
        ).astype(BF16)

    pl.semaphore_wait(barrier, nv + nt - 2)

    own_w = pltpu.make_async_copy(w_ref.at[core, :, block], wf.at[core, row, me], w_recv)
    own_w.start()
    own_p = pltpu.make_async_copy(pt.at[me], px.at[me], pix_recv)
    own_p.start()

    @pl.loop(1, nv)
    def _(o):
        peer = var_peer(o)
        their = lax.rem(peer, 2)
        pltpu.make_async_remote_copy(
            w_ref.at[their, :, block], wf.at[their, row, me], w_send, w_recv,
            device_id=(peer, row), device_id_type=MESH,
        ).start()
        pltpu.make_async_remote_copy(
            pt.at[peer], px.at[me], pix_send, pix_recv,
            device_id=(peer, row), device_id_type=MESH,
        ).start()

    load_ow.wait()
    cot = cot_ref[...].astype(F32).reshape(OWN, width).astype(BF16)
    cg = dot_nt(cot, ow[...]).astype(BF16)
    cgs[chip, core] = cg

    @pl.loop(1, nc)
    def _(o):
        peer = lax.rem(chip + o, nc) * 2 + core
        pltpu.make_async_remote_copy(
            cgs.at[chip, core], cgs.at[chip, core], cg_send, cg_recv,
            device_id=(peer, row), device_id_type=MESH,
        ).start()

    pltpu.make_async_copy(px, px, pix_recv).wait()
    pick = ones_at(
        iota((2 * nv, nv * 16), 1)
        == (iota((2 * nv, nv * 16), 0) % nv) * 16 + 4 + iota((2 * nv, nv * 16), 0) // nv
    )
    bt[row] = dot(pick, px[...].reshape(nv * 16, LANES)).astype(BF16)

    @pl.loop(1, nt)
    def _(o):
        pltpu.make_async_remote_copy(
            bt.at[row], bt.at[row], bt_send.at[o], bt_recv.at[o],
            device_id=(me, tok_peer(o)), device_id_type=MESH,
        ).start()

    pltpu.make_async_copy(wf.at[core, row], wf.at[core, row], w_recv).wait()

    @pl.loop(1, nt)
    def _(o):
        pltpu.make_async_remote_copy(
            wf.at[core, row], wf.at[core, row], wt_send.at[o], wt_recv.at[o],
            device_id=(me, tok_peer(o)), device_id_type=MESH,
        ).start()

    def to_sibling(k, o):
        pltpu.make_async_remote_copy(
            wf.at[core, k], wf.at[core, k], wc_send, wc_recv,
            device_id=(sib, row), device_id_type=MESH,
        ).start()

    to_sibling(row, 0)

    @pl.loop(1, nt)
    def _(o):
        k = lax.rem(row - o + nt, nt)
        pltpu.make_async_copy(wf.at[core, k], wf.at[core, k], wt_recv.at[o]).wait()
        pltpu.make_async_copy(bt.at[k], bt.at[k], bt_recv.at[o]).wait()
        to_sibling(k, o)

    load_kv.wait()
    r_r = iota((rows, rows), 0)
    r_k = iota((rows, rows), 1)
    l_r = iota((rows, LANES), 0)
    l_k = iota((rows, LANES), 1)
    same_lon = (l_r & 7) == (l_k >> 4)
    fold = ones_at((iota((LANES, rows), 0) & 15) == (iota((LANES, rows), 1) & 15))
    query = q_ref[...].astype(F32)
    head_of = iota((width, LANES), 0) // HEAD_DIM == iota((width, LANES), 1)
    sum_heads = ones_at(head_of)
    q_cols = jnp.broadcast_to(query, (LANES, width)).T
    q_block = jnp.where(head_of, q_cols, 0.0).astype(BF16)
    cg_f = cg.astype(F32)

    def row_select(first):
        return ones_at(((r_k >> 4) == (r_r >> 4)) & ((r_k & 15) == first + ((r_r & 15) >> 3)))

    def chunk(par, g):
        held = pl.ds(pl.multiple_of(g * gi, gi), gi)
        x = dot(row_select(par * 2), px[held].reshape(rows, LANES))
        x = jnp.where(same_lon, x, 0.0).astype(BF16)
        x = jnp.where((r_r >> 4) == (r_k >> 4), dot(x, fold), 0.0).astype(BF16)
        which = ones_at(iota((rows, 2 * nv), 1) == par * nv + g * gi + (iota((rows, 2 * nv), 0) >> 4))
        for k in range(nt):
            e = dot(x, wf[par, k, held].reshape(rows, LANES)) + dot(which, bt[k])
            emb[:, k * LANES:(k + 1) * LANES] = e.astype(BF16)
        at = pl.ds(pl.multiple_of((par * groups + g) * rows, rows), rows)
        keys = dot(emb[...], kv[:, :width]).astype(BF16)
        sc[at, :] = dot(keys, q_block) * scale
        values = dot(emb[...], kv[:, width:]).astype(BF16)
        val[at, :] = values
        product = values.astype(F32).reshape(gi, OWN, width) * cg_f[None]
        high, low = split(product.reshape(rows, width))
        wgs[at, :] = dot(high, sum_heads) + dot(low, sum_heads)

    @pl.loop(0, groups)
    def _(g):
        chunk(core, g)

    pltpu.make_async_copy(wf.at[1 - core], wf.at[1 - core], wc_recv).wait()
    pltpu.make_async_copy(cgs.at[pl.ds(0, nc - 1), core], cgs.at[pl.ds(0, nc - 1), core], cg_recv).wait()
    cg_forward = pltpu.make_async_remote_copy(
        cgs.at[:, core], cgs.at[:, core], cc_send, cc_recv,
        device_id=(sib, row), device_id_type=MESH,
    )
    cg_forward.start()

    @pl.loop(0, groups)
    def _(g):
        chunk(1 - core, g)

    s = sc[...].reshape(2 * nv, OWN, LANES)
    e = jnp.exp(s - jnp.max(s, axis=0, keepdims=True))
    weights_f = e / jnp.sum(e, axis=0, keepdims=True)
    wg = wgs[...].reshape(2 * nv, OWN, LANES)
    sg = weights_f * (wg - jnp.sum(weights_f * wg, axis=0, keepdims=True)) * scale
    sc[...] = weights_f.reshape(2 * nv * OWN, LANES)
    wgs[...] = sg.reshape(2 * nv * OWN, LANES)

    spread = ones_at(
        (iota((LANES, LANES), 0) == (iota((LANES, LANES), 1) & 15)) & (iota((LANES, LANES), 0) < HEADS)
    )

    @pl.loop(0, groups)
    def _(g):
        out = jnp.zeros((rows, LANES), F32)
        for par in range(2):
            at = pl.ds(pl.multiple_of((par * groups + g) * rows, rows), rows)
            high, low = split(wgs[at, :])
            for a, part in enumerate((sc[at, :].astype(BF16), high, low)):
                t = jnp.where(same_lon, dot(part, spread), 0.0).astype(BF16)
                put = ones_at(
                    ((r_k >> 4) == (r_r >> 4)) & ((r_r & 15) == a * 4 + par * 2 + ((r_k & 15) >> 3))
                )
                out = out + dot(put, t)
        d4[pl.ds(pl.multiple_of(g * gi, gi), gi)] = out.astype(BF16).reshape(gi, 16, LANES)

    own_d = pltpu.make_async_copy(d4.at[me], rd.at[me], d_recv)
    own_d.start()

    @pl.loop(1, nv)
    def _(o):
        peer = var_peer(o)
        pltpu.make_async_remote_copy(
            d4.at[peer], rd.at[me], d_send, d_recv, device_id=(peer, row), device_id_type=MESH,
        ).start()

    head_spread = ones_at(iota((LANES, width), 1) // HEAD_DIM == iota((LANES, width), 0))

    def add_context(c, total):
        at = pl.ds(pl.multiple_of(c * rows, rows), rows)
        w = dot(sc[at, :].astype(BF16), head_spread)
        return total + jnp.sum((w * val[at, :].astype(F32)).reshape(gi, OWN, width), axis=0)

    context = lax.fori_loop(0, 2 * groups, add_context, jnp.zeros((OWN, width), F32))
    agg_ref[...] = dot(context.astype(BF16), ow[...]).astype(BF16)

    pltpu.make_async_copy(cgs.at[:, 1 - core], cgs.at[:, 1 - core], cc_recv).wait()
    pltpu.make_async_copy(rd, rd, d_recv).wait()
    lane_spread = ones_at((iota((LANES, width), 0) & 15) == iota((LANES, width), 1) // HEAD_DIM)
    lane_fold = ones_at((iota((LANES, LANES), 0) & 15) == iota((LANES, LANES), 1))

    def add_grads(g, totals):
        g_val, g_key = totals
        held = pl.ds(pl.multiple_of(g * gi, gi), gi)
        x = rd[held].reshape(rows, LANES)
        own = pt[held].reshape(rows, LANES)
        half = pl.ds(pl.multiple_of(g * (gi // 2), gi // 2), gi // 2)
        cg_g = cgs[half].reshape(rows, width).astype(F32)

        def picked(first, source):
            return jnp.where(same_lon, dot(row_select(first), source), 0.0).astype(BF16)

        for par in range(2):
            to_rows = ones_at(
                ((iota((LANES, LANES), 0) & 15) == iota((LANES, LANES), 1) - par * 16)
            )
            pix = dot(picked(par * 2, own), to_rows)
            pix = jnp.where(l_k == 32 + par, 1.0, pix)
            pix_t = pix.T.astype(BF16)
            w = dot(picked(par * 2, x), lane_spread)
            value_grad = (w * cg_g).astype(BF16)
            g_val = g_val + dot(pix_t, value_grad)
            for a in (1, 2):
                part = dot(picked(a * 4 + par * 2, x), lane_fold).astype(BF16)
                g_key = g_key + dot(pix_t, part)
        return g_val, g_key

    g_val, g_key = lax.fori_loop(
        0, groups, add_grads, (jnp.zeros((LANES, width), F32), jnp.zeros((LANES, LANES), F32))
    )
    g_key = g_key.T
    per = HEADS // nt
    for k in range(nt):
        gs[k] = g_val[0:GROWS, k * LANES:(k + 1) * LANES]
        gs[k, 34:34 + per, :] = g_key[k * per:(k + 1) * per, :]

    own_g = pltpu.make_async_copy(gs.at[row], gr.at[row], gs_recv)
    own_g.start()

    @pl.loop(1, nt)
    def _(o):
        peer = tok_peer(o)
        pltpu.make_async_remote_copy(
            gs.at[peer], gr.at[row], gs_send, gs_recv, device_id=(me, peer), device_id_type=MESH,
        ).start()

    pltpu.make_async_copy(gr, gr, gs_recv).wait()
    gj[...] = jnp.sum(gr[...], axis=0)

    own_t = pltpu.make_async_copy(gj, gt.at[row], gt_recv)
    own_t.start()
    own_v = pltpu.make_async_copy(gj, gv.at[me], gv_recv)
    own_v.start()

    @pl.loop(1, nt)
    def _(o):
        pltpu.make_async_remote_copy(
            gj, gt.at[row], gt_send, gt_recv, device_id=(me, tok_peer(o)), device_id_type=MESH,
        ).start()

    @pl.loop(1, nv)
    def _(o):
        pltpu.make_async_remote_copy(
            gj, gv.at[me], gv_send, gv_recv, device_id=(var_peer(o), row), device_id_type=MESH,
        ).start()

    pltpu.make_async_copy(gt, gt, gt_recv).wait()
    gk[...] = jnp.zeros((LANES, LANES), F32)
    for k in range(nt):
        gk[k * per:(k + 1) * per, :] = gt[k, 34:34 + per, :]
    key_high, key_low = split(gk[...].T[0:GROWS])
    q_rows = jnp.where(
        iota((LANES, width), 1) // HEAD_DIM == iota((LANES, width), 0), jnp.broadcast_to(query, (LANES, width)), 0.0
    ).astype(BF16)
    high, low = split(dot(key_high, q_rows) + dot(key_low, q_rows))
    gx[0:GROWS, :width] = high
    gx[GROWS:, :width] = low
    for k in range(nt):
        high, low = split(gt[k])
        lanes = slice(width + k * LANES, width + (k + 1) * LANES)
        gx[0:GROWS, lanes] = high
        gx[GROWS:, lanes] = low
    both = dot_nt(gx[...], kv[...])
    table = both[0:GROWS] + both[GROWS:]
    gw_ref[0] = table[0:16]
    gw_ref[1] = table[16:32]
    gb_ref[...] = table[32:34]

    pltpu.make_async_copy(gv, gv, gv_recv).wait()
    lane = iota((nv * 16, LANES), 1)
    sub = iota((nv * 16, LANES), 0) & 15
    lane_b = iota((nv, LANES), 1)
    heads_here = [gv[:, 34 + h, :] for h in range(per)]

    def columns(cols, at):
        out = jnp.zeros(at.shape, F32)
        for h, col in enumerate(cols):
            out = jnp.where(at == h, col, out)
        return out

    rights = []
    for par in range(2):
        value = gv[:, par * 16:par * 16 + 16, :].reshape(nv * 16, LANES)
        cols = []
        for a in heads_here:
            wide = jnp.broadcast_to(a[:, None, :], (nv, 16, LANES)).reshape(nv * 16, LANES)
            cols.append(jnp.sum(jnp.where(lane == par * 16 + sub, wide, 0.0), axis=1, keepdims=True))
        rights.append(jnp.concatenate(split(value) + split(columns(cols, lane)), axis=1))
    right_b = []
    for par in range(2):
        cols = [jnp.sum(jnp.where(lane_b == 32 + par, a, 0.0), axis=1, keepdims=True) for a in heads_here]
        right_b.append(jnp.concatenate([gv[:, 32 + par, :], columns(cols, lane_b)], axis=1))
    right_b = jnp.concatenate(right_b, axis=0)
    high, low = split(right_b)
    right_b = jnp.concatenate([high[:, :LANES], low[:, :LANES], high[:, LANES:], low[:, LANES:]], axis=1)
    size = min(cpi, LANES)
    for t in range(max(1, cpi // LANES)):
        k = (me * cpi) // LANES + t
        total = dot(bt[k].astype(F32).T.astype(BF16), right_b)
        for par in range(2):
            left = wf[par, k].reshape(nv * 16, LANES).astype(F32).T.astype(BF16)
            total = total + dot(left, rights[par])
        rb[:, 0:LANES] = total[:, 0:LANES] + total[:, LANES:2 * LANES]
        rb[:, LANES:] = total[:, 2 * LANES:3 * LANES] + total[:, 3 * LANES:]
        mine = rb[pl.ds(pl.multiple_of(lax.rem(me * cpi, LANES), size), size), :]
        for d in range(size // rpd):
            to = t * (size // rpd) + d
            os_[to, 0:rpd, :] = mine[d * rpd:(d + 1) * rpd, 0:LANES]
            os_[to, rpd:, :] = mine[d * rpd:(d + 1) * rpd, LANES:]

    own_o = pltpu.make_async_copy(os_.at[row], or_.at[row], o_recv)
    own_o.start()

    @pl.loop(1, nt)
    def _(o):
        peer = tok_peer(o)
        pltpu.make_async_remote_copy(
            os_.at[peer], or_.at[row], o_send, o_recv, device_id=(me, peer), device_id_type=MESH,
        ).start()

    pltpu.make_async_copy(or_, or_, o_recv).wait()
    small = iota((rpd, LANES), 1)
    for k in range(nt):
        lanes = slice(k * LANES, (k + 1) * LANES)
        gkv_ref[:, width + k * LANES:width + (k + 1) * LANES] = or_[k, 0:rpd, :]
        keyed = or_[k, rpd:, :]
        spread_key = jnp.zeros((rpd, LANES), F32)
        for h in range(per):
            spread_key = jnp.where(small // HEAD_DIM == h, keyed[:, h:h + 1], spread_key)
        gkv_ref[:, lanes] = spread_key * query[:, lanes]

    def sent(ref, sem):
        pltpu.make_async_copy(ref, ref, sem).wait()

    sent(px.at[pl.ds(0, nv - 1)], pix_send)
    sent(px.at[pl.ds(0, nv - 1)], w_send)
    sent(cgs.at[pl.ds(0, nc - 1), 0], cg_send)
    sent(wf.at[0], wc_send)
    cg_forward.wait_send()

    @pl.loop(1, nt)
    def _(o):
        sent(bt.at[row], bt_send.at[o])
        sent(wf.at[core, row], wt_send.at[o])

    sent(rd.at[pl.ds(0, nv - 1)], d_send)
    sent(gr.at[pl.ds(0, nt - 1)], gs_send)
    sent(gt.at[pl.ds(0, nt - 1)], gt_send)
    sent(gv.at[pl.ds(0, nv - 1)], gv_send)
    sent(or_.at[pl.ds(0, nt - 1)], o_send)


def shards(nv, nt, patches, embed_w, embed_b, query, kv_w, out_w, cotangent):
    width = kv_w.shape[0]
    rpd = width // (nv * nt)
    vmem = pl.BlockSpec(memory_space=pltpu.VMEM)
    hbm = pl.BlockSpec(memory_space=pl.ANY)
    dma = pltpu.SemaphoreType.DMA
    tile = (16, LANES)
    rows = min(16, nv) * OWN
    aggregated, grad_kv, grad_w, grad_b = pl.pallas_call(
        functools.partial(kernel, nv, nt),
        out_shape=(
            jax.ShapeDtypeStruct((OWN, width), BF16),
            jax.ShapeDtypeStruct((rpd, 2 * width), F32),
            jax.ShapeDtypeStruct(embed_w.shape, F32),
            jax.ShapeDtypeStruct(embed_b.shape, F32),
        ),
        in_specs=[vmem] * 5 + [hbm] * 2,
        out_specs=(vmem,) * 4,
        scratch_shapes=[
            pltpu.VMEM((width, 2 * width), BF16),
            pltpu.VMEM((width, width), BF16),
            pltpu.VMEM((nv,) + tile, BF16),
            pltpu.VMEM((nv,) + tile, BF16),
            pltpu.VMEM((2, nt, nv) + tile, BF16),
            pltpu.VMEM((nt, 2 * nv, LANES), BF16),
            pltpu.VMEM((nv // 2, 2, OWN, width), BF16),
            pltpu.VMEM((rows, width), BF16),
            pltpu.VMEM((2 * nv * OWN, width), BF16),
            pltpu.VMEM((2 * nv * OWN, LANES), F32),
            pltpu.VMEM((2 * nv * OWN, LANES), F32),
            pltpu.VMEM((nv,) + tile, BF16),
            pltpu.VMEM((nv,) + tile, BF16),
            pltpu.VMEM((nt, GROWS, LANES), F32),
            pltpu.VMEM((nt, GROWS, LANES), F32),
            pltpu.VMEM((GROWS, LANES), F32),
            pltpu.VMEM((nt, GROWS, LANES), F32),
            pltpu.VMEM((nv, GROWS, LANES), F32),
            pltpu.VMEM((LANES, LANES), F32),
            pltpu.VMEM((2 * GROWS, 2 * width), BF16),
            pltpu.VMEM((LANES, 2 * LANES), F32),
            pltpu.VMEM((nt, 2 * rpd, LANES), F32),
            pltpu.VMEM((nt, 2 * rpd, LANES), F32),
            dma((2,)), dma, dma, dma, dma, dma((nt,)), dma((nt,)), dma((nt,)), dma((nt,)), dma, dma,
            dma, dma, dma, dma, dma, dma, dma, dma, dma, dma, dma, dma,
            dma, dma,
        ],
        compiler_params=pltpu.CompilerParams(
            collective_id=0, has_side_effects=True, vmem_limit_bytes=56 * 1024 * 1024
        ),
        cost_estimate=pl.CostEstimate(flops=5_000_000_000, bytes_accessed=8_000_000, transcendentals=20_000),
    )(patches, embed_w, embed_b, query.reshape(1, width), cotangent, kv_w, out_w)
    return aggregated.reshape(cotangent.shape), grad_kv, grad_w, grad_b


def solution(mesh):
    return jax.shard_map(
        functools.partial(shards, mesh.shape["var"], mesh.shape["tok"]),
        mesh=mesh,
        in_specs=(
            P("var", "tok", None),
            P("var", None, None),
            P("var", None),
            P(),
            P(),
            P(),
            P("tok", "var", None),
        ),
        out_specs=(
            P("tok", "var", None),
            P(("var", "tok"), None),
            P("var", None, None),
            P("var", None),
        ),
        check_vma=False,
    )
```

```python
import functools

import jax
import jax.numpy as jnp
from jax import lax
from jax.experimental import pallas as pl
from jax.experimental.pallas import tpu as pltpu
from jax.sharding import PartitionSpec as P

MESH = pl.DeviceIdType.MESH
F32 = jnp.float32
BF16 = jnp.bfloat16
LANES = 128
PIX = 16
OWN = 16
HEADS = 16
HEAD_DIM = 64
GROWS = 40


def dot(a, b):
    return jnp.dot(a, b, preferred_element_type=F32)


def dot_nt(a, b):
    return lax.dot_general(a, b, (((1,), (1,)), ((), ())), preferred_element_type=F32)


def iota(shape, dim):
    return lax.broadcasted_iota(jnp.int32, shape, dim)


def ones_at(cond):
    return jnp.where(cond, 1.0, 0.0).astype(BF16)


def split(x):
    high = x.astype(BF16)
    return high, (x - high.astype(F32)).astype(BF16)


def remote(src, dst, send_sem, recv_sem, device):
    pltpu.make_async_remote_copy(
        src, dst, send_sem, recv_sem, device_id=device, device_id_type=MESH
    ).start()


def local(src, dst, sem):
    pltpu.make_async_copy(src, dst, sem).start()


def wait_for(ref, sem):
    pltpu.make_async_copy(ref, ref, sem).wait()


def kernel(
    nv, nt,
    p_ref, w_ref, b_ref, q_ref, cot_ref, kv_hbm, ow_hbm,
    agg_ref, gkv_ref, gw_ref, gb_ref,
    kv, ow, pt, px, wf, bt, bown, cgs, emb, val, sc, wgs, d4, rd, gs, gr, gj, gjb, gt, gv, gk, gx, rb, os_, or_,
    sel1, selb, put, sel3, pixt, lane_spread, head_spread,
    load_sem, pix_send, pix_recv, w_send, w_recv, b_send, b_recv, wt_send, wt_recv, bt_send, bt_recv, wc_send, wc_recv,
    cg_send, cg_recv, cc_send, cc_recv, d_send, d_recv, gs_send, gs_recv, gt_send, gt_recv, gv_send, gv_recv,
    gc_send, gc_recv, o_send, o_recv,
):
    me = lax.axis_index("var")
    row = lax.axis_index("tok")
    core = lax.rem(me, 2)
    chip = me // 2
    sib = chip * 2 + 1 - core
    nc = nv // 2
    na = nv // nt
    gi = min(16, nv)
    groups = nv // gi
    rows = gi * OWN
    crows = 4 * na * OWN
    cpi = (nt * LANES) // nv
    rpd = cpi // nt
    width = nt * LANES
    per = HEADS // nt
    scale = HEAD_DIM ** -0.5
    pending = []

    def var_peer(o):
        return lax.rem(me + o, nv)

    def shared_by(i):
        return lax.rem(i + 4 * (i // 16), nt), i // nt

    def tok_peer(ox, oy):
        return lax.rem(row // 4 + oy, 2) * 4 + lax.rem(lax.rem(row, 4) + ox, 4)

    def tok_source(ox, oy):
        return lax.rem(row // 4 + oy, 2) * 4 + lax.rem(lax.rem(row, 4) - ox + 4, 4)

    def slot_of(r):
        return lax.rem(row - r + 8, 4), lax.rem(row // 4 + r // 4, 2)

    load_ow = pltpu.make_async_copy(ow_hbm, ow, load_sem.at[0])
    load_kv = pltpu.make_async_copy(kv_hbm, kv, load_sem.at[1])

    barrier = pltpu.get_barrier_semaphore()

    @pl.loop(1, nv)
    def _(o):
        pl.semaphore_signal(barrier, inc=1, device_id=(var_peer(o), row), device_id_type=MESH)

    @pl.loop(1, nt)
    def _(o):
        pl.semaphore_signal(barrier, inc=1, device_id=(me, lax.rem(row + o, nt)), device_id_type=MESH)

    load_ow.start()
    load_kv.start()

    for k in range(nv):
        lanes = slice(k * LANES, (k + 1) * LANES)
        pt[k] = jnp.concatenate(
            [p_ref[0, :, lanes].astype(F32), p_ref[1, :, lanes].astype(F32), jnp.zeros((12, LANES), F32)], axis=0
        ).astype(BF16)
    bias = b_ref[...].astype(F32)
    bown[...] = jnp.concatenate(
        [bias[v:v + 1, k * LANES:(k + 1) * LANES] for v in range(2) for k in range(nt)], axis=0
    ).astype(BF16)

    pl.semaphore_wait(barrier, nv + nt - 2)

    my_r, my_a = shared_by(me)

    @pl.when(my_r == row)
    def _():
        local(w_ref.at[core], wf.at[0, core, my_a], w_recv)
        local(bown, bt.at[0, my_a], b_recv)

        @pl.loop(1, nv)
        def _(o):
            peer = var_peer(o)
            their = lax.rem(peer, 2)
            remote(w_ref.at[their], wf.at[0, their, my_a], w_send.at[o], w_recv, (peer, row))
            remote(bown, bt.at[0, my_a], b_send.at[o], b_recv, (peer, row))

    def w_sent():
        @pl.when(my_r == row)
        def _():
            @pl.loop(1, nv)
            def _(o):
                wait_for(w_ref.at[0], w_send.at[o])
                wait_for(bown, b_send.at[o])

    pending.append(w_sent)
    local(pt.at[me], px.at[my_a, my_r], pix_recv)

    @pl.loop(1, nv)
    def _(o):
        peer = var_peer(o)
        remote(pt.at[peer], px.at[my_a, my_r], pix_send, pix_recv, (peer, row))

    pending.append(lambda: wait_for(pt.at[pl.ds(0, nv - 1)], pix_send))

    half = crows // 2
    c_r = iota((crows, half), 0)
    c_q = iota((crows, half), 1)
    c_par = (c_r // (16 * na)) & 1
    c_same = (c_q >> 4) == (c_r // (32 * na)) * na + ((c_r >> 4) & (na - 1))
    sel1[...] = ones_at(c_same & ((c_q & 15) == c_par * 2 + ((c_r & 15) >> 3)))
    for k in range(nt):
        selb[k] = ones_at(c_same & ((c_q & 15) == c_par * 8 + k))
    p_r = iota((half, crows), 1)
    p_q = iota((half, crows), 0)
    p_par = (p_r // (16 * na)) & 1
    p_same = (p_q >> 4) == (p_r // (32 * na)) * na + ((p_r >> 4) & (na - 1))
    for a in range(3):
        put[a] = ones_at(p_same & ((p_q & 15) == a * 4 + p_par * 2 + ((p_r & 15) >> 3)))
    s_r = iota((rows, rows), 0)
    s_k = iota((rows, rows), 1)
    for a in range(6):
        sel3[a] = ones_at(((s_k >> 4) == (s_r >> 4)) & ((s_k & 15) == a * 2 + ((s_r & 15) >> 3)))
    lane_spread[...] = ones_at((iota((LANES, width), 0) & 15) == iota((LANES, width), 1) // HEAD_DIM)
    head_spread[...] = ones_at(iota((LANES, width), 1) // HEAD_DIM == iota((LANES, width), 0))

    load_ow.wait()
    cot = cot_ref[...].astype(F32).reshape(OWN, width).astype(BF16)
    cg = dot_nt(cot, ow[...]).astype(BF16)
    cgs[chip, core] = cg

    wait_for(bt.at[0], b_recv)
    wait_for(wf.at[0, core], w_recv)

    def share(s, ox, oy, to):
        peer = (me, to)
        remote(wf.at[s, core], wf.at[ox * 2 + oy, core], wt_send.at[ox * 2 + oy], wt_recv.at[ox * 2 + oy], peer)
        remote(bt.at[s], bt.at[ox * 2 + oy], bt_send.at[ox * 2 + oy], bt_recv.at[ox * 2 + oy], peer)

    def to_sibling(s):
        remote(wf.at[s, core], wf.at[s, core], wc_send.at[s], wc_recv.at[s], (sib, row))

    def arrived(s):
        wait_for(wf.at[s, core], wt_recv.at[s])
        wait_for(bt.at[s], bt_recv.at[s])
        to_sibling(s)

    share(0, 0, 1, tok_peer(0, 1))
    for ox in (1, 3, 2):
        share(0, ox, 0, tok_peer(ox, 0))
    to_sibling(0)

    @pl.loop(1, nc)
    def _(o):
        peer = lax.rem(chip + o, nc) * 2 + core
        remote(cgs.at[chip, core], cgs.at[chip, core], cg_send, cg_recv, (peer, row))

    pending.append(lambda: wait_for(cgs.at[pl.ds(0, nc - 1), 0], cg_send))

    arrived(1)
    for ox in (1, 3, 2):
        share(1, ox, 1, tok_peer(ox, 0))

    def shared_sent():
        @pl.loop(1, 8)
        def _(s):
            wait_for(wf.at[s, core], wt_send.at[s])
            wait_for(bt.at[s], bt_send.at[s])

        @pl.loop(0, 8)
        def _(s):
            wait_for(wf.at[s, core], wc_send.at[s])

    pending.append(shared_sent)

    def shared_recv():
        @pl.loop(0, 8)
        def _(s):
            wait_for(wf.at[s, 1 - core], wc_recv.at[s])


    l_k = iota((rows, LANES), 1)
    same_lon = (iota((rows, LANES), 0) & 7) == (l_k >> 4)
    same_lon_c = (iota((crows, LANES), 0) & 7) == (iota((crows, LANES), 1) >> 4)
    fold = ones_at((iota((LANES, crows), 0) & 15) == (iota((LANES, crows), 1) & 15))
    same_block = (iota((crows, crows), 0) >> 4) == (iota((crows, crows), 1) >> 4)
    query = q_ref[...].astype(F32).reshape(1, width)
    head_of = iota((width, LANES), 0) // HEAD_DIM == iota((width, LANES), 1)
    sum_heads = ones_at(head_of)
    q_cols = jnp.broadcast_to(query, (LANES, width)).T
    q_block = jnp.where(head_of, q_cols, 0.0).astype(BF16)
    cg_f = cg.astype(F32)

    for g in range(groups):
        for par in range(2):
            own = pt[g * gi:(g + 1) * gi].reshape(rows, LANES)
            own = jnp.where(same_lon, dot(sel3[par], own), 0.0).astype(BF16)
            to_rows = ones_at((iota((LANES, LANES), 0) & 15) == iota((LANES, LANES), 1) - par * 16)
            pix = jnp.where(l_k == 32 + par, 1.0, dot(own, to_rows))
            pixt[g * 2 + par] = pix.T.astype(BF16)

    wait_for(px, pix_recv)
    load_kv.wait()

    def chunk(ox):
        pair = pl.ds(ox * 2, 2)
        x = jnp.concatenate(
            [px[:, tok_source(ox, oy)].reshape(na * 16, LANES) for oy in range(2)], axis=0
        )
        x = jnp.where(same_lon_c, dot(sel1[...], x), 0.0).astype(BF16)
        x = jnp.where(same_block, dot(x, fold), 0.0).astype(BF16)
        biases = bt[pair].reshape(half, LANES)
        for k in range(nt):
            lanes = slice(k * LANES, (k + 1) * LANES)
            e = dot(x, wf[pair, :, :, :, lanes].reshape(crows, LANES)) + dot(selb[k], biases)
            emb[:, lanes] = e.astype(BF16)
        at = pl.ds(pl.multiple_of(ox * crows, crows), crows)
        keys = dot(emb[...], kv[:, :width]).astype(BF16)
        sc[at, :] = dot(keys, q_block) * scale
        values = dot(emb[...], kv[:, width:]).astype(BF16)
        val[at, :] = values
        product = values.astype(F32).reshape(crows // OWN, OWN, width) * cg_f[None]
        high, low = split(product.reshape(crows, width))
        wgs[at, :] = dot(high, sum_heads) + dot(low, sum_heads)

    @pl.loop(0, 4)
    def _(k):
        @pl.when(k < 3)
        def _():
            later = (k + 1) ^ ((k + 1) >> 1)
            arrived(later * 2)
            arrived(later * 2 + 1)

        now = k ^ (k >> 1)
        wait_for(wf.at[now * 2, 1 - core], wc_recv.at[now * 2])
        wait_for(wf.at[now * 2 + 1, 1 - core], wc_recv.at[now * 2 + 1])
        chunk(now)

    s = sc[...].reshape(2 * nv, OWN, LANES)
    e = jnp.exp(s - jnp.max(s, axis=0, keepdims=True))
    weights_f = e / jnp.sum(e, axis=0, keepdims=True)
    wg = wgs[...].reshape(2 * nv, OWN, LANES)
    sg = weights_f * (wg - jnp.sum(weights_f * wg, axis=0, keepdims=True)) * scale
    sc[...] = weights_f.reshape(2 * nv * OWN, LANES)
    wgs[...] = sg.reshape(2 * nv * OWN, LANES)

    spread = ones_at(
        (iota((LANES, LANES), 0) == (iota((LANES, LANES), 1) & 15)) & (iota((LANES, LANES), 0) < HEADS)
    )

    @pl.loop(0, 4)
    def _(ox):
        at = pl.ds(pl.multiple_of(ox * crows, crows), crows)
        high, low = split(wgs[at, :])
        out = jnp.zeros((half, LANES), F32)
        for a, part in enumerate((sc[at, :].astype(BF16), high, low)):
            out = out + dot(put[a], jnp.where(same_lon_c, dot(part, spread), 0.0).astype(BF16))
        d4[ox] = out.astype(BF16).reshape(2, na, 16, LANES)

    def d_part(i):
        r, a = shared_by(i)
        ox, oy = slot_of(r)
        return d4.at[ox, oy, a]

    local(d_part(me), rd.at[me], d_recv)

    @pl.loop(1, nv)
    def _(o):
        peer = var_peer(o)
        remote(d_part(peer), rd.at[me], d_send, d_recv, (peer, row))

    pending.append(lambda: wait_for(rd.at[pl.ds(0, nv - 1)], d_send))

    wait_for(cgs.at[pl.ds(0, nc - 1), core], cg_recv)
    remote(cgs.at[:, core], cgs.at[:, core], cc_send, cc_recv, (sib, row))
    pending.append(lambda: wait_for(cgs.at[:, 0], cc_send))

    def add_context(c, total):
        at = pl.ds(pl.multiple_of(c * crows, crows), crows)
        w = dot(sc[at, :].astype(BF16), head_spread[...])
        return total + jnp.sum((w * val[at, :].astype(F32)).reshape(crows // OWN, OWN, width), axis=0)

    context = lax.fori_loop(0, 4, add_context, jnp.zeros((OWN, width), F32))
    agg_ref[...] = dot(context.astype(BF16), ow[...]).astype(BF16)

    wait_for(cgs.at[:, 1 - core], cc_recv)
    wait_for(rd, d_recv)
    lane_fold = ones_at((iota((LANES, LANES), 0) & 15) == iota((LANES, LANES), 1))

    def add_grads(g, totals):
        g_val, g_key = totals
        x = rd[pl.ds(pl.multiple_of(g * gi, gi), gi)].reshape(rows, LANES)
        cg_g = cgs[pl.ds(pl.multiple_of(g * (gi // 2), gi // 2), gi // 2)].reshape(rows, width).astype(F32)

        def picked(a):
            return jnp.where(same_lon, dot(sel3[a], x), 0.0).astype(BF16)

        for par in range(2):
            left = pixt[g * 2 + par]
            value_grad = (dot(picked(par), lane_spread[...]) * cg_g).astype(BF16)
            g_val = g_val + dot(left, value_grad)
            for a in (2, 4):
                g_key = g_key + dot(left, dot(picked(a + par), lane_fold).astype(BF16))
        return g_val, g_key

    g_val, g_key = lax.fori_loop(
        0, groups, add_grads, (jnp.zeros((LANES, width), F32), jnp.zeros((LANES, LANES), F32))
    )
    g_key = g_key.T
    for k in range(nt):
        gs[k] = g_val[0:GROWS, k * LANES:(k + 1) * LANES]
        gs[k, 34:34 + per, :] = g_key[k * per:(k + 1) * per, :]

    local(gs.at[row], gr.at[row], gs_recv)

    @pl.loop(1, nt)
    def _(o):
        peer = lax.rem(row + o, nt)
        remote(gs.at[peer], gr.at[row], gs_send, gs_recv, (me, peer))

    pending.append(lambda: wait_for(gr.at[pl.ds(0, nt - 1)], gs_send))
    wait_for(gr, gs_recv)
    total = jnp.sum(gr[...], axis=0)
    gj[...] = total
    high, low = split(total[32:40])
    gjb[0:32] = total[0:32].astype(BF16)
    high, low = high.astype(F32), low.astype(F32)
    gjb[32:48] = jnp.concatenate(
        [high[0:2], low[0:2], high[2:2 + per], low[2:2 + per], jnp.zeros((12 - 2 * per, LANES), F32)], axis=0
    ).astype(BF16)

    mx, my = slot_of(my_r)
    ours = lax.rem(mx, 2)
    mine = gv.at[mx // 2, ours, my, my_a]
    local(gjb, mine, gv_recv)

    @pl.loop(1, nc)
    def _(o):
        peer = lax.rem(chip + o, nc) * 2 + core
        remote(gjb, mine, gv_send, gv_recv, (peer, row))

    local(gj, gt.at[row], gt_recv)

    @pl.loop(1, nt)
    def _(o):
        remote(gj, gt.at[row], gt_send, gt_recv, (me, lax.rem(row + o, nt)))

    pending.append(lambda: wait_for(gt.at[pl.ds(0, nt - 1)], gt_send))

    def gv_sent():
        @pl.loop(1, nc)
        def _(o):
            wait_for(gjb, gv_send)

    pending.append(gv_sent)

    wait_for(gt, gt_recv)
    gk[...] = jnp.zeros((LANES, LANES), F32)
    for k in range(nt):
        gk[k * per:(k + 1) * per, :] = gt[k, 34:34 + per, :]
        high, low = split(gt[k])
        lanes = slice(width + k * LANES, width + (k + 1) * LANES)
        gx[0:GROWS, lanes] = high
        gx[GROWS:, lanes] = low
    key_high, key_low = split(gk[...].T[0:GROWS])
    q_rows = (head_spread[...].astype(F32) * query).astype(BF16)
    high, low = split(dot(key_high, q_rows) + dot(key_low, q_rows))
    gx[0:GROWS, :width] = high
    gx[GROWS:, :width] = low

    wait_for(gv.at[:, ours], gv_recv)
    remote(gv.at[:, ours], gv.at[:, ours], gc_send, gc_recv, (sib, row))
    pending.append(lambda: wait_for(gv.at[:, ours], gc_send))
    both = dot_nt(gx[...], kv[...])
    table = both[0:GROWS] + both[GROWS:]
    gw_ref[0] = table[0:16]
    gw_ref[1] = table[16:32]
    gb_ref[...] = table[32:34]

    wait_for(gv.at[:, 1 - ours], gc_recv)
    tail = gv[:, :, :, :, 32:48, :].astype(F32).reshape(nv, 16, LANES)
    lane = iota((nv * 16, LANES), 1)
    sub = iota((nv * 16, LANES), 0) & 15
    lane_b = iota((nv, LANES), 1)
    keys_here = [tail[:, 4 + h, :] + tail[:, 4 + per + h, :] for h in range(per)]

    def columns(cols, at):
        out = jnp.zeros(at.shape, F32)
        for h, col in enumerate(cols):
            out = jnp.where(at == h, col, out)
        return split(out)

    rights = []
    for par in range(2):
        value = gv[:, :, :, :, par * 16:par * 16 + 16, :].reshape(nv * 16, LANES)
        cols = []
        for a in keys_here:
            wide = jnp.broadcast_to(a[:, None, :], (nv, 16, LANES)).reshape(nv * 16, LANES)
            cols.append(jnp.sum(jnp.where(lane == par * 16 + sub, wide, 0.0), axis=1, keepdims=True))
        rights.append(jnp.concatenate((value,) + columns(cols, lane), axis=1))
    right_b = []
    for par in range(2):
        cols = [jnp.sum(jnp.where(lane_b == 32 + par, a, 0.0), axis=1, keepdims=True) for a in keys_here]
        high, low = columns(cols, lane_b)
        right_b.append(jnp.concatenate(
            [tail[:, par, :], tail[:, 2 + par, :], high.astype(F32), low.astype(F32)], axis=1))
    right_b = jnp.concatenate(right_b, axis=0).astype(BF16)
    pick_q = iota((2 * nv, nv * 16), 1)
    pick_r = iota((2 * nv, nv * 16), 0)
    size = min(cpi, LANES)
    for t in range(max(1, cpi // LANES)):
        k = (me * cpi) // LANES + t
        lanes = pl.ds(pl.multiple_of(k * LANES, LANES), LANES)
        pick = ones_at(pick_q == (pick_r & (nv - 1)) * 16 + (pick_r // nv) * 8 + k)
        left = dot(pick, bt[...].reshape(nv * 16, LANES)).T.astype(BF16)
        both_b = dot(left, right_b)
        total = jnp.zeros((LANES, 3 * LANES), F32)
        for par in range(2):
            left = wf[:, par, :, :, lanes].reshape(nv * 16, LANES).astype(F32).T.astype(BF16)
            total = total + dot(left, rights[par])
        rb[:, 0:LANES] = total[:, 0:LANES] + both_b[:, 0:LANES] + both_b[:, LANES:2 * LANES]
        rb[:, LANES:] = (
            total[:, LANES:2 * LANES] + total[:, 2 * LANES:]
            + both_b[:, 2 * LANES:3 * LANES] + both_b[:, 3 * LANES:]
        )
        block = rb[pl.ds(pl.multiple_of(lax.rem(me * cpi, LANES), size), size), :]
        for d in range(size // rpd):
            to = t * (size // rpd) + d
            os_[to, 0:rpd, :] = block[d * rpd:(d + 1) * rpd, 0:LANES]
            os_[to, rpd:, :] = block[d * rpd:(d + 1) * rpd, LANES:]

    local(os_.at[row], or_.at[row], o_recv)

    @pl.loop(1, nt)
    def _(o):
        peer = lax.rem(row + o, nt)
        remote(os_.at[peer], or_.at[row], o_send, o_recv, (me, peer))

    pending.append(lambda: wait_for(or_.at[pl.ds(0, nt - 1)], o_send))
    wait_for(or_, o_recv)
    small = iota((rpd, LANES), 1)
    for k in range(nt):
        lanes = slice(k * LANES, (k + 1) * LANES)
        gkv_ref[:, width + k * LANES:width + (k + 1) * LANES] = or_[k, 0:rpd, :]
        keyed = or_[k, rpd:, :]
        spread_key = jnp.zeros((rpd, LANES), F32)
        for h in range(per):
            spread_key = jnp.where(small // HEAD_DIM == h, keyed[:, h:h + 1], spread_key)
        gkv_ref[:, lanes] = spread_key * query[:, lanes]

    for done in pending:
        done()


def copy_kernel(*refs):
    for k in range(4):
        refs[4 + k][...] = refs[k][...]


def shards(nv, nt, patches, embed_w, embed_b, query, kv_w, out_w, cotangent):
    width = kv_w.shape[0]
    rpd = width // (nv * nt)
    na = nv // nt
    vmem = pl.BlockSpec(memory_space=pltpu.VMEM)
    hbm = pl.BlockSpec(memory_space=pl.ANY)
    dma = pltpu.SemaphoreType.DMA
    tile = (16, LANES)
    rows = min(16, nv) * OWN
    crows = 4 * na * OWN
    outs = pl.pallas_call(
        functools.partial(kernel, nv, nt),
        out_shape=(
            jax.ShapeDtypeStruct((OWN, width), BF16),
            jax.ShapeDtypeStruct((rpd, 2 * width), F32),
            jax.ShapeDtypeStruct(embed_w.shape, F32),
            jax.ShapeDtypeStruct(embed_b.shape, F32),
        ),
        in_specs=[vmem] * 5 + [hbm] * 2,
        out_specs=(vmem,) * 4,
        scratch_shapes=[
            pltpu.VMEM((width, 2 * width), BF16),
            pltpu.VMEM((width, width), BF16),
            pltpu.VMEM((nv,) + tile, BF16),
            pltpu.VMEM((na, nt) + tile, BF16),
            pltpu.VMEM((8, 2, na, PIX, width), BF16),
            pltpu.VMEM((8, na) + tile, BF16),
            pltpu.VMEM(tile, BF16),
            pltpu.VMEM((nv // 2, 2, OWN, width), BF16),
            pltpu.VMEM((crows, width), BF16),
            pltpu.VMEM((2 * nv * OWN, width), BF16),
            pltpu.VMEM((2 * nv * OWN, LANES), F32),
            pltpu.VMEM((2 * nv * OWN, LANES), F32),
            pltpu.VMEM((4, 2, na) + tile, BF16),
            pltpu.VMEM((nv,) + tile, BF16),
            pltpu.VMEM((nt, GROWS, LANES), F32),
            pltpu.VMEM((nt, GROWS, LANES), F32),
            pltpu.VMEM((GROWS, LANES), F32),
            pltpu.VMEM((48, LANES), BF16),
            pltpu.VMEM((nt, GROWS, LANES), F32),
            pltpu.VMEM((2, 2, 2, na, 48, LANES), BF16),
            pltpu.VMEM((LANES, LANES), F32),
            pltpu.VMEM((2 * GROWS, 2 * width), BF16),
            pltpu.VMEM((LANES, 2 * LANES), F32),
            pltpu.VMEM((nt, 2 * rpd, LANES), F32),
            pltpu.VMEM((nt, 2 * rpd, LANES), F32),
            pltpu.VMEM((crows, crows // 2), BF16),
            pltpu.VMEM((nt, crows, crows // 2), BF16),
            pltpu.VMEM((3, crows // 2, crows), BF16),
            pltpu.VMEM((6, rows, rows), BF16),
            pltpu.VMEM((2 * (nv // min(16, nv)), LANES, rows), BF16),
            pltpu.VMEM((LANES, width), BF16),
            pltpu.VMEM((LANES, width), BF16),
            dma((2,)), dma, dma, dma((nv,)), dma, dma((nv,)), dma,
            dma((8,)), dma((8,)), dma((8,)), dma((8,)), dma((8,)), dma((8,)),
            dma, dma, dma, dma, dma, dma, dma, dma, dma, dma, dma, dma,
            dma, dma, dma, dma,
        ],
        compiler_params=pltpu.CompilerParams(
            collective_id=0, has_side_effects=True, vmem_limit_bytes=56 * 1024 * 1024
        ),
        cost_estimate=pl.CostEstimate(flops=5_000_000_000, bytes_accessed=8_000_000, transcendentals=20_000),
    )(patches, embed_w, embed_b, query, cotangent, kv_w, out_w)
    aggregated, grad_kv, grad_w, grad_b = pl.pallas_call(
        copy_kernel,
        out_shape=[jax.ShapeDtypeStruct(x.shape, x.dtype) for x in outs],
        in_specs=[vmem] * 4,
        out_specs=[vmem] * 4,
    )(*outs)
    return aggregated.reshape(cotangent.shape), grad_kv, grad_w, grad_b


def solution(mesh):
    return jax.shard_map(
        functools.partial(shards, mesh.shape["var"], mesh.shape["tok"]),
        mesh=mesh,
        in_specs=(
            P("var", "tok", None),
            P("var", None, None),
            P("var", None),
            P(),
            P(),
            P(),
            P("tok", "var", None),
        ),
        out_specs=(
            P("tok", "var", None),
            P(("var", "tok"), None),
            P("var", None, None),
            P("var", None),
        ),
        check_vma=False,
    )
```

```python
import functools

import jax
import jax.numpy as jnp
from jax import lax
from jax.experimental import pallas as pl
from jax.experimental.pallas import tpu as pltpu
from jax.sharding import PartitionSpec as P

MESH = pl.DeviceIdType.MESH
F32 = jnp.float32
BF16 = jnp.bfloat16
LANES = 128
PIX = 16
OWN = 16
HEADS = 16
HEAD_DIM = 64
TAIL = 34


def dot(a, b):
    return jnp.dot(a, b, preferred_element_type=F32)


def dot_nt(a, b):
    return lax.dot_general(a, b, (((1,), (1,)), ((), ())), preferred_element_type=F32)


def iota(shape, dim):
    return lax.broadcasted_iota(jnp.int32, shape, dim)


def ones_at(cond):
    return jnp.where(cond, 1.0, 0.0).astype(BF16)


def split(x):
    high = x.astype(BF16)
    return high, (x - high.astype(F32)).astype(BF16)


def remote(src, dst, send_sem, recv_sem, device):
    pltpu.make_async_remote_copy(
        src, dst, send_sem, recv_sem, device_id=device, device_id_type=MESH
    ).start()


def local(src, dst, sem):
    pltpu.make_async_copy(src, dst, sem).start()


def wait_for(ref, sem):
    pltpu.make_async_copy(ref, ref, sem).wait()


def kernel(
    nv, nt,
    p_ref, w_ref, b_ref, q_ref, cot_ref, kv_hbm, ow_hbm,
    agg_ref, gkv_ref, gw_ref, gb_ref,
    kv, ow, pl_, pg, pd, perm, px, wf, bt, bown, cgs, emb, val, st, wgt, stat_own, stat, wtr, xo, pixt,
    gs, g1, h1, g2, h2, g3, gp, gt, gk, gx, perm2, wbp, wt_c, ps, p1, q1, p2, os_, or_, ctx, cr, spread,
    load_sem, pg_send, pg_recv, w_send, w_recv, b_send, b_recv, px_send, px_recv, wc_send, wc_recv,
    cg_send, cg_recv, st_send, st_recv, g1_send, g1_recv, g2_send, g2_recv, g3_send, g3_recv,
    gt_send, gt_recv, p1_send, p1_recv, p2_send, p2_recv, o_send, o_recv, c_send, c_recv,
):
    me = lax.axis_index("var")
    row = lax.axis_index("tok")
    nz = nv // 4
    core = lax.rem(me, 2)
    zed = lax.rem(me // 2, nz)
    far = me // (2 * nz)
    sib = me + 1 - 2 * core
    width = kv.shape[0]
    toks = nt * OWN
    cw = width // nz
    per = HEADS // nz
    grows = gp.shape[0]
    cp = width // (4 * nt)
    rpd = cp // nz
    scale = HEAD_DIM ** -0.5
    pending = []

    def var_peer(o):
        return lax.rem(me + o, nv)

    def tok_peer(o):
        return lax.rem(row + o, nt)

    def at(y, z, c):
        return (y * nz + z) * 2 + c

    def group_of(i):
        return lax.rem(i + (nt // 2) * (i // (2 * nz)), nt), i // nt

    def owner_of(r, a):
        return nt * a + lax.rem(r + (nt // 2) * (a // 2), nt)

    my_r, my_a = group_of(me)
    sender = my_r == row

    load_ow = pltpu.make_async_copy(ow_hbm, ow, load_sem.at[0])
    load_kv = pltpu.make_async_copy(kv_hbm, kv, load_sem.at[1])

    barrier = pltpu.get_barrier_semaphore()

    def greet(device):
        pl.semaphore_signal(barrier, inc=1, device_id=device, device_id_type=MESH)

    @pl.loop(1, nv)
    def _(o):
        greet((var_peer(o), row))

    @pl.loop(1, nt)
    def _(o):
        greet((me, tok_peer(o)))
        greet((at(1 - far, zed, core), tok_peer(o)))

    @pl.loop(0, nz)
    def _(z):
        source = at(lax.rem(my_a, 2), z, my_a // 2)

        @pl.when(jnp.logical_not(jnp.logical_and(source == me, sender)))
        def _():
            greet((source, my_r))

    load_ow.start()
    load_kv.start()

    for k in range(nv):
        lanes = slice(k * LANES, (k + 1) * LANES)
        st_k = jnp.concatenate([p_ref[0, :, lanes].astype(F32), p_ref[1, :, lanes].astype(F32)], axis=0)
        cr[0, 4 * (k % 4):4 * (k % 4) + 4, 0:LANES] = st_k
        if k % 4 == 3:
            pl_[4 * k - 12:4 * k + 4, :] = cr[0, 0:16, 0:LANES].astype(BF16)
    bias = b_ref[...].astype(F32)
    bown[...] = jnp.concatenate(
        [bias[v:v + 1, k * LANES:(k + 1) * LANES] for v in range(2) for k in range(width // LANES)], axis=0
    ).astype(BF16)

    held = core * 2 + far
    mine = owner_of(row, held)
    pl.semaphore_wait(barrier, nv - 1 + 2 * (nt - 1) + nt - jnp.where(mine == me, 1, 0))

    @pl.when(sender)
    def _():
        local(pl_, pg.at[row], pg_recv)

    @pl.when(jnp.logical_not(sender))
    def _():
        remote(pl_, pg.at[row], pg_send, pg_recv, (me, my_r))

    @pl.when(sender)
    def _():
        local(w_ref.at[core], wf.at[my_a, core], w_recv.at[my_a])
        local(bown, bt.at[my_a], b_recv.at[my_a])

        @pl.loop(1, nv)
        def _(o):
            peer = var_peer(o)
            their = lax.rem(peer, 2)
            remote(w_ref.at[their], wf.at[my_a, their], w_send.at[o], w_recv.at[my_a], (peer, row))
            remote(bown, bt.at[my_a], b_send.at[o], b_recv.at[my_a], (peer, row))

        in_q = iota((256, 4 * nv * nt), 1)
        step = min(256, 4 * nv * nt)
        for blk in range(4 * nv * nt // step):
            o_q = iota((step, 4 * nv * nt), 0) + blk * step
            source = (((o_q >> 2) & (nt - 1)) * nv + o_q // (4 * nt)) * 4 + (o_q & 3)
            perm[blk * step:(blk + 1) * step, :] = ones_at(in_q[0:step] == source)
        wait_for(pg, pg_recv)
        pixels = dot(perm[...], pg[...].reshape(4 * nv * nt, LANES)).astype(BF16)
        pd[...] = pixels.reshape(nv, 4 * nt, LANES)
        local(pd.at[me], px.at[my_a], px_recv.at[my_a])

        @pl.loop(1, nv)
        def _(o):
            peer = var_peer(o)
            remote(pd.at[peer], px.at[my_a], px_send.at[o], px_recv.at[my_a], (peer, row))

    def first_sent():
        @pl.when(jnp.logical_not(sender))
        def _():
            wait_for(pl_, pg_send)

        @pl.when(sender)
        def _():
            @pl.loop(1, nv)
            def _(o):
                wait_for(w_ref.at[0], w_send.at[o])
                wait_for(bown, b_send.at[o])
                wait_for(pd.at[0], px_send.at[o])

    pending.append(first_sent)

    load_ow.wait()
    cot = cot_ref[...].astype(F32).reshape(OWN, width).astype(BF16)
    cgs[row] = dot_nt(cot, ow[...]).astype(BF16)

    @pl.loop(1, nt)
    def _(o):
        remote(cgs.at[row], cgs.at[row], cg_send.at[o], cg_recv.at[o], (me, tok_peer(o)))

    def cg_sent():
        @pl.loop(1, nt)
        def _(o):
            wait_for(cgs.at[0], cg_send.at[o])

    pending.append(cg_sent)

    lane2 = iota((2 * toks, LANES), 1)
    tok2 = iota((2 * toks, LANES), 0) & (toks - 1)
    par2 = iota((2 * toks, LANES), 0) // toks
    sel_k = iota((2 * toks, 4 * nt), 1)
    sel_r = iota((2 * toks, 4 * nt), 0)
    sel_t = sel_r & (toks - 1)
    sel = ones_at(sel_k == (sel_t >> 4) * 4 + (sel_r // toks) * 2 + ((sel_t >> 3) & 1))
    same_lon = (tok2 & 7) == (lane2 >> 4)
    fold = ones_at(
        ((iota((LANES, LANES), 0) & 15) == (iota((LANES, LANES), 1) & 15)) & (iota((LANES, LANES), 1) < 32)
    )
    query = q_ref[...].astype(F32).reshape(1, width)
    head_of = iota((width, LANES), 0) // HEAD_DIM == iota((width, LANES), 1)
    sum_heads = ones_at(head_of)
    q_cols = jnp.broadcast_to(query, (LANES, width)).T
    q_block = jnp.where(head_of, q_cols, 0.0).astype(BF16)
    spread[...] = ones_at(iota((LANES, width), 1) // HEAD_DIM == iota((LANES, width), 0))
    n_r = iota((width, LANES), 1)
    n_c = iota((width, LANES), 0)
    for blk in range(width // LANES):
        new = n_r + blk * LANES
        c_core = new // (2 * nt * cp)
        c_far = (new // (nt * cp)) & 1
        c_row = (new // cp) & (nt - 1)
        c_z = (new // rpd) & (nz - 1)
        c_e = new & (rpd - 1)
        old = ((((c_far * nz + c_z) * 2 + c_core) * nt) + c_row) * rpd + c_e
        perm2[:, blk * LANES:(blk + 1) * LANES] = ones_at(n_c == old)

    def weights_arrived(a):
        wait_for(wf.at[a, core], w_recv.at[a])
        remote(wf.at[a, core], wf.at[a, core], wc_send.at[a], wc_recv.at[a], (sib, row))

    def wc_sent():
        @pl.loop(0, 4)
        def _(a):
            wait_for(wf.at[a, 0], wc_send.at[a])

    pending.append(wc_sent)
    load_kv.wait()
    weights_arrived(0)

    @pl.loop(1, nt)
    def _(o):
        k = lax.rem(row - o + nt, nt)
        wait_for(cgs.at[k], cg_recv.at[o])

    cg_f = cgs[...].reshape(toks, width).astype(F32)

    def chunk(a):
        x = dot(sel, px[a])
        x = jnp.where(same_lon, x, 0.0).astype(BF16)
        x = jnp.where((lane2 >> 4) == par2, dot(x, fold), 0.0)
        with_ones = jnp.where(lane2 == 32 + par2, 1.0, x)
        for par in range(2):
            xo[a * 2 + par] = with_ones[par * toks:(par + 1) * toks].astype(BF16)
            pixt[a * 2 + par] = with_ones[par * toks:(par + 1) * toks].T[0:48].astype(BF16)
        x = x.astype(BF16)[:, 0:32]
        biases = bt[a].astype(F32)
        w = wf[a].reshape(32, width)
        for k in range(width // LANES):
            lanes = slice(k * LANES, (k + 1) * LANES)
            e = dot(x, w[:, lanes])
            n = width // LANES
            e = e + jnp.where(par2 == 0, biases[k:k + 1], biases[n + k:n + k + 1])
            emb[:, lanes] = e.astype(BF16)
        keys = dot(emb[...], kv[:, :width]).astype(BF16)
        s = (dot(keys, q_block) * scale).T
        values = dot(emb[...], kv[:, width:]).astype(BF16)
        product = values.astype(F32).reshape(2, toks, width) * cg_f[None]
        high, low = split(product.reshape(2 * toks, width))
        g = (dot(high, sum_heads) + dot(low, sum_heads)).T
        for par in range(2):
            mine = slice(par * toks, (par + 1) * toks)
            st[a * 2 + par] = s[0:HEADS, mine]
            wgt[a * 2 + par] = g[0:HEADS, mine]
            val[a * 2 + par] = values[mine]

    @pl.loop(0, 4)
    def _(a):
        @pl.when(a < 3)
        def _():
            weights_arrived(a + 1)

        wait_for(px.at[a], px_recv.at[a])
        wait_for(bt.at[a], b_recv.at[a])
        wait_for(wf.at[a, 1 - core], wc_recv.at[a])
        chunk(a)

    s = st[...]
    wg = wgt[...]
    top = jnp.max(s, axis=0)
    e = jnp.exp(s - top[None])
    stat_own[0:16] = top
    stat_own[16:32] = jnp.sum(e, axis=0)
    stat_own[32:48] = jnp.sum(e * wg, axis=0)

    @pl.loop(1, nt)
    def _(o):
        remote(stat_own, stat.at[o], st_send.at[o], st_recv.at[o], (me, tok_peer(o)))

    def st_sent():
        @pl.loop(1, nt)
        def _(o):
            wait_for(stat_own, st_send.at[o])

    pending.append(st_sent)

    pair = jnp.concatenate(
        [wf[held].reshape(32, width).astype(F32)]
        + [jnp.concatenate([bt[held].astype(F32)[par * 8 + k:par * 8 + k + 1] for k in range(width // LANES)], axis=1)
           for par in range(2)]
        + [jnp.zeros((LANES - TAIL, width), F32)], axis=0
    ).astype(BF16)
    wbp[...] = dot(pair, perm2[...]).astype(BF16)
    wt_c[...] = wbp[...].astype(F32).T.astype(BF16)

    stat[0] = stat_own[...]

    @pl.loop(1, nt)
    def _(o):
        wait_for(stat.at[o], st_recv.at[o])

    tops = stat[:, 0:16]
    highest = jnp.max(tops, axis=0)
    factor = jnp.exp(tops - highest[None])
    norm = jnp.sum(stat[:, 16:32] * factor, axis=0)
    mean = jnp.sum(stat[:, 32:48] * factor, axis=0) / norm
    weights_f = e * (jnp.exp(top - highest) / norm)[None]
    sg = weights_f * (wg - mean[None]) * scale
    wgt[...] = sg
    wtr[...] = weights_f.reshape(8 * HEADS, toks).T

    for a in range(4):
        g_val = jnp.zeros((48, width), F32)
        g_key = jnp.zeros((HEADS, LANES), F32)
        for v in (2 * a, 2 * a + 1):
            w = dot(wtr[:, v * HEADS:(v + 1) * HEADS].astype(BF16), spread[0:HEADS, :])
            value_grad = (w * cg_f).astype(BF16)
            g_val = g_val + dot(pixt[v], value_grad)
            high, low = split(wgt[v])
            g_key = g_key + dot(high, xo[v]) + dot(low, xo[v])
        to_core, to_far = a // 2, a % 2
        for z in range(nz):
            gs[to_core, to_far, z] = g_val[0:grows, z * cw:(z + 1) * cw]
            gs[to_core, to_far, z, TAIL:TAIL + per, 0:LANES] = g_key[z * per:(z + 1) * per, :]

    remote(gs.at[1 - core], g1, g1_send, g1_recv, (sib, row))
    pending.append(lambda: wait_for(g1, g1_send))
    wait_for(g1, g1_recv)
    h1[...] = gs[core] + g1[...]
    remote(h1.at[1 - far], g2, g2_send, g2_recv, (at(1 - far, zed, core), row))
    pending.append(lambda: wait_for(g2, g2_send))

    total = jnp.zeros((toks, width), F32)
    for v in range(8):
        w = dot(wtr[:, v * HEADS:(v + 1) * HEADS].astype(BF16), spread[0:HEADS, :])
        total = total + w * val[v].astype(F32)
    ctx[...] = total.reshape(nt, OWN, width)
    cr[row] = ctx[row]

    wait_for(g2, g2_recv)
    h2[...] = h1[far] + g2[...]

    @pl.loop(1, nz)
    def _(o):
        z = lax.rem(zed + o, nz)
        remote(h2.at[z], g3.at[o], g3_send.at[o], g3_recv.at[o], (at(far, z, core), row))

    def g3_sent():
        @pl.loop(1, nz)
        def _(o):
            wait_for(h2.at[0], g3_send.at[o])

    pending.append(g3_sent)

    @pl.loop(1, nt)
    def _(o):
        peer = tok_peer(o)
        remote(ctx.at[peer], cr.at[row], c_send.at[o], c_recv.at[o], (me, peer))

    def c_sent():
        @pl.loop(1, nt)
        def _(o):
            wait_for(ctx.at[0], c_send.at[o])

    pending.append(c_sent)
    g3[0] = h2[zed]

    @pl.loop(1, nz)
    def _(o):
        wait_for(g3.at[o], g3_recv.at[o])

    gp[...] = jnp.sum(g3[...], axis=0)

    def to_owner(r, then_remote, then_local):
        itself = jnp.logical_and(mine == me, r == row)

        @pl.when(itself)
        def _():
            then_local()

        @pl.when(jnp.logical_not(itself))
        def _():
            then_remote()

    lines = iota((grows, cw), 0)
    high, low = split(jnp.where(lines < TAIL, gp[...], 0.0))
    part = dot(wt_c[:, 0:grows], high) + dot(wt_c[:, 0:grows], low)
    keys_here = jnp.concatenate([gp[TAIL:TAIL + per, 0:LANES], jnp.zeros((16 - per, LANES), F32)], axis=0)
    high, low = split(keys_here)
    key_part = (dot(high, wbp[...]) + dot(low, wbp[...]))[0:8]
    for c in range(2):
        for y in range(2):
            for r in range(nt):
                k = (c * 2 + y) * nt + r
                ps[c, y, r, 0:cp, :] = part[k * cp:(k + 1) * cp]
                ps[c, y, r, cp:, :] = jnp.zeros((8, cw), F32)
                ps[c, y, r, cp:, 0:cp] = key_part[:, k * cp:(k + 1) * cp]

    remote(ps.at[1 - core], p1, p1_send, p1_recv, (sib, row))
    pending.append(lambda: wait_for(p1, p1_send))

    @pl.loop(0, nt)
    def _(r):
        to_owner(
            r,
            lambda: remote(gp, gt.at[zed], gt_send.at[r], gt_recv, (mine, r)),
            lambda: local(gp, gt.at[zed], gt_recv),
        )

    def gt_sent():
        @pl.loop(0, nt)
        def _(r):
            to_owner(r, lambda: wait_for(gp, gt_send.at[r]), lambda: None)

    pending.append(gt_sent)
    wait_for(p1, p1_recv)
    q1[...] = ps[core] + p1[...]

    @pl.loop(1, nt)
    def _(o):
        peer = tok_peer(o)
        remote(q1.at[far, peer], p2.at[far, row], p2_send.at[far, o], p2_recv, (me, peer))

    @pl.loop(0, nt)
    def _(o):
        peer = tok_peer(o)
        remote(
            q1.at[1 - far, peer], p2.at[far, row], p2_send.at[1 - far, o], p2_recv,
            (at(1 - far, zed, core), peer),
        )

    local(q1.at[far, row], p2.at[far, row], p2_recv)

    def p2_sent():
        @pl.loop(1, nt)
        def _(o):
            wait_for(q1.at[0, 0], p2_send.at[far, o])

        @pl.loop(0, nt)
        def _(o):
            wait_for(q1.at[0, 0], p2_send.at[1 - far, o])

    pending.append(p2_sent)

    def wait_c():
        @pl.loop(1, nt)
        def _(o):
            wait_for(cr.at[lax.rem(row - o + nt, nt)], c_recv.at[o])

    wait_c()
    context = jnp.sum(cr[...], axis=0).astype(BF16)
    agg_ref[...] = dot(context, ow[...]).astype(BF16)

    wait_for(gt, gt_recv)
    gk[...] = jnp.zeros((LANES, LANES), F32)
    for z in range(nz):
        gk[z * per:(z + 1) * per, :] = gt[z, TAIL:TAIL + per, 0:LANES]
        high, low = split(gt[z])
        lanes = slice(width + z * cw, width + (z + 1) * cw)
        gx[0:grows, lanes] = high
        gx[grows:, lanes] = low
    key_high, key_low = split(gk[...].T[0:grows])
    q_rows = (spread[...].astype(F32) * query).astype(BF16)
    high, low = split(dot(key_high, q_rows) + dot(key_low, q_rows))
    gx[0:grows, :width] = high
    gx[grows:, :width] = low

    wait_for(p2, p2_recv)
    mine_c = jnp.sum(p2[...].reshape(2 * nt, cp + 8, cw), axis=0)
    key_cols = jnp.concatenate([mine_c[cp:, 0:LANES], jnp.zeros((LANES - 8, LANES), F32)], axis=0).T
    for z in range(nz):
        os_[z, 0:rpd, :] = mine_c[z * rpd:(z + 1) * rpd]
        os_[z, rpd:, 0:LANES] = key_cols[z * rpd:(z + 1) * rpd]
    local(os_.at[zed], or_.at[zed], o_recv)

    @pl.loop(1, nz)
    def _(o):
        z = lax.rem(zed + o, nz)
        remote(os_.at[z], or_.at[zed], o_send.at[o], o_recv, (at(far, z, core), row))

    def o_sent():
        @pl.loop(1, nz)
        def _(o):
            wait_for(os_.at[0], o_send.at[o])

    pending.append(o_sent)

    both = dot_nt(gx[...], kv[...])
    table = both[0:grows] + both[grows:]
    gw_ref[0] = table[0:16]
    gw_ref[1] = table[16:32]
    gb_ref[...] = table[32:34]

    wait_for(or_, o_recv)
    small = iota((rpd, cw), 1)
    for z in range(nz):
        lanes = slice(z * cw, (z + 1) * cw)
        gkv_ref[:, width + z * cw:width + (z + 1) * cw] = or_[z, 0:rpd, :]
        keyed = or_[z, rpd:, :]
        spread_key = jnp.zeros((rpd, cw), F32)
        for h in range(per):
            spread_key = jnp.where(small // HEAD_DIM == h, keyed[:, h:h + 1], spread_key)
        gkv_ref[:, lanes] = spread_key * query[:, lanes]

    for done in pending:
        done()


def copy_kernel(*refs):
    for k in range(4):
        refs[4 + k][...] = refs[k][...]


def shards(nv, nt, patches, embed_w, embed_b, query, kv_w, out_w, cotangent):
    width = kv_w.shape[0]
    rpd = width // (nv * nt)
    nz = nv // 4
    cw = width // nz
    grows = -(-(TAIL + HEADS // nz) // 8) * 8
    cp = width // (4 * nt)
    toks = nt * OWN
    vmem = pl.BlockSpec(memory_space=pltpu.VMEM)
    hbm = pl.BlockSpec(memory_space=pl.ANY)
    dma = pltpu.SemaphoreType.DMA
    f32 = lambda *shape: pltpu.VMEM(shape, F32)
    bf16 = lambda *shape: pltpu.VMEM(shape, BF16)
    outs = pl.pallas_call(
        functools.partial(kernel, nv, nt),
        out_shape=(
            jax.ShapeDtypeStruct((OWN, width), BF16),
            jax.ShapeDtypeStruct((rpd, 2 * width), F32),
            jax.ShapeDtypeStruct(embed_w.shape, F32),
            jax.ShapeDtypeStruct(embed_b.shape, F32),
        ),
        in_specs=[vmem] * 5 + [hbm] * 2,
        out_specs=(vmem,) * 4,
        scratch_shapes=[
            bf16(width, 2 * width),
            bf16(width, width),
            bf16(4 * nv, LANES),
            bf16(nt, 4 * nv, LANES),
            bf16(nv, 4 * nt, LANES),
            bf16(4 * nv * nt, 4 * nv * nt),
            bf16(4, 4 * nt, LANES),
            bf16(4, 2, PIX, width),
            bf16(4, 16, LANES),
            bf16(16, LANES),
            bf16(nt, OWN, width),
            bf16(2 * toks, width),
            bf16(8, toks, width),
            f32(8, HEADS, toks),
            f32(8, HEADS, toks),
            f32(48, toks),
            f32(nt, 48, toks),
            f32(toks, LANES),
            bf16(8, toks, LANES),
            bf16(8, 48, toks),
            f32(2, 2, nz, grows, cw),
            f32(2, nz, grows, cw),
            f32(2, nz, grows, cw),
            f32(nz, grows, cw),
            f32(nz, grows, cw),
            f32(nz, grows, cw),
            f32(grows, cw),
            f32(nz, grows, cw),
            f32(LANES, LANES),
            bf16(2 * grows, 2 * width),
            bf16(width, width),
            bf16(LANES, width),
            bf16(width, LANES),
            f32(2, 2, nt, cp + 8, cw),
            f32(2, nt, cp + 8, cw),
            f32(2, nt, cp + 8, cw),
            f32(2, nt, cp + 8, cw),
            f32(nz, 2 * rpd, cw),
            f32(nz, 2 * rpd, cw),
            f32(nt, OWN, width),
            f32(nt, OWN, width),
            bf16(LANES, width),
            dma((2,)), dma, dma, dma((nv,)), dma((4,)), dma((nv,)), dma((4,)), dma((nv,)), dma((4,)), dma((4,)), dma((4,)),
            dma((nt,)), dma((nt,)), dma((nt,)), dma((nt,)), dma, dma, dma, dma, dma((nz,)), dma((nz,)),
            dma((nt,)), dma, dma, dma, dma((2, nt)), dma, dma((nz,)), dma, dma((nt,)), dma((nt,)),
        ],
        compiler_params=pltpu.CompilerParams(
            collective_id=0, has_side_effects=True, vmem_limit_bytes=56 * 1024 * 1024
        ),
        cost_estimate=pl.CostEstimate(flops=5_000_000_000, bytes_accessed=8_000_000, transcendentals=20_000),
    )(patches, embed_w, embed_b, query, cotangent, kv_w, out_w)
    aggregated, grad_kv, grad_w, grad_b = pl.pallas_call(
        copy_kernel,
        out_shape=[jax.ShapeDtypeStruct(x.shape, x.dtype) for x in outs],
        in_specs=[vmem] * 4,
        out_specs=[vmem] * 4,
    )(*outs)
    return aggregated.reshape(cotangent.shape), grad_kv, grad_w, grad_b


def solution(mesh):
    return jax.shard_map(
        functools.partial(shards, mesh.shape["var"], mesh.shape["tok"]),
        mesh=mesh,
        in_specs=(
            P("var", "tok", None),
            P("var", None, None),
            P("var", None),
            P(),
            P(),
            P(),
            P("tok", "var", None),
        ),
        out_specs=(
            P("tok", "var", None),
            P(("var", "tok"), None),
            P("var", None, None),
            P("var", None),
        ),
        check_vma=False,
    )
```

```python
import functools

import jax
import jax.numpy as jnp
import numpy as np
from jax import lax
from jax.experimental import pallas as pl
from jax.experimental.pallas import tpu as pltpu
from jax.sharding import PartitionSpec as P

MESH = pl.DeviceIdType.MESH
F32 = jnp.float32
BF16 = jnp.bfloat16
LANES = 128
PIX = 16
OWN = 16
HEADS = 16
HEAD_DIM = 64
TAIL = 34


def dot(a, b):
    return jnp.dot(a, b, preferred_element_type=F32)


def dot_nt(a, b):
    return lax.dot_general(a, b, (((1,), (1,)), ((), ())), preferred_element_type=F32)


def iota(shape, dim):
    return lax.broadcasted_iota(jnp.int32, shape, dim)


def ones_at(cond):
    return jnp.where(cond, 1.0, 0.0).astype(BF16)


def split(x):
    high = x.astype(BF16)
    return high, (x - high.astype(F32)).astype(BF16)


def bits(n):
    return n.bit_length() - 1


def remote(src, dst, send_sem, recv_sem, device):
    pltpu.make_async_remote_copy(
        src, dst, send_sem, recv_sem, device_id=device, device_id_type=MESH
    ).start()


def local(src, dst, sem):
    pltpu.make_async_copy(src, dst, sem).start()


def wait_for(ref, sem):
    pltpu.make_async_copy(ref, ref, sem).wait()


def kernel(
    nv, nt,
    p_ref, w_ref, b_ref, q_ref, cot_ref, kv_hbm, ow_hbm, perm_hbm,
    agg_ref, gkv_ref, gw_ref, gb_ref,
    kv, ow, pl_, pg, pd, px, wf, bt, bown, cgs, emb, val, st, wgt, stat_own, stat, wtr, xo, pixt,
    gs, g1, h1, g2, h2, g3, gp, gt, gk, gx, perm2, wbp, wt_c, ps, p1, q1, p2, os_, or_, ctx, cr, spread,
    load_sem, pg_send, pg_recv, w_send, w_recv, b_send, b_recv, px_send, px_recv, wc_send, wc_recv,
    cg_send, cg_recv, st_send, st_recv, g1_send, g1_recv, g2_send, g2_recv, g3_send, g3_recv,
    gt_send, gt_recv, p1_send, p1_recv, p2_send, p2_recv, o_send, o_recv, c_send, c_recv,
):
    me = lax.axis_index("var")
    row = lax.axis_index("tok")
    nz = nv // 4
    core = lax.rem(me, 2)
    zed = lax.rem(me // 2, nz)
    far = me // (2 * nz)
    sib = me + 1 - 2 * core
    width = kv.shape[0]
    toks = nt * OWN
    cw = width // nz
    per = HEADS // nz
    grows = gp.shape[0]
    cp = width // (4 * nt)
    rpd = cp // nz
    scale = HEAD_DIM ** -0.5
    pending = []

    def tok_peer(o):
        return lax.rem(row + o, nt)

    def at(y, z, c):
        return (y * nz + z) * 2 + c

    def group_of(i):
        return lax.rem(i + (nt // 2) * (i // (2 * nz)), nt), i // nt

    def owner_of(r, a):
        return nt * a + lax.rem(r + (nt // 2) * (a // 2), nt)

    my_r, my_a = group_of(me)
    sender = my_r == row

    load_ow = pltpu.make_async_copy(ow_hbm, ow, load_sem.at[0])
    load_kv = pltpu.make_async_copy(kv_hbm, kv, load_sem.at[1])
    load_perm = pltpu.make_async_copy(perm_hbm, perm2, load_sem.at[2])

    barrier = pltpu.get_barrier_semaphore()

    def greet(device):
        pl.semaphore_signal(barrier, inc=1, device_id=device, device_id_type=MESH)

    greet((sib, row))

    @pl.loop(1, nz)
    def _(o):
        greet((at(far, lax.rem(zed + o, nz), core), row))

    @pl.loop(0, nt)
    def _(o):
        greet((at(1 - far, zed, core), tok_peer(o)))

    @pl.loop(0, 4)
    def _(b):
        partner = owner_of(row, b)

        @pl.when(jnp.logical_not(jnp.logical_and(partner == me, sender)))
        def _():
            greet((partner, my_r))

    @pl.loop(1, nt)
    def _(o):
        greet((me, tok_peer(o)))

    @pl.loop(0, nz)
    def _(z):
        source = at(lax.rem(my_a, 2), z, my_a // 2)

        @pl.when(jnp.logical_not(jnp.logical_and(source == me, sender)))
        def _():
            greet((source, my_r))

    load_ow.start()
    load_kv.start()
    load_perm.start()

    for r in range(nt):
        parts = []
        for b in range(4):
            k = nt * b + (r + (nt // 2) * (b // 2)) % nt
            parts += [p_ref[v, :, k * LANES:(k + 1) * LANES].astype(F32) for v in range(2)]
        pl_[r] = jnp.concatenate(parts, axis=0).astype(BF16)
    bias = b_ref[...].astype(F32)
    bown[...] = jnp.concatenate(
        [bias[v:v + 1, k * LANES:(k + 1) * LANES] for v in range(2) for k in range(width // LANES)], axis=0
    ).astype(BF16)

    held = core * 2 + far
    mine = owner_of(row, held)
    unsent = jnp.where(mine == me, 1, 0) + jnp.where(sender, 1, 0)
    pl.semaphore_wait(barrier, 1 + (nz - 1) + nt + 4 + (nt - 1) + nt - unsent)

    local(pl_.at[row], pg.at[row], pg_recv)

    @pl.loop(1, nt)
    def _(o):
        peer = tok_peer(o)
        remote(pl_.at[peer], pg.at[row], pg_send.at[o], pg_recv, (me, peer))

    def to_partner(b, then_remote, then_local):
        partner = owner_of(row, b)
        itself = jnp.logical_and(partner == me, sender)

        @pl.when(itself)
        def _():
            then_local()

        @pl.when(jnp.logical_not(itself))
        def _():
            then_remote(partner, lax.rem(partner, 2))

    def send_weights(b):
        def away(partner, their):
            device = (partner, my_r)
            remote(w_ref.at[their], wf.at[my_a, their], w_send.at[b], w_recv.at[my_a], device)
            remote(bown, bt.at[my_a], b_send.at[b], b_recv.at[my_a], device)

        def here():
            local(w_ref.at[core], wf.at[my_a, core], w_recv.at[my_a])
            local(bown, bt.at[my_a], b_recv.at[my_a])

        to_partner(b, away, here)

    def send_pixels(b):
        to_partner(
            b,
            lambda partner, _: remote(pd.at[b], px.at[my_a], px_send.at[b], px_recv.at[my_a], (partner, my_r)),
            lambda: local(pd.at[b], px.at[my_a], px_recv.at[my_a]),
        )

    def partner_sent(b):
        def away(partner, their):
            wait_for(w_ref.at[0], w_send.at[b])
            wait_for(bown, b_send.at[b])
            wait_for(pd.at[0], px_send.at[b])

        to_partner(b, away, lambda: None)

    def first_sent():
        @pl.loop(1, nt)
        def _(o):
            wait_for(pl_.at[0], pg_send.at[o])

        pl.loop(0, 4)(partner_sent)

    pending.append(first_sent)
    pl.loop(0, 4)(send_weights)
    lines = 16 * nt
    o_q = iota((lines, lines), 0)
    order = ones_at(
        iota((lines, lines), 1) == ((o_q >> 2) & (nt - 1)) * 16 + (o_q >> bits(4 * nt)) * 4 + (o_q & 3)
    )
    wait_for(pg, pg_recv)
    pd[...] = dot(order, pg[...].reshape(lines, LANES)).astype(BF16).reshape(4, 4 * nt, LANES)
    pl.loop(0, 4)(send_pixels)

    load_ow.wait()
    cot = cot_ref[...].astype(F32).reshape(OWN, width).astype(BF16)
    cgs[row] = dot_nt(cot, ow[...]).astype(BF16)

    @pl.loop(1, nt)
    def _(o):
        remote(cgs.at[row], cgs.at[row], cg_send.at[o], cg_recv.at[o], (me, tok_peer(o)))

    def cg_sent():
        @pl.loop(1, nt)
        def _(o):
            wait_for(cgs.at[0], cg_send.at[o])

    pending.append(cg_sent)

    lane2 = iota((2 * toks, LANES), 1)
    tok2 = iota((2 * toks, LANES), 0) & (toks - 1)
    par2 = iota((2 * toks, LANES), 0) >> bits(toks)
    sel_k = iota((2 * toks, 4 * nt), 1)
    sel_r = iota((2 * toks, 4 * nt), 0)
    sel_t = sel_r & (toks - 1)
    sel = ones_at(sel_k == (sel_t >> 4) * 4 + (sel_r >> bits(toks)) * 2 + ((sel_t >> 3) & 1))
    same_lon = (tok2 & 7) == (lane2 >> 4)
    fold = ones_at(
        ((iota((LANES, LANES), 0) & 15) == (iota((LANES, LANES), 1) & 15)) & (iota((LANES, LANES), 1) < 32)
    )
    query = q_ref[...].astype(F32).reshape(1, width)
    head_of = (iota((width, LANES), 0) >> bits(HEAD_DIM)) == iota((width, LANES), 1)
    sum_heads = ones_at(head_of)
    q_cols = jnp.broadcast_to(query, (LANES, width)).T
    q_block = jnp.where(head_of, q_cols, 0.0).astype(BF16)
    spread[...] = ones_at((iota((LANES, width), 1) >> bits(HEAD_DIM)) == iota((LANES, width), 0))
    def weights_arrived(a):
        wait_for(wf.at[a, core], w_recv.at[a])
        remote(wf.at[a, core], wf.at[a, core], wc_send.at[a], wc_recv.at[a], (sib, row))

    def wc_sent():
        @pl.loop(0, 4)
        def _(a):
            wait_for(wf.at[a, 0], wc_send.at[a])

    pending.append(wc_sent)
    load_kv.wait()
    weights_arrived(0)

    @pl.loop(1, nt)
    def _(o):
        k = lax.rem(row - o + nt, nt)
        wait_for(cgs.at[k], cg_recv.at[o])

    cg_f = cgs[...].reshape(toks, width).astype(F32)

    def chunk(a):
        x = dot(sel, px[a])
        x = jnp.where(same_lon, x, 0.0).astype(BF16)
        x = jnp.where((lane2 >> 4) == par2, dot(x, fold), 0.0)
        with_ones = jnp.where(lane2 == 32 + par2, 1.0, x)
        for par in range(2):
            xo[a * 2 + par] = with_ones[par * toks:(par + 1) * toks].astype(BF16)
            pixt[a * 2 + par] = with_ones[par * toks:(par + 1) * toks].T[0:48].astype(BF16)
        x = x.astype(BF16)[:, 0:32]
        biases = bt[a].astype(F32)
        w = wf[a].reshape(32, width)
        for k in range(width // LANES):
            lanes = slice(k * LANES, (k + 1) * LANES)
            e = dot(x, w[:, lanes])
            n = width // LANES
            e = e + jnp.where(par2 == 0, biases[k:k + 1], biases[n + k:n + k + 1])
            emb[:, lanes] = e.astype(BF16)
        keys = dot(emb[...], kv[:, :width]).astype(BF16)
        s = (dot(keys, q_block) * scale).T
        values = dot(emb[...], kv[:, width:]).astype(BF16)
        product = values.astype(F32).reshape(2, toks, width) * cg_f[None]
        high, low = split(product.reshape(2 * toks, width))
        g = (dot(high, sum_heads) + dot(low, sum_heads)).T
        for par in range(2):
            mine = slice(par * toks, (par + 1) * toks)
            st[a * 2 + par] = s[0:HEADS, mine]
            wgt[a * 2 + par] = g[0:HEADS, mine]
            val[a * 2 + par] = values[mine]

    @pl.loop(0, 4)
    def _(a):
        @pl.when(a < 3)
        def _():
            weights_arrived(a + 1)

        wait_for(px.at[a], px_recv.at[a])
        wait_for(bt.at[a], b_recv.at[a])
        wait_for(wf.at[a, 1 - core], wc_recv.at[a])
        chunk(a)

    s = st[...]
    wg = wgt[...]
    top = jnp.max(s, axis=0)
    e = jnp.exp(s - top[None])
    stat_own[0:16] = top
    stat_own[16:32] = jnp.sum(e, axis=0)
    stat_own[32:48] = jnp.sum(e * wg, axis=0)

    @pl.loop(1, nt)
    def _(o):
        remote(stat_own, stat.at[o], st_send.at[o], st_recv.at[o], (me, tok_peer(o)))

    def st_sent():
        @pl.loop(1, nt)
        def _(o):
            wait_for(stat_own, st_send.at[o])

    pending.append(st_sent)

    load_perm.wait()
    pair = jnp.concatenate(
        [wf[held].reshape(32, width).astype(F32)]
        + [jnp.concatenate([bt[held].astype(F32)[par * 8 + k:par * 8 + k + 1] for k in range(width // LANES)], axis=1)
           for par in range(2)]
        + [jnp.zeros((LANES - TAIL, width), F32)], axis=0
    ).astype(BF16)
    wbp[...] = dot(pair, perm2[...]).astype(BF16)
    wt_c[...] = wbp[...].astype(F32).T.astype(BF16)

    stat[0] = stat_own[...]

    @pl.loop(1, nt)
    def _(o):
        wait_for(stat.at[o], st_recv.at[o])

    tops = stat[:, 0:16]
    highest = jnp.max(tops, axis=0)
    factor = jnp.exp(tops - highest[None])
    norm = jnp.sum(stat[:, 16:32] * factor, axis=0)
    mean = jnp.sum(stat[:, 32:48] * factor, axis=0) / norm
    weights_f = e * (jnp.exp(top - highest) / norm)[None]
    sg = weights_f * (wg - mean[None]) * scale
    wgt[...] = sg
    wtr[...] = weights_f.reshape(8 * HEADS, toks).T

    for a in range(4):
        g_val = jnp.zeros((48, width), F32)
        g_key = jnp.zeros((HEADS, LANES), F32)
        for v in (2 * a, 2 * a + 1):
            w = dot(wtr[:, v * HEADS:(v + 1) * HEADS].astype(BF16), spread[0:HEADS, :])
            value_grad = (w * cg_f).astype(BF16)
            g_val = g_val + dot(pixt[v], value_grad)
            high, low = split(wgt[v])
            g_key = g_key + dot(high, xo[v]) + dot(low, xo[v])
        to_core, to_far = a // 2, a % 2
        for z in range(nz):
            gs[to_core, to_far, z] = g_val[0:grows, z * cw:(z + 1) * cw]
            gs[to_core, to_far, z, TAIL:TAIL + per, 0:LANES] = g_key[z * per:(z + 1) * per, :]

    remote(gs.at[1 - core], g1, g1_send, g1_recv, (sib, row))
    pending.append(lambda: wait_for(g1, g1_send))
    wait_for(g1, g1_recv)
    h1[...] = gs[core] + g1[...]
    remote(h1.at[1 - far], g2, g2_send, g2_recv, (at(1 - far, zed, core), row))
    pending.append(lambda: wait_for(g2, g2_send))

    total = jnp.zeros((toks, width), F32)
    for v in range(8):
        w = dot(wtr[:, v * HEADS:(v + 1) * HEADS].astype(BF16), spread[0:HEADS, :])
        total = total + w * val[v].astype(F32)
    ctx[...] = total.reshape(nt, OWN, width)
    cr[row] = ctx[row]

    wait_for(g2, g2_recv)
    h2[...] = h1[far] + g2[...]

    @pl.loop(1, nz)
    def _(o):
        z = lax.rem(zed + o, nz)
        remote(h2.at[z], g3.at[o], g3_send.at[o], g3_recv.at[o], (at(far, z, core), row))

    def g3_sent():
        @pl.loop(1, nz)
        def _(o):
            wait_for(h2.at[0], g3_send.at[o])

    pending.append(g3_sent)

    @pl.loop(1, nt)
    def _(o):
        peer = tok_peer(o)
        remote(ctx.at[peer], cr.at[row], c_send.at[o], c_recv.at[o], (me, peer))

    def c_sent():
        @pl.loop(1, nt)
        def _(o):
            wait_for(ctx.at[0], c_send.at[o])

    pending.append(c_sent)

    def wait_c():
        @pl.loop(1, nt)
        def _(o):
            wait_for(cr.at[lax.rem(row - o + nt, nt)], c_recv.at[o])

    g3[0] = h2[zed]

    @pl.loop(1, nz)
    def _(o):
        wait_for(g3.at[o], g3_recv.at[o])

    gp[...] = jnp.sum(g3[...], axis=0)

    def to_owner(r, then_remote, then_local):
        itself = jnp.logical_and(mine == me, r == row)

        @pl.when(itself)
        def _():
            then_local()

        @pl.when(jnp.logical_not(itself))
        def _():
            then_remote()

    lines = iota((grows, cw), 0)
    high, low = split(jnp.where(lines < TAIL, gp[...], 0.0))
    part = dot(wt_c[:, 0:grows], high) + dot(wt_c[:, 0:grows], low)
    keys_here = jnp.concatenate([gp[TAIL:TAIL + per, 0:LANES], jnp.zeros((16 - per, LANES), F32)], axis=0)
    high, low = split(keys_here)
    key_part = (dot(high, wbp[...]) + dot(low, wbp[...]))[0:8]
    for c in range(2):
        for y in range(2):
            for r in range(nt):
                k = (c * 2 + y) * nt + r
                ps[c, y, r, 0:cp, :] = part[k * cp:(k + 1) * cp]
                ps[c, y, r, cp:, :] = jnp.zeros((8, cw), F32)
                ps[c, y, r, cp:, 0:cp] = key_part[:, k * cp:(k + 1) * cp]

    remote(ps.at[1 - core], p1, p1_send, p1_recv, (sib, row))
    pending.append(lambda: wait_for(p1, p1_send))

    @pl.loop(0, nt)
    def _(r):
        to_owner(
            r,
            lambda: remote(gp, gt.at[zed], gt_send.at[r], gt_recv, (mine, r)),
            lambda: local(gp, gt.at[zed], gt_recv),
        )

    def gt_sent():
        @pl.loop(0, nt)
        def _(r):
            to_owner(r, lambda: wait_for(gp, gt_send.at[r]), lambda: None)

    pending.append(gt_sent)
    wait_for(p1, p1_recv)
    q1[...] = ps[core] + p1[...]

    @pl.loop(1, nt)
    def _(o):
        peer = tok_peer(o)
        remote(q1.at[far, peer], p2.at[far, row], p2_send.at[far, o], p2_recv, (me, peer))

    @pl.loop(0, nt)
    def _(o):
        peer = tok_peer(o)
        remote(
            q1.at[1 - far, peer], p2.at[far, row], p2_send.at[1 - far, o], p2_recv,
            (at(1 - far, zed, core), peer),
        )

    local(q1.at[far, row], p2.at[far, row], p2_recv)

    def p2_sent():
        @pl.loop(1, nt)
        def _(o):
            wait_for(q1.at[0, 0], p2_send.at[far, o])

        @pl.loop(0, nt)
        def _(o):
            wait_for(q1.at[0, 0], p2_send.at[1 - far, o])

    pending.append(p2_sent)

    wait_c()
    context = jnp.sum(cr[...], axis=0).astype(BF16)
    agg_ref[...] = dot(context, ow[...]).astype(BF16)

    wait_for(gt, gt_recv)
    gk[...] = jnp.zeros((LANES, LANES), F32)
    for z in range(nz):
        gk[z * per:(z + 1) * per, :] = gt[z, TAIL:TAIL + per, 0:LANES]
        high, low = split(gt[z])
        lanes = slice(width + z * cw, width + (z + 1) * cw)
        gx[0:grows, lanes] = high
        gx[grows:, lanes] = low
    key_high, key_low = split(gk[...].T[0:grows])
    q_rows = (spread[...].astype(F32) * query).astype(BF16)
    high, low = split(dot(key_high, q_rows) + dot(key_low, q_rows))
    gx[0:grows, :width] = high
    gx[grows:, :width] = low

    wait_for(p2, p2_recv)
    mine_c = jnp.sum(p2[...].reshape(2 * nt, cp + 8, cw), axis=0)
    key_cols = jnp.concatenate([mine_c[cp:, 0:LANES], jnp.zeros((LANES - 8, LANES), F32)], axis=0).T
    for z in range(nz):
        os_[z, 0:rpd, :] = mine_c[z * rpd:(z + 1) * rpd]
        os_[z, rpd:, 0:LANES] = key_cols[z * rpd:(z + 1) * rpd]
    local(os_.at[zed], or_.at[zed], o_recv)

    @pl.loop(1, nz)
    def _(o):
        z = lax.rem(zed + o, nz)
        remote(os_.at[z], or_.at[zed], o_send.at[o], o_recv, (at(far, z, core), row))

    def o_sent():
        @pl.loop(1, nz)
        def _(o):
            wait_for(os_.at[0], o_send.at[o])

    pending.append(o_sent)

    both = dot_nt(gx[...], kv[...])
    table = both[0:grows] + both[grows:]
    gw_ref[0] = table[0:16]
    gw_ref[1] = table[16:32]
    gb_ref[...] = table[32:34]

    wait_for(or_, o_recv)
    small = iota((rpd, cw), 1)
    for z in range(nz):
        lanes = slice(z * cw, (z + 1) * cw)
        gkv_ref[:, width + z * cw:width + (z + 1) * cw] = or_[z, 0:rpd, :]
        keyed = or_[z, rpd:, :]
        spread_key = jnp.zeros((rpd, cw), F32)
        for h in range(per):
            spread_key = jnp.where((small >> bits(HEAD_DIM)) == h, keyed[:, h:h + 1], spread_key)
        gkv_ref[:, lanes] = spread_key * query[:, lanes]

    for done in pending:
        done()


def copy_kernel(*refs):
    for k in range(4):
        refs[4 + k][...] = refs[k][...]


def shards(nv, nt, patches, embed_w, embed_b, query, kv_w, out_w, cotangent):
    width = kv_w.shape[0]
    rpd = width // (nv * nt)
    nz = nv // 4
    cw = width // nz
    grows = -(-(TAIL + HEADS // nz) // 8) * 8
    cp = width // (4 * nt)
    toks = nt * OWN
    order = np.arange(width).reshape(2, nz, 2, nt, rpd).transpose(2, 0, 3, 1, 4).reshape(-1)
    order = (np.arange(width)[:, None] == order[None, :]).astype(BF16)
    vmem = pl.BlockSpec(memory_space=pltpu.VMEM)
    hbm = pl.BlockSpec(memory_space=pl.ANY)
    dma = pltpu.SemaphoreType.DMA
    f32 = lambda *shape: pltpu.VMEM(shape, F32)
    bf16 = lambda *shape: pltpu.VMEM(shape, BF16)
    outs = pl.pallas_call(
        functools.partial(kernel, nv, nt),
        out_shape=(
            jax.ShapeDtypeStruct((OWN, width), BF16),
            jax.ShapeDtypeStruct((rpd, 2 * width), F32),
            jax.ShapeDtypeStruct(embed_w.shape, F32),
            jax.ShapeDtypeStruct(embed_b.shape, F32),
        ),
        in_specs=[vmem] * 5 + [hbm] * 3,
        out_specs=(vmem,) * 4,
        scratch_shapes=[
            bf16(width, 2 * width),
            bf16(width, width),
            bf16(nt, 16, LANES),
            bf16(nt, 16, LANES),
            bf16(4, 4 * nt, LANES),
            bf16(4, 4 * nt, LANES),
            bf16(4, 2, PIX, width),
            bf16(4, 16, LANES),
            bf16(16, LANES),
            bf16(nt, OWN, width),
            bf16(2 * toks, width),
            bf16(8, toks, width),
            f32(8, HEADS, toks),
            f32(8, HEADS, toks),
            f32(48, toks),
            f32(nt, 48, toks),
            f32(toks, LANES),
            bf16(8, toks, LANES),
            bf16(8, 48, toks),
            f32(2, 2, nz, grows, cw),
            f32(2, nz, grows, cw),
            f32(2, nz, grows, cw),
            f32(nz, grows, cw),
            f32(nz, grows, cw),
            f32(nz, grows, cw),
            f32(grows, cw),
            f32(nz, grows, cw),
            f32(LANES, LANES),
            bf16(2 * grows, 2 * width),
            bf16(width, width),
            bf16(LANES, width),
            bf16(width, LANES),
            f32(2, 2, nt, cp + 8, cw),
            f32(2, nt, cp + 8, cw),
            f32(2, nt, cp + 8, cw),
            f32(2, nt, cp + 8, cw),
            f32(nz, 2 * rpd, cw),
            f32(nz, 2 * rpd, cw),
            f32(nt, OWN, width),
            f32(nt, OWN, width),
            bf16(LANES, width),
            dma((3,)), dma((nt,)), dma, dma((4,)), dma((4,)), dma((4,)), dma((4,)), dma((4,)), dma((4,)), dma((4,)), dma((4,)),
            dma((nt,)), dma((nt,)), dma((nt,)), dma((nt,)), dma, dma, dma, dma, dma((nz,)), dma((nz,)),
            dma((nt,)), dma, dma, dma, dma((2, nt)), dma, dma((nz,)), dma, dma((nt,)), dma((nt,)),
        ],
        compiler_params=pltpu.CompilerParams(
            collective_id=0, has_side_effects=True, vmem_limit_bytes=56 * 1024 * 1024
        ),
        cost_estimate=pl.CostEstimate(flops=5_000_000_000, bytes_accessed=8_000_000, transcendentals=20_000),
    )(patches, embed_w, embed_b, query, cotangent, kv_w, out_w, order)
    aggregated, grad_kv, grad_w, grad_b = pl.pallas_call(
        copy_kernel,
        out_shape=[jax.ShapeDtypeStruct(x.shape, x.dtype) for x in outs],
        in_specs=[vmem] * 4,
        out_specs=[vmem] * 4,
    )(*outs)
    return aggregated.reshape(cotangent.shape), grad_kv, grad_w, grad_b


def solution(mesh):
    return jax.shard_map(
        functools.partial(shards, mesh.shape["var"], mesh.shape["tok"]),
        mesh=mesh,
        in_specs=(
            P("var", "tok", None),
            P("var", None, None),
            P("var", None),
            P(),
            P(),
            P(),
            P("tok", "var", None),
        ),
        out_specs=(
            P("tok", "var", None),
            P(("var", "tok"), None),
            P("var", None, None),
            P("var", None),
        ),
        check_vma=False,
    )
```

```python
import functools

import jax
import jax.numpy as jnp
from jax import lax
from jax.experimental import pallas as pl
from jax.experimental.pallas import tpu as pltpu
from jax.sharding import PartitionSpec as P

MESH = pl.DeviceIdType.MESH
F32 = jnp.float32
BF16 = jnp.bfloat16
LANES = 128
PIX = 16
OWN = 16
HEADS = 16
HEAD_DIM = 64
SPLIT = 24
TAIL = 34


def dot(a, b):
    return jnp.dot(a, b, preferred_element_type=F32)


def dot_nt(a, b):
    return lax.dot_general(a, b, (((1,), (1,)), ((), ())), preferred_element_type=F32)


def iota(shape, dim):
    return lax.broadcasted_iota(jnp.int32, shape, dim)


def ones_at(cond):
    return jnp.where(cond, 1.0, 0.0).astype(BF16)


def split(x):
    high = x.astype(BF16)
    return high, (x - high.astype(F32)).astype(BF16)


def bits(n):
    return n.bit_length() - 1


def remote(src, dst, send_sem, recv_sem, device):
    pltpu.make_async_remote_copy(
        src, dst, send_sem, recv_sem, device_id=device, device_id_type=MESH
    ).start()


def local(src, dst, sem):
    pltpu.make_async_copy(src, dst, sem).start()


def wait_for(ref, sem):
    pltpu.make_async_copy(ref, ref, sem).wait()


def kernel(
    nv, nt,
    p_ref, w_ref, b_ref, q_ref, cot_ref, kv_hbm, ow_hbm,
    agg_ref, gkv_ref, gw_ref, gb_ref,
    kv, ow, pl_, pg, pd, px, wf, bt, bown, cgs, emb, val, st, wgt, stat_own, stat, wtr, xo, pixt,
    gs, g1, h1, g2, h2, g3, k3, k4, k5, gp, gt, gk, gx, perm2, wbp, wt_c, ps, p1, q1, p2, os_, or_, ctx, cr, spread,
    load_sem, pg_send, pg_recv, w_send, w_recv, b_send, b_recv, px_send, px_recv, wc_send, wc_recv,
    cg_send, cg_recv, st_send, st_recv, g1_send, g1_recv, g2_send, g2_recv, g3_send, g3_recv, k3_send, k3_recv, k5_send, k5_recv,
    gt_send, gt_recv, p1_send, p1_recv, p2_send, p2_recv, o_send, o_recv, c_send, c_recv,
):
    me = lax.axis_index("var")
    row = lax.axis_index("tok")
    nz = nv // 4
    core = lax.rem(me, 2)
    zed = lax.rem(me // 2, nz)
    far = me // (2 * nz)
    sib = me + 1 - 2 * core
    width = kv.shape[0]
    toks = nt * OWN
    cw = width // nz
    per = HEADS // nz
    grows = gp.shape[0]
    cp = width // (4 * nt)
    rpd = cp // nz
    scale = HEAD_DIM ** -0.5
    pending = []

    def tok_peer(o):
        return lax.rem(row + o, nt)

    def at(y, z, c):
        return (y * nz + z) * 2 + c

    def group_of(i):
        return lax.rem(i + (nt // 2) * (i // (2 * nz)), nt), i // nt

    def owner_of(r, a):
        return nt * a + lax.rem(r + (nt // 2) * (a // 2), nt)

    my_r, my_a = group_of(me)
    sender = my_r == row

    load_ow = pltpu.make_async_copy(ow_hbm, ow, load_sem.at[0])
    load_kv = pltpu.make_async_copy(kv_hbm, kv, load_sem.at[1])

    barrier = pltpu.get_barrier_semaphore()

    def greet(device):
        pl.semaphore_signal(barrier, inc=1, device_id=device, device_id_type=MESH)

    greet((sib, row))

    @pl.loop(1, nz)
    def _(o):
        greet((at(far, lax.rem(zed + o, nz), core), row))

    @pl.loop(0, nt)
    def _(o):
        greet((at(1 - far, zed, core), tok_peer(o)))

    @pl.loop(0, 4)
    def _(b):
        partner = owner_of(row, b)

        @pl.when(jnp.logical_not(jnp.logical_and(partner == me, sender)))
        def _():
            greet((partner, my_r))

    @pl.loop(1, nt)
    def _(o):
        greet((me, tok_peer(o)))

    @pl.loop(0, nz)
    def _(z):
        source = at(lax.rem(my_a, 2), z, my_a // 2)

        @pl.when(jnp.logical_not(jnp.logical_and(source == me, sender)))
        def _():
            greet((source, my_r))

    load_ow.start()
    load_kv.start()

    for r in range(nt):
        parts = []
        for b in range(4):
            k = nt * b + (r + (nt // 2) * (b // 2)) % nt
            parts += [p_ref[v, :, k * LANES:(k + 1) * LANES].astype(F32) for v in range(2)]
        pl_[r] = jnp.concatenate(parts, axis=0).astype(BF16)
    bias = b_ref[...].astype(F32)
    bown[...] = jnp.concatenate(
        [bias[v:v + 1, k * LANES:(k + 1) * LANES] for v in range(2) for k in range(width // LANES)], axis=0
    ).astype(BF16)

    held = core * 2 + far
    mine = owner_of(row, held)
    unsent = jnp.where(mine == me, 1, 0) + jnp.where(sender, 1, 0)
    pl.semaphore_wait(barrier, 1 + (nz - 1) + nt + 4 + (nt - 1) + nt - unsent)

    local(pl_.at[row], pg.at[row], pg_recv)

    @pl.loop(1, nt)
    def _(o):
        peer = tok_peer(o)
        remote(pl_.at[peer], pg.at[row], pg_send.at[o], pg_recv, (me, peer))

    def to_partner(b, then_remote, then_local):
        partner = owner_of(row, b)
        itself = jnp.logical_and(partner == me, sender)

        @pl.when(itself)
        def _():
            then_local()

        @pl.when(jnp.logical_not(itself))
        def _():
            then_remote(partner, lax.rem(partner, 2))

    def send_weights(b):
        def away(partner, their):
            device = (partner, my_r)
            remote(w_ref.at[their], wf.at[my_a, their], w_send.at[b], w_recv.at[my_a], device)
            remote(bown, bt.at[my_a], b_send.at[b], b_recv.at[my_a], device)

        def here():
            local(w_ref.at[core], wf.at[my_a, core], w_recv.at[my_a])
            local(bown, bt.at[my_a], b_recv.at[my_a])

        to_partner(b, away, here)

    def send_pixels(b):
        to_partner(
            b,
            lambda partner, _: remote(pd.at[b], px.at[my_a], px_send.at[b], px_recv.at[my_a], (partner, my_r)),
            lambda: local(pd.at[b], px.at[my_a], px_recv.at[my_a]),
        )

    def partner_sent(b):
        def away(partner, their):
            wait_for(w_ref.at[0], w_send.at[b])
            wait_for(bown, b_send.at[b])
            wait_for(pd.at[0], px_send.at[b])

        to_partner(b, away, lambda: None)

    def first_sent():
        @pl.loop(1, nt)
        def _(o):
            wait_for(pl_.at[0], pg_send.at[o])

        pl.loop(0, 4)(partner_sent)

    pending.append(first_sent)
    pl.loop(0, 4)(send_weights)
    load_ow.wait()
    cot = cot_ref[...].astype(F32).reshape(OWN, width).astype(BF16)
    cgs[row] = dot_nt(cot, ow[...]).astype(BF16)

    lines = 16 * nt
    o_q = iota((lines, lines), 0)
    order = ones_at(
        iota((lines, lines), 1) == ((o_q >> 2) & (nt - 1)) * 16 + (o_q >> bits(4 * nt)) * 4 + (o_q & 3)
    )
    wait_for(pg, pg_recv)
    pd[...] = dot(order, pg[...].reshape(lines, LANES)).astype(BF16).reshape(4, 4 * nt, LANES)
    pl.loop(0, 4)(send_pixels)

    @pl.loop(1, nt)
    def _(o):
        remote(cgs.at[row], cgs.at[row], cg_send.at[o], cg_recv.at[o], (me, tok_peer(o)))

    def cg_sent():
        @pl.loop(1, nt)
        def _(o):
            wait_for(cgs.at[0], cg_send.at[o])

    pending.append(cg_sent)

    lane2 = iota((2 * toks, LANES), 1)
    tok2 = iota((2 * toks, LANES), 0) & (toks - 1)
    par2 = iota((2 * toks, LANES), 0) >> bits(toks)
    sel_k = iota((2 * toks, 4 * nt), 1)
    sel_r = iota((2 * toks, 4 * nt), 0)
    sel_t = sel_r & (toks - 1)
    sel = ones_at(sel_k == (sel_t >> 4) * 4 + (sel_r >> bits(toks)) * 2 + ((sel_t >> 3) & 1))
    same_lon = (tok2 & 7) == (lane2 >> 4)
    fold = ones_at(
        ((iota((LANES, LANES), 0) & 15) == (iota((LANES, LANES), 1) & 15)) & (iota((LANES, LANES), 1) < 32)
    )
    query = q_ref[...].astype(F32).reshape(1, width)
    head_of = (iota((width, LANES), 0) >> bits(HEAD_DIM)) == iota((width, LANES), 1)
    sum_heads = ones_at(head_of)
    q_cols = jnp.broadcast_to(query, (LANES, width)).T
    q_block = jnp.where(head_of, q_cols, 0.0).astype(BF16)
    spread[...] = ones_at((iota((LANES, width), 1) >> bits(HEAD_DIM)) == iota((LANES, width), 0))
    def weights_arrived(a):
        wait_for(wf.at[a, core], w_recv.at[a])
        remote(wf.at[a, core], wf.at[a, core], wc_send.at[a], wc_recv.at[a], (sib, row))

    def wc_sent():
        @pl.loop(0, 4)
        def _(a):
            wait_for(wf.at[a, 0], wc_send.at[a])

    pending.append(wc_sent)
    load_kv.wait()
    weights_arrived(0)

    def chunk(a):
        x = dot(sel, px[a])
        x = jnp.where(same_lon, x, 0.0).astype(BF16)
        x = jnp.where((lane2 >> 4) == par2, dot(x, fold), 0.0)
        with_ones = jnp.where(lane2 == 32 + par2, 1.0, x)
        for par in range(2):
            xo[a * 2 + par] = with_ones[par * toks:(par + 1) * toks].astype(BF16)
            pixt[a * 2 + par] = with_ones[par * toks:(par + 1) * toks].T[0:48].astype(BF16)
        x = x.astype(BF16)[:, 0:32]
        biases = bt[a].astype(F32)
        w = wf[a].reshape(32, width)
        for k in range(width // LANES):
            lanes = slice(k * LANES, (k + 1) * LANES)
            e = dot(x, w[:, lanes])
            n = width // LANES
            e = e + jnp.where(par2 == 0, biases[k:k + 1], biases[n + k:n + k + 1])
            emb[:, lanes] = e.astype(BF16)
        keys = dot(emb[...], kv[:, :width]).astype(BF16)
        s = (dot(keys, q_block) * scale).T
        values = dot(emb[...], kv[:, width:]).astype(BF16)
        for par in range(2):
            mine = slice(par * toks, (par + 1) * toks)
            st[a * 2 + par] = s[0:HEADS, mine]
            val[a * 2 + par] = values[mine]

    @pl.loop(0, 4)
    def _(a):
        @pl.when(a < 3)
        def _():
            weights_arrived(a + 1)

        wait_for(px.at[a], px_recv.at[a])
        wait_for(bt.at[a], b_recv.at[a])
        wait_for(wf.at[a, 1 - core], wc_recv.at[a])
        chunk(a)

    @pl.loop(1, nt)
    def _(o):
        k = lax.rem(row - o + nt, nt)
        wait_for(cgs.at[k], cg_recv.at[o])

    cg_f = cgs[...].reshape(toks, width).astype(F32)

    @pl.loop(0, 4)
    def _(a):
        product = val[pl.ds(a * 2, 2)].astype(F32) * cg_f[None]
        high, low = split(product.reshape(2 * toks, width))
        g = (dot(high, sum_heads) + dot(low, sum_heads)).T
        for par in range(2):
            wgt[a * 2 + par] = g[0:HEADS, par * toks:(par + 1) * toks]

    s = st[...]
    wg = wgt[...]
    top = jnp.max(s, axis=0)
    e = jnp.exp(s - top[None])
    stat_own[0:16] = top
    stat_own[16:32] = jnp.sum(e, axis=0)
    stat_own[32:48] = jnp.sum(e * wg, axis=0)

    @pl.loop(1, nt)
    def _(o):
        remote(stat_own, stat.at[o], st_send.at[o], st_recv.at[o], (me, tok_peer(o)))

    def st_sent():
        @pl.loop(1, nt)
        def _(o):
            wait_for(stat_own, st_send.at[o])

    pending.append(st_sent)

    new = iota((1, width), 1)
    c_core = new >> bits(2 * nt * cp)
    c_far = (new >> bits(nt * cp)) & 1
    c_row = (new >> bits(cp)) & (nt - 1)
    c_z = (new >> bits(rpd)) & (nz - 1)
    old = ((((c_far * nz + c_z) * 2 + c_core) * nt) + c_row) * rpd + (new & (rpd - 1))
    for blk in range(width // LANES):
        lines = slice(blk * LANES, (blk + 1) * LANES)
        perm2[lines, :] = ones_at(iota((LANES, width), 0) + blk * LANES == old)
    pair = jnp.concatenate(
        [wf[held].reshape(32, width).astype(F32)]
        + [jnp.concatenate([bt[held].astype(F32)[par * 8 + k:par * 8 + k + 1] for k in range(width // LANES)], axis=1)
           for par in range(2)]
        + [jnp.zeros((LANES - TAIL, width), F32)], axis=0
    ).astype(BF16)
    wbp[...] = dot(pair, perm2[...]).astype(BF16)
    wt_c[...] = wbp[...].astype(F32).T.astype(BF16)

    stat[0] = stat_own[...]

    @pl.loop(1, nt)
    def _(o):
        wait_for(stat.at[o], st_recv.at[o])

    tops = stat[:, 0:16]
    highest = jnp.max(tops, axis=0)
    factor = jnp.exp(tops - highest[None])
    norm = jnp.sum(stat[:, 16:32] * factor, axis=0)
    mean = jnp.sum(stat[:, 32:48] * factor, axis=0) / norm
    weights_f = e * (jnp.exp(top - highest) / norm)[None]
    sg = weights_f * (wg - mean[None]) * scale
    wgt[...] = sg
    wtr[...] = weights_f.reshape(8 * HEADS, toks).T

    for a in range(4):
        g_val = jnp.zeros((48, width), F32)
        g_key = jnp.zeros((HEADS, LANES), F32)
        for v in (2 * a, 2 * a + 1):
            w = dot(wtr[:, v * HEADS:(v + 1) * HEADS].astype(BF16), spread[0:HEADS, :])
            value_grad = (w * cg_f).astype(BF16)
            g_val = g_val + dot(pixt[v], value_grad)
            high, low = split(wgt[v])
            g_key = g_key + dot(high, xo[v]) + dot(low, xo[v])
        to_core, to_far = a // 2, a % 2
        for z in range(nz):
            gs[to_core, to_far, z] = g_val[0:grows, z * cw:(z + 1) * cw]
            gs[to_core, to_far, z, TAIL:TAIL + per, 0:LANES] = g_key[z * per:(z + 1) * per, :]

    remote(gs.at[1 - core], g1, g1_send, g1_recv, (sib, row))
    pending.append(lambda: wait_for(g1, g1_send))
    wait_for(g1, g1_recv)
    h1[...] = gs[core] + g1[...]
    opposite = (at(1 - far, zed, core), row)
    remote(h1.at[1 - far, :, 0:SPLIT], g2, g2_send, g2_recv, opposite)
    pending.append(lambda: wait_for(g2, g2_send))

    @pl.loop(1, nz)
    def _(o):
        z = lax.rem(zed + o, nz)
        remote(h1.at[:, z, SPLIT:], k3.at[o], k3_send.at[o], k3_recv.at[o], (at(far, z, core), row))

    def k3_sent():
        @pl.loop(1, nz)
        def _(o):
            wait_for(k3.at[0], k3_send.at[o])

    pending.append(k3_sent)

    total = jnp.zeros((toks, width), F32)
    for v in range(8):
        w = dot(wtr[:, v * HEADS:(v + 1) * HEADS].astype(BF16), spread[0:HEADS, :])
        total = total + w * val[v].astype(F32)
    ctx[...] = total.reshape(nt, OWN, width)
    cr[row] = ctx[row]

    wait_for(g2, g2_recv)
    h2[...] = h1[far, :, 0:SPLIT] + g2[...]

    @pl.loop(1, nz)
    def _(o):
        z = lax.rem(zed + o, nz)
        remote(h2.at[z], g3.at[o], g3_send.at[o], g3_recv.at[o], (at(far, z, core), row))

    def g3_sent():
        @pl.loop(1, nz)
        def _(o):
            wait_for(h2.at[0], g3_send.at[o])

    pending.append(g3_sent)

    @pl.loop(1, nt)
    def _(o):
        peer = tok_peer(o)
        remote(ctx.at[peer], cr.at[row], c_send.at[o], c_recv.at[o], (me, peer))

    def c_sent():
        @pl.loop(1, nt)
        def _(o):
            wait_for(ctx.at[0], c_send.at[o])

    pending.append(c_sent)

    def wait_c():
        @pl.loop(1, nt)
        def _(o):
            wait_for(cr.at[lax.rem(row - o + nt, nt)], c_recv.at[o])

    g3[0] = h2[zed]
    k3[0] = h1[:, zed, SPLIT:]

    @pl.loop(1, nz)
    def _(o):
        wait_for(k3.at[o], k3_recv.at[o])

    k4[...] = jnp.sum(k3[...], axis=0)
    remote(k4.at[1 - far], k5, k5_send, k5_recv, opposite)
    pending.append(lambda: wait_for(k5, k5_send))

    @pl.loop(1, nz)
    def _(o):
        wait_for(g3.at[o], g3_recv.at[o])

    gp[0:SPLIT, :] = jnp.sum(g3[...], axis=0)
    wait_for(k5, k5_recv)
    gp[SPLIT:, :] = k4[far] + k5[...]

    def to_owner(r, then_remote, then_local):
        itself = jnp.logical_and(mine == me, r == row)

        @pl.when(itself)
        def _():
            then_local()

        @pl.when(jnp.logical_not(itself))
        def _():
            then_remote()

    lines = iota((grows, cw), 0)
    high, low = split(jnp.where(lines < TAIL, gp[...], 0.0))
    part = dot(wt_c[:, 0:grows], high) + dot(wt_c[:, 0:grows], low)
    keys_here = jnp.concatenate([gp[TAIL:TAIL + per, 0:LANES], jnp.zeros((16 - per, LANES), F32)], axis=0)
    high, low = split(keys_here)
    key_part = (dot(high, wbp[...]) + dot(low, wbp[...]))[0:8]
    for c in range(2):
        for y in range(2):
            for r in range(nt):
                k = (c * 2 + y) * nt + r
                ps[c, y, r, 0:cp, :] = part[k * cp:(k + 1) * cp]
                ps[c, y, r, cp:, :] = jnp.zeros((8, cw), F32)
                ps[c, y, r, cp:, 0:cp] = key_part[:, k * cp:(k + 1) * cp]

    remote(ps.at[1 - core], p1, p1_send, p1_recv, (sib, row))
    pending.append(lambda: wait_for(p1, p1_send))

    wait_for(p1, p1_recv)
    q1[...] = ps[core] + p1[...]

    @pl.loop(1, nt)
    def _(o):
        peer = tok_peer(o)
        remote(q1.at[far, peer], p2.at[far, row], p2_send.at[far, o], p2_recv, (me, peer))

    @pl.loop(0, nt)
    def _(o):
        peer = tok_peer(o)
        remote(
            q1.at[1 - far, peer], p2.at[far, row], p2_send.at[1 - far, o], p2_recv,
            (at(1 - far, zed, core), peer),
        )

    local(q1.at[far, row], p2.at[far, row], p2_recv)

    def p2_sent():
        @pl.loop(1, nt)
        def _(o):
            wait_for(q1.at[0, 0], p2_send.at[far, o])

        @pl.loop(0, nt)
        def _(o):
            wait_for(q1.at[0, 0], p2_send.at[1 - far, o])

    pending.append(p2_sent)

    @pl.loop(0, nt)
    def _(r):
        to_owner(
            r,
            lambda: remote(gp, gt.at[zed], gt_send.at[r], gt_recv, (mine, r)),
            lambda: local(gp, gt.at[zed], gt_recv),
        )

    def gt_sent():
        @pl.loop(0, nt)
        def _(r):
            to_owner(r, lambda: wait_for(gp, gt_send.at[r]), lambda: None)

    pending.append(gt_sent)

    wait_c()
    context = jnp.sum(cr[...], axis=0).astype(BF16)
    agg_ref[...] = dot(context, ow[...]).astype(BF16)

    wait_for(gt, gt_recv)
    gk[...] = jnp.zeros((LANES, LANES), F32)
    for z in range(nz):
        gk[z * per:(z + 1) * per, :] = gt[z, TAIL:TAIL + per, 0:LANES]
        high, low = split(gt[z])
        lanes = slice(width + z * cw, width + (z + 1) * cw)
        gx[0:grows, lanes] = high
        gx[grows:, lanes] = low
    key_high, key_low = split(gk[...].T[0:grows])
    q_rows = (spread[...].astype(F32) * query).astype(BF16)
    high, low = split(dot(key_high, q_rows) + dot(key_low, q_rows))
    gx[0:grows, :width] = high
    gx[grows:, :width] = low

    wait_for(p2, p2_recv)
    mine_c = jnp.sum(p2[...].reshape(2 * nt, cp + 8, cw), axis=0)
    key_cols = jnp.concatenate([mine_c[cp:, 0:LANES], jnp.zeros((LANES - 8, LANES), F32)], axis=0).T
    for z in range(nz):
        os_[z, 0:rpd, :] = mine_c[z * rpd:(z + 1) * rpd]
        os_[z, rpd:, 0:LANES] = key_cols[z * rpd:(z + 1) * rpd]
    local(os_.at[zed], or_.at[zed], o_recv)

    @pl.loop(1, nz)
    def _(o):
        z = lax.rem(zed + o, nz)
        remote(os_.at[z], or_.at[zed], o_send.at[o], o_recv, (at(far, z, core), row))

    def o_sent():
        @pl.loop(1, nz)
        def _(o):
            wait_for(os_.at[0], o_send.at[o])

    pending.append(o_sent)

    both = dot_nt(gx[...], kv[...])
    table = both[0:grows] + both[grows:]
    gw_ref[0] = table[0:16]
    gw_ref[1] = table[16:32]
    gb_ref[...] = table[32:34]

    wait_for(or_, o_recv)
    small = iota((rpd, cw), 1)
    for z in range(nz):
        lanes = slice(z * cw, (z + 1) * cw)
        gkv_ref[:, width + z * cw:width + (z + 1) * cw] = or_[z, 0:rpd, :]
        keyed = or_[z, rpd:, :]
        spread_key = jnp.zeros((rpd, cw), F32)
        for h in range(per):
            spread_key = jnp.where((small >> bits(HEAD_DIM)) == h, keyed[:, h:h + 1], spread_key)
        gkv_ref[:, lanes] = spread_key * query[:, lanes]

    for done in pending:
        done()


def copy_kernel(*refs):
    for k in range(4):
        refs[4 + k][...] = refs[k][...]


def shards(nv, nt, patches, embed_w, embed_b, query, kv_w, out_w, cotangent):
    width = kv_w.shape[0]
    rpd = width // (nv * nt)
    nz = nv // 4
    cw = width // nz
    grows = -(-(TAIL + HEADS // nz) // 8) * 8
    cp = width // (4 * nt)
    toks = nt * OWN
    vmem = pl.BlockSpec(memory_space=pltpu.VMEM)
    hbm = pl.BlockSpec(memory_space=pl.ANY)
    dma = pltpu.SemaphoreType.DMA
    f32 = lambda *shape: pltpu.VMEM(shape, F32)
    bf16 = lambda *shape: pltpu.VMEM(shape, BF16)
    outs = pl.pallas_call(
        functools.partial(kernel, nv, nt),
        out_shape=(
            jax.ShapeDtypeStruct((OWN, width), BF16),
            jax.ShapeDtypeStruct((rpd, 2 * width), F32),
            jax.ShapeDtypeStruct(embed_w.shape, F32),
            jax.ShapeDtypeStruct(embed_b.shape, F32),
        ),
        in_specs=[vmem] * 5 + [hbm] * 2,
        out_specs=(vmem,) * 4,
        scratch_shapes=[
            bf16(width, 2 * width),
            bf16(width, width),
            bf16(nt, 16, LANES),
            bf16(nt, 16, LANES),
            bf16(4, 4 * nt, LANES),
            bf16(4, 4 * nt, LANES),
            bf16(4, 2, PIX, width),
            bf16(4, 16, LANES),
            bf16(16, LANES),
            bf16(nt, OWN, width),
            bf16(2 * toks, width),
            bf16(8, toks, width),
            f32(8, HEADS, toks),
            f32(8, HEADS, toks),
            f32(48, toks),
            f32(nt, 48, toks),
            f32(toks, LANES),
            bf16(8, toks, LANES),
            bf16(8, 48, toks),
            f32(2, 2, nz, grows, cw),
            f32(2, nz, grows, cw),
            f32(2, nz, grows, cw),
            f32(nz, SPLIT, cw),
            f32(nz, SPLIT, cw),
            f32(nz, SPLIT, cw),
            f32(nz, 2, grows - SPLIT, cw),
            f32(2, grows - SPLIT, cw),
            f32(grows - SPLIT, cw),
            f32(grows, cw),
            f32(nz, grows, cw),
            f32(LANES, LANES),
            bf16(2 * grows, 2 * width),
            bf16(width, width),
            bf16(LANES, width),
            bf16(width, LANES),
            f32(2, 2, nt, cp + 8, cw),
            f32(2, nt, cp + 8, cw),
            f32(2, nt, cp + 8, cw),
            f32(2, nt, cp + 8, cw),
            f32(nz, 2 * rpd, cw),
            f32(nz, 2 * rpd, cw),
            f32(nt, OWN, width),
            f32(nt, OWN, width),
            bf16(LANES, width),
            dma((2,)), dma((nt,)), dma, dma((4,)), dma((4,)), dma((4,)), dma((4,)), dma((4,)), dma((4,)), dma((4,)), dma((4,)),
            dma((nt,)), dma((nt,)), dma((nt,)), dma((nt,)), dma, dma, dma, dma, dma((nz,)), dma((nz,)), dma((nz,)), dma((nz,)), dma, dma,
            dma((nt,)), dma, dma, dma, dma((2, nt)), dma, dma((nz,)), dma, dma((nt,)), dma((nt,)),
        ],
        compiler_params=pltpu.CompilerParams(
            collective_id=0, has_side_effects=True, vmem_limit_bytes=56 * 1024 * 1024
        ),
        cost_estimate=pl.CostEstimate(flops=5_000_000_000, bytes_accessed=8_000_000, transcendentals=20_000),
    )(patches, embed_w, embed_b, query, cotangent, kv_w, out_w)
    aggregated, grad_kv, grad_w, grad_b = pl.pallas_call(
        copy_kernel,
        out_shape=[jax.ShapeDtypeStruct(x.shape, x.dtype) for x in outs],
        in_specs=[vmem] * 4,
        out_specs=[vmem] * 4,
    )(*outs)
    return aggregated.reshape(cotangent.shape), grad_kv, grad_w, grad_b


def solution(mesh):
    return jax.shard_map(
        functools.partial(shards, mesh.shape["var"], mesh.shape["tok"]),
        mesh=mesh,
        in_specs=(
            P("var", "tok", None),
            P("var", None, None),
            P("var", None),
            P(),
            P(),
            P(),
            P("tok", "var", None),
        ),
        out_specs=(
            P("tok", "var", None),
            P(("var", "tok"), None),
            P("var", None, None),
            P("var", None),
        ),
        check_vma=False,
    )
```

```python
import functools

import jax
import jax.numpy as jnp
from jax import lax
from jax.experimental import pallas as pl
from jax.experimental.pallas import tpu as pltpu
from jax.sharding import PartitionSpec as P

MESH = pl.DeviceIdType.MESH
F32 = jnp.float32
BF16 = jnp.bfloat16
LANES = 128
PIX = 16
OWN = 16
HEADS = 16
HEAD_DIM = 64
SPLIT = 24
TAIL = 34


def dot(a, b):
    return jnp.dot(a, b, preferred_element_type=F32)


def dot_nt(a, b):
    return lax.dot_general(a, b, (((1,), (1,)), ((), ())), preferred_element_type=F32)


def iota(shape, dim):
    return lax.broadcasted_iota(jnp.int32, shape, dim)


def ones_at(cond):
    return jnp.where(cond, 1.0, 0.0).astype(BF16)


def split(x):
    high = x.astype(BF16)
    return high, (x - high.astype(F32)).astype(BF16)


def bits(n):
    return n.bit_length() - 1


def remote(src, dst, send_sem, recv_sem, device):
    pltpu.make_async_remote_copy(
        src, dst, send_sem, recv_sem, device_id=device, device_id_type=MESH
    ).start()


def local(src, dst, sem):
    pltpu.make_async_copy(src, dst, sem).start()


def wait_for(ref, sem):
    pltpu.make_async_copy(ref, ref, sem).wait()


def kernel(
    nv, nt,
    p_hbm, w_hbm, b_hbm, q_hbm, cot_hbm, kv_hbm, ow_hbm,
    agg_ref, gkv_ref, gw_ref, gb_ref,
    p_ref, w_ref, b_ref, q_ref, cot_ref, kv, ow, pl_, pg, pd, px, wf, bt, bown, cgs, emb, val, st, wgt, stat_own, stat, wtr, xo, pixt,
    gs, g1, h1, g2, h2, g3, k3, k4, k5, gp, gt, gk, gx, perm2, wbp, wt_c, ps, p1, q1, p2, os_, or_, ctx, cr, spread,
    load_sem, pg_send, pg_recv, w_send, w_recv, b_send, b_recv, px_send, px_recv, wc_send, wc_recv,
    cg_send, cg_recv, st_send, st_recv, g1_send, g1_recv, g2_send, g2_recv, g3_send, g3_recv, k3_send, k3_recv, k5_send, k5_recv,
    gt_send, gt_recv, p1_send, p1_recv, p2_send, p2_recv, o_send, o_recv, c_send, c_recv,
):
    me = lax.axis_index("var")
    row = lax.axis_index("tok")
    nz = nv // 4
    core = lax.rem(me, 2)
    zed = lax.rem(me // 2, nz)
    far = me // (2 * nz)
    sib = me + 1 - 2 * core
    width = kv.shape[0]
    toks = nt * OWN
    cw = width // nz
    per = HEADS // nz
    grows = gp.shape[0]
    cp = width // (4 * nt)
    rpd = cp // nz
    scale = HEAD_DIM ** -0.5
    pending = []

    def tok_peer(o):
        return lax.rem(row + o, nt)

    def at(y, z, c):
        return (y * nz + z) * 2 + c

    def group_of(i):
        return lax.rem(i + (nt // 2) * (i // (2 * nz)), nt), i // nt

    def owner_of(r, a):
        return nt * a + lax.rem(r + (nt // 2) * (a // 2), nt)

    my_r, my_a = group_of(me)
    sender = my_r == row

    load_ow = pltpu.make_async_copy(ow_hbm, ow, load_sem.at[0])
    load_kv = pltpu.make_async_copy(kv_hbm, kv, load_sem.at[1])

    barrier = pltpu.get_barrier_semaphore()

    def greet(device):
        pl.semaphore_signal(barrier, inc=1, device_id=device, device_id_type=MESH)

    greet((sib, row))

    @pl.loop(1, nz)
    def _(o):
        greet((at(far, lax.rem(zed + o, nz), core), row))

    @pl.loop(0, nt)
    def _(o):
        greet((at(1 - far, zed, core), tok_peer(o)))

    @pl.loop(0, 4)
    def _(b):
        partner = owner_of(row, b)

        @pl.when(jnp.logical_not(jnp.logical_and(partner == me, sender)))
        def _():
            greet((partner, my_r))

    @pl.loop(1, nt)
    def _(o):
        greet((me, tok_peer(o)))

    @pl.loop(0, nz)
    def _(z):
        source = at(lax.rem(my_a, 2), z, my_a // 2)

        @pl.when(jnp.logical_not(jnp.logical_and(source == me, sender)))
        def _():
            greet((source, my_r))

    small_loads = [
        pltpu.make_async_copy(source, ref, load_sem.at[2 + k])
        for k, (source, ref) in enumerate(
            ((p_hbm, p_ref), (b_hbm, b_ref), (w_hbm, w_ref), (cot_hbm, cot_ref), (q_hbm, q_ref))
        )
    ]
    for load in small_loads:
        load.start()
    load_ow.start()
    load_kv.start()

    for load in small_loads:
        load.wait()
    for r in range(nt):
        parts = []
        for b in range(4):
            k = nt * b + (r + (nt // 2) * (b // 2)) % nt
            parts += [p_ref[v, :, k * LANES:(k + 1) * LANES].astype(F32) for v in range(2)]
        pl_[r] = jnp.concatenate(parts, axis=0).astype(BF16)
    bias = b_ref[...].astype(F32)
    bown[...] = jnp.concatenate(
        [bias[v:v + 1, k * LANES:(k + 1) * LANES] for v in range(2) for k in range(width // LANES)], axis=0
    ).astype(BF16)

    held = core * 2 + far
    mine = owner_of(row, held)
    unsent = jnp.where(mine == me, 1, 0) + jnp.where(sender, 1, 0)
    pl.semaphore_wait(barrier, 1 + (nz - 1) + nt + 4 + (nt - 1) + nt - unsent)

    local(pl_.at[row], pg.at[row], pg_recv)

    @pl.loop(1, nt)
    def _(o):
        peer = tok_peer(o)
        remote(pl_.at[peer], pg.at[row], pg_send.at[o], pg_recv, (me, peer))

    def to_partner(b, then_remote, then_local):
        partner = owner_of(row, b)
        itself = jnp.logical_and(partner == me, sender)

        @pl.when(itself)
        def _():
            then_local()

        @pl.when(jnp.logical_not(itself))
        def _():
            then_remote(partner, lax.rem(partner, 2))

    def send_weights(b):
        def away(partner, their):
            device = (partner, my_r)
            remote(w_ref.at[their], wf.at[my_a, their], w_send.at[b], w_recv.at[my_a], device)
            remote(bown, bt.at[my_a], b_send.at[b], b_recv.at[my_a], device)

        def here():
            local(w_ref.at[core], wf.at[my_a, core], w_recv.at[my_a])
            local(bown, bt.at[my_a], b_recv.at[my_a])

        to_partner(b, away, here)

    def send_pixels(b):
        to_partner(
            b,
            lambda partner, _: remote(pd.at[b], px.at[my_a], px_send.at[b], px_recv.at[my_a], (partner, my_r)),
            lambda: local(pd.at[b], px.at[my_a], px_recv.at[my_a]),
        )

    def partner_sent(b):
        def away(partner, their):
            wait_for(w_ref.at[0], w_send.at[b])
            wait_for(bown, b_send.at[b])
            wait_for(pd.at[0], px_send.at[b])

        to_partner(b, away, lambda: None)

    def first_sent():
        @pl.loop(1, nt)
        def _(o):
            wait_for(pl_.at[0], pg_send.at[o])

        pl.loop(0, 4)(partner_sent)

    pending.append(first_sent)
    pl.loop(0, 4)(send_weights)
    load_ow.wait()
    cot = cot_ref[...].astype(F32).reshape(OWN, width).astype(BF16)
    cgs[row] = dot_nt(cot, ow[...]).astype(BF16)

    lines = 16 * nt
    o_q = iota((lines, lines), 0)
    order = ones_at(
        iota((lines, lines), 1) == ((o_q >> 2) & (nt - 1)) * 16 + (o_q >> bits(4 * nt)) * 4 + (o_q & 3)
    )
    wait_for(pg, pg_recv)
    pd[...] = dot(order, pg[...].reshape(lines, LANES)).astype(BF16).reshape(4, 4 * nt, LANES)
    pl.loop(0, 4)(send_pixels)

    @pl.loop(1, nt)
    def _(o):
        remote(cgs.at[row], cgs.at[row], cg_send.at[o], cg_recv.at[o], (me, tok_peer(o)))

    def cg_sent():
        @pl.loop(1, nt)
        def _(o):
            wait_for(cgs.at[0], cg_send.at[o])

    pending.append(cg_sent)

    lane2 = iota((2 * toks, LANES), 1)
    tok2 = iota((2 * toks, LANES), 0) & (toks - 1)
    par2 = iota((2 * toks, LANES), 0) >> bits(toks)
    sel_k = iota((2 * toks, 4 * nt), 1)
    sel_r = iota((2 * toks, 4 * nt), 0)
    sel_t = sel_r & (toks - 1)
    sel = ones_at(sel_k == (sel_t >> 4) * 4 + (sel_r >> bits(toks)) * 2 + ((sel_t >> 3) & 1))
    same_lon = (tok2 & 7) == (lane2 >> 4)
    fold = ones_at(
        ((iota((LANES, LANES), 0) & 15) == (iota((LANES, LANES), 1) & 15)) & (iota((LANES, LANES), 1) < 32)
    )
    query = q_ref[...].astype(F32).reshape(1, width)
    head_of = (iota((width, LANES), 0) >> bits(HEAD_DIM)) == iota((width, LANES), 1)
    sum_heads = ones_at(head_of)
    q_cols = jnp.broadcast_to(query, (LANES, width)).T
    q_block = jnp.where(head_of, q_cols, 0.0).astype(BF16)
    spread[...] = ones_at((iota((LANES, width), 1) >> bits(HEAD_DIM)) == iota((LANES, width), 0))
    def weights_arrived(a):
        wait_for(wf.at[a, core], w_recv.at[a])
        remote(wf.at[a, core], wf.at[a, core], wc_send.at[a], wc_recv.at[a], (sib, row))

    def wc_sent():
        @pl.loop(0, 4)
        def _(a):
            wait_for(wf.at[a, 0], wc_send.at[a])

    pending.append(wc_sent)
    load_kv.wait()
    weights_arrived(0)

    def chunk(a):
        x = dot(sel, px[a])
        x = jnp.where(same_lon, x, 0.0).astype(BF16)
        x = jnp.where((lane2 >> 4) == par2, dot(x, fold), 0.0)
        with_ones = jnp.where(lane2 == 32 + par2, 1.0, x)
        for par in range(2):
            xo[a * 2 + par] = with_ones[par * toks:(par + 1) * toks].astype(BF16)
            pixt[a * 2 + par] = with_ones[par * toks:(par + 1) * toks].T[0:48].astype(BF16)
        x = x.astype(BF16)[:, 0:32]
        biases = bt[a].astype(F32)
        w = wf[a].reshape(32, width)
        for k in range(width // LANES):
            lanes = slice(k * LANES, (k + 1) * LANES)
            e = dot(x, w[:, lanes])
            n = width // LANES
            e = e + jnp.where(par2 == 0, biases[k:k + 1], biases[n + k:n + k + 1])
            emb[:, lanes] = e.astype(BF16)
        keys = dot(emb[...], kv[:, :width]).astype(BF16)
        s = (dot(keys, q_block) * scale).T
        values = dot(emb[...], kv[:, width:]).astype(BF16)
        for par in range(2):
            mine = slice(par * toks, (par + 1) * toks)
            st[a * 2 + par] = s[0:HEADS, mine]
            val[a * 2 + par] = values[mine]

    @pl.loop(0, 4)
    def _(a):
        @pl.when(a < 3)
        def _():
            weights_arrived(a + 1)

        wait_for(px.at[a], px_recv.at[a])
        wait_for(bt.at[a], b_recv.at[a])
        wait_for(wf.at[a, 1 - core], wc_recv.at[a])
        chunk(a)

    @pl.loop(1, nt)
    def _(o):
        k = lax.rem(row - o + nt, nt)
        wait_for(cgs.at[k], cg_recv.at[o])

    cg_f = cgs[...].reshape(toks, width).astype(F32)

    @pl.loop(0, 4)
    def _(a):
        product = val[pl.ds(a * 2, 2)].astype(F32) * cg_f[None]
        high, low = split(product.reshape(2 * toks, width))
        g = (dot(high, sum_heads) + dot(low, sum_heads)).T
        for par in range(2):
            wgt[a * 2 + par] = g[0:HEADS, par * toks:(par + 1) * toks]

    s = st[...]
    wg = wgt[...]
    top = jnp.max(s, axis=0)
    e = jnp.exp(s - top[None])
    stat_own[0:16] = top
    stat_own[16:32] = jnp.sum(e, axis=0)
    stat_own[32:48] = jnp.sum(e * wg, axis=0)

    @pl.loop(1, nt)
    def _(o):
        remote(stat_own, stat.at[o], st_send.at[o], st_recv.at[o], (me, tok_peer(o)))

    def st_sent():
        @pl.loop(1, nt)
        def _(o):
            wait_for(stat_own, st_send.at[o])

    pending.append(st_sent)

    new = iota((1, width), 1)
    c_core = new >> bits(2 * nt * cp)
    c_far = (new >> bits(nt * cp)) & 1
    c_row = (new >> bits(cp)) & (nt - 1)
    c_z = (new >> bits(rpd)) & (nz - 1)
    old = ((((c_far * nz + c_z) * 2 + c_core) * nt) + c_row) * rpd + (new & (rpd - 1))
    for blk in range(width // LANES):
        lines = slice(blk * LANES, (blk + 1) * LANES)
        perm2[lines, :] = ones_at(iota((LANES, width), 0) + blk * LANES == old)
    pair = jnp.concatenate(
        [wf[held].reshape(32, width).astype(F32)]
        + [jnp.concatenate([bt[held].astype(F32)[par * 8 + k:par * 8 + k + 1] for k in range(width // LANES)], axis=1)
           for par in range(2)]
        + [jnp.zeros((LANES - TAIL, width), F32)], axis=0
    ).astype(BF16)
    wbp[...] = dot(pair, perm2[...]).astype(BF16)
    wt_c[...] = wbp[...].astype(F32).T.astype(BF16)

    stat[0] = stat_own[...]

    @pl.loop(1, nt)
    def _(o):
        wait_for(stat.at[o], st_recv.at[o])

    tops = stat[:, 0:16]
    highest = jnp.max(tops, axis=0)
    factor = jnp.exp(tops - highest[None])
    norm = jnp.sum(stat[:, 16:32] * factor, axis=0)
    mean = jnp.sum(stat[:, 32:48] * factor, axis=0) / norm
    weights_f = e * (jnp.exp(top - highest) / norm)[None]
    sg = weights_f * (wg - mean[None]) * scale
    wgt[...] = sg
    turned = weights_f.reshape(8 * HEADS, toks).T
    for v in range(8):
        wtr[v] = turned[:, v * HEADS:(v + 1) * HEADS].astype(BF16)

    for t in range(4):
        a = lax.rem((1 - core) * 2 + t, 4)
        g_val = jnp.zeros((48, width), F32)
        g_key = jnp.zeros((HEADS, LANES), F32)
        for v in (2 * a, 2 * a + 1):
            w = dot(wtr[v], spread[0:HEADS, :])
            value_grad = (w * cg_f).astype(BF16)
            g_val = g_val + dot(pixt[v], value_grad)
            high, low = split(wgt[v])
            g_key = g_key + dot(high, xo[v]) + dot(low, xo[v])
        to_core, to_far = a // 2, lax.rem(a, 2)
        for z in range(nz):
            gs[to_core, to_far, z] = g_val[0:grows, z * cw:(z + 1) * cw]
            gs[to_core, to_far, z, TAIL:TAIL + per, 0:LANES] = g_key[z * per:(z + 1) * per, :]

        if t == 1:
            remote(gs.at[1 - core], g1, g1_send, g1_recv, (sib, row))

    pending.append(lambda: wait_for(g1, g1_send))
    wait_for(g1, g1_recv)
    h1[...] = gs[core] + g1[...]
    opposite = (at(1 - far, zed, core), row)
    remote(h1.at[1 - far, :, 0:SPLIT], g2, g2_send, g2_recv, opposite)
    pending.append(lambda: wait_for(g2, g2_send))

    @pl.loop(1, nz)
    def _(o):
        z = lax.rem(zed + o, nz)
        remote(h1.at[:, z, SPLIT:], k3.at[o], k3_send.at[o], k3_recv.at[o], (at(far, z, core), row))

    def k3_sent():
        @pl.loop(1, nz)
        def _(o):
            wait_for(k3.at[0], k3_send.at[o])

    pending.append(k3_sent)

    total = jnp.zeros((toks, width), F32)
    for v in range(8):
        w = dot(wtr[v], spread[0:HEADS, :])
        total = total + w * val[v].astype(F32)
    ctx[...] = total.reshape(nt, OWN, width)
    cr[row] = ctx[row]

    wait_for(g2, g2_recv)
    h2[...] = h1[far, :, 0:SPLIT] + g2[...]

    @pl.loop(1, nz)
    def _(o):
        z = lax.rem(zed + o, nz)
        remote(h2.at[z], g3.at[o], g3_send.at[o], g3_recv.at[o], (at(far, z, core), row))

    def g3_sent():
        @pl.loop(1, nz)
        def _(o):
            wait_for(h2.at[0], g3_send.at[o])

    pending.append(g3_sent)

    @pl.loop(1, nt)
    def _(o):
        peer = tok_peer(o)
        remote(ctx.at[peer], cr.at[row], c_send.at[o], c_recv.at[o], (me, peer))

    def c_sent():
        @pl.loop(1, nt)
        def _(o):
            wait_for(ctx.at[0], c_send.at[o])

    pending.append(c_sent)

    def wait_c():
        @pl.loop(1, nt)
        def _(o):
            wait_for(cr.at[lax.rem(row - o + nt, nt)], c_recv.at[o])

    g3[0] = h2[zed]
    k3[0] = h1[:, zed, SPLIT:]

    @pl.loop(1, nz)
    def _(o):
        wait_for(k3.at[o], k3_recv.at[o])

    k4[...] = jnp.sum(k3[...], axis=0)
    remote(k4.at[1 - far], k5, k5_send, k5_recv, opposite)
    pending.append(lambda: wait_for(k5, k5_send))

    @pl.loop(1, nz)
    def _(o):
        wait_for(g3.at[o], g3_recv.at[o])

    gp[0:SPLIT, :] = jnp.sum(g3[...], axis=0)
    wait_for(k5, k5_recv)
    gp[SPLIT:, :] = k4[far] + k5[...]

    def to_owner(r, then_remote, then_local):
        itself = jnp.logical_and(mine == me, r == row)

        @pl.when(itself)
        def _():
            then_local()

        @pl.when(jnp.logical_not(itself))
        def _():
            then_remote()

    @pl.loop(0, nt)
    def _(r):
        to_owner(
            r,
            lambda: remote(gp, gt.at[zed], gt_send.at[r], gt_recv, (mine, r)),
            lambda: local(gp, gt.at[zed], gt_recv),
        )

    def gt_sent():
        @pl.loop(0, nt)
        def _(r):
            to_owner(r, lambda: wait_for(gp, gt_send.at[r]), lambda: None)

    pending.append(gt_sent)

    lines = iota((grows, cw), 0)
    high, low = split(jnp.where(lines < TAIL, gp[...], 0.0))
    keys_here = jnp.concatenate([gp[TAIL:TAIL + per, 0:LANES], jnp.zeros((16 - per, LANES), F32)], axis=0)
    key_high, key_low = split(keys_here)
    half = width // 2

    def products(c):
        lines_c = pl.ds(pl.multiple_of(c * half, half), half)
        left = wt_c[lines_c, 0:grows]
        part = dot(left, high) + dot(left, low)
        right = wbp[:, lines_c]
        key_part = (dot(key_high, right) + dot(key_low, right))[0:8]
        for y in range(2):
            for r in range(nt):
                k = y * nt + r
                ps[c, y, r, 0:cp, :] = part[k * cp:(k + 1) * cp]
                ps[c, y, r, cp:, :] = jnp.zeros((8, cw), F32)
                ps[c, y, r, cp:, 0:cp] = key_part[:, k * cp:(k + 1) * cp]

    products(1 - core)
    remote(ps.at[1 - core], p1, p1_send, p1_recv, (sib, row))
    pending.append(lambda: wait_for(p1, p1_send))
    products(core)
    wait_for(p1, p1_recv)
    q1[...] = ps[core] + p1[...]

    @pl.loop(1, nt)
    def _(o):
        peer = tok_peer(o)
        remote(q1.at[far, peer], p2.at[far, row], p2_send.at[far, o], p2_recv, (me, peer))

    @pl.loop(0, nt)
    def _(o):
        peer = tok_peer(o)
        remote(
            q1.at[1 - far, peer], p2.at[far, row], p2_send.at[1 - far, o], p2_recv,
            (at(1 - far, zed, core), peer),
        )

    local(q1.at[far, row], p2.at[far, row], p2_recv)

    def p2_sent():
        @pl.loop(1, nt)
        def _(o):
            wait_for(q1.at[0, 0], p2_send.at[far, o])

        @pl.loop(0, nt)
        def _(o):
            wait_for(q1.at[0, 0], p2_send.at[1 - far, o])

    pending.append(p2_sent)

    wait_c()
    context = jnp.sum(cr[...], axis=0).astype(BF16)
    agg_ref[...] = dot(context, ow[...]).astype(BF16)

    wait_for(p2, p2_recv)
    mine_c = jnp.sum(p2[...].reshape(2 * nt, cp + 8, cw), axis=0)
    key_cols = jnp.concatenate([mine_c[cp:, 0:LANES], jnp.zeros((LANES - 8, LANES), F32)], axis=0).T
    for z in range(nz):
        os_[z, 0:rpd, :] = mine_c[z * rpd:(z + 1) * rpd]
        os_[z, rpd:, 0:LANES] = key_cols[z * rpd:(z + 1) * rpd]
    local(os_.at[zed], or_.at[zed], o_recv)

    @pl.loop(1, nz)
    def _(o):
        z = lax.rem(zed + o, nz)
        remote(os_.at[z], or_.at[zed], o_send.at[o], o_recv, (at(far, z, core), row))

    def o_sent():
        @pl.loop(1, nz)
        def _(o):
            wait_for(os_.at[0], o_send.at[o])

    pending.append(o_sent)

    wait_for(gt, gt_recv)
    gk[...] = jnp.zeros((LANES, LANES), F32)
    for z in range(nz):
        gk[z * per:(z + 1) * per, :] = gt[z, TAIL:TAIL + per, 0:LANES]
        high, low = split(gt[z])
        lanes = slice(width + z * cw, width + (z + 1) * cw)
        gx[0:grows, lanes] = high
        gx[grows:, lanes] = low
    key_high, key_low = split(gk[...].T[0:grows])
    q_rows = (spread[...].astype(F32) * query).astype(BF16)
    high, low = split(dot(key_high, q_rows) + dot(key_low, q_rows))
    gx[0:grows, :width] = high
    gx[grows:, :width] = low

    both = dot_nt(gx[...], kv[...])
    table = both[0:grows] + both[grows:]
    gw_ref[0] = table[0:16]
    gw_ref[1] = table[16:32]
    gb_ref[...] = table[32:34]

    wait_for(or_, o_recv)
    small = iota((rpd, cw), 1)
    for z in range(nz):
        lanes = slice(z * cw, (z + 1) * cw)
        gkv_ref[:, width + z * cw:width + (z + 1) * cw] = or_[z, 0:rpd, :]
        keyed = or_[z, rpd:, :]
        spread_key = jnp.zeros((rpd, cw), F32)
        for h in range(per):
            spread_key = jnp.where((small >> bits(HEAD_DIM)) == h, keyed[:, h:h + 1], spread_key)
        gkv_ref[:, lanes] = spread_key * query[:, lanes]

    for done in pending:
        done()


def copy_kernel(*refs):
    for k in range(4):
        refs[4 + k][...] = refs[k][...]


def shards(nv, nt, patches, embed_w, embed_b, query, kv_w, out_w, cotangent):
    width = kv_w.shape[0]
    rpd = width // (nv * nt)
    nz = nv // 4
    cw = width // nz
    grows = -(-(TAIL + HEADS // nz) // 8) * 8
    cp = width // (4 * nt)
    toks = nt * OWN
    vmem = pl.BlockSpec(memory_space=pltpu.VMEM)
    hbm = pl.BlockSpec(memory_space=pl.ANY)
    dma = pltpu.SemaphoreType.DMA
    f32 = lambda *shape: pltpu.VMEM(shape, F32)
    bf16 = lambda *shape: pltpu.VMEM(shape, BF16)
    outs = pl.pallas_call(
        functools.partial(kernel, nv, nt),
        out_shape=(
            jax.ShapeDtypeStruct((OWN, width), BF16),
            jax.ShapeDtypeStruct((rpd, 2 * width), F32),
            jax.ShapeDtypeStruct(embed_w.shape, F32),
            jax.ShapeDtypeStruct(embed_b.shape, F32),
        ),
        in_specs=[hbm] * 7,
        out_specs=(vmem,) * 4,
        scratch_shapes=[
            pltpu.VMEM(patches.shape, BF16),
            pltpu.VMEM(embed_w.shape, BF16),
            pltpu.VMEM(embed_b.shape, BF16),
            pltpu.VMEM(query.shape, BF16),
            pltpu.VMEM(cotangent.shape, BF16),
            bf16(width, 2 * width),
            bf16(width, width),
            bf16(nt, 16, LANES),
            bf16(nt, 16, LANES),
            bf16(4, 4 * nt, LANES),
            bf16(4, 4 * nt, LANES),
            bf16(4, 2, PIX, width),
            bf16(4, 16, LANES),
            bf16(16, LANES),
            bf16(nt, OWN, width),
            bf16(2 * toks, width),
            bf16(8, toks, width),
            f32(8, HEADS, toks),
            f32(8, HEADS, toks),
            f32(48, toks),
            f32(nt, 48, toks),
            bf16(8, toks, HEADS),
            bf16(8, toks, LANES),
            bf16(8, 48, toks),
            f32(2, 2, nz, grows, cw),
            f32(2, nz, grows, cw),
            f32(2, nz, grows, cw),
            f32(nz, SPLIT, cw),
            f32(nz, SPLIT, cw),
            f32(nz, SPLIT, cw),
            f32(nz, 2, grows - SPLIT, cw),
            f32(2, grows - SPLIT, cw),
            f32(grows - SPLIT, cw),
            f32(grows, cw),
            f32(nz, grows, cw),
            f32(LANES, LANES),
            bf16(2 * grows, 2 * width),
            bf16(width, width),
            bf16(LANES, width),
            bf16(width, LANES),
            f32(2, 2, nt, cp + 8, cw),
            f32(2, nt, cp + 8, cw),
            f32(2, nt, cp + 8, cw),
            f32(2, nt, cp + 8, cw),
            f32(nz, 2 * rpd, cw),
            f32(nz, 2 * rpd, cw),
            f32(nt, OWN, width),
            f32(nt, OWN, width),
            bf16(LANES, width),
            dma((7,)), dma((nt,)), dma, dma((4,)), dma((4,)), dma((4,)), dma((4,)), dma((4,)), dma((4,)), dma((4,)), dma((4,)),
            dma((nt,)), dma((nt,)), dma((nt,)), dma((nt,)), dma, dma, dma, dma, dma((nz,)), dma((nz,)), dma((nz,)), dma((nz,)), dma, dma,
            dma((nt,)), dma, dma, dma, dma((2, nt)), dma, dma((nz,)), dma, dma((nt,)), dma((nt,)),
        ],
        compiler_params=pltpu.CompilerParams(
            collective_id=0, has_side_effects=True, vmem_limit_bytes=56 * 1024 * 1024
        ),
        cost_estimate=pl.CostEstimate(flops=5_000_000_000, bytes_accessed=8_000_000, transcendentals=20_000),
    )(patches, embed_w, embed_b, query, cotangent, kv_w, out_w)
    aggregated, grad_kv, grad_w, grad_b = pl.pallas_call(
        copy_kernel,
        out_shape=[jax.ShapeDtypeStruct(x.shape, x.dtype) for x in outs],
        in_specs=[vmem] * 4,
        out_specs=[vmem] * 4,
    )(*outs)
    return aggregated.reshape(cotangent.shape), grad_kv, grad_w, grad_b


def solution(mesh):
    return jax.shard_map(
        functools.partial(shards, mesh.shape["var"], mesh.shape["tok"]),
        mesh=mesh,
        in_specs=(
            P("var", "tok", None),
            P("var", None, None),
            P("var", None),
            P(),
            P(),
            P(),
            P("tok", "var", None),
        ),
        out_specs=(
            P("tok", "var", None),
            P(("var", "tok"), None),
            P("var", None, None),
            P("var", None),
        ),
        check_vma=False,
    )
```

```python
import functools

import jax
import jax.numpy as jnp
from jax import lax
from jax.experimental import pallas as pl
from jax.experimental.pallas import tpu as pltpu
from jax.sharding import PartitionSpec as P

MESH = pl.DeviceIdType.MESH
F32 = jnp.float32
BF16 = jnp.bfloat16
LANES = 128
PIX = 16
OWN = 16
HEADS = 16
HEAD_DIM = 64
SPLIT = 24
TAIL = 34


def dot(a, b):
    return jnp.dot(a, b, preferred_element_type=F32)


def dot_nt(a, b):
    return lax.dot_general(a, b, (((1,), (1,)), ((), ())), preferred_element_type=F32)


def iota(shape, dim):
    return lax.broadcasted_iota(jnp.int32, shape, dim)


def ones_at(cond):
    return jnp.where(cond, 1.0, 0.0).astype(BF16)


def split(x):
    high = x.astype(BF16)
    return high, (x - high.astype(F32)).astype(BF16)


def bits(n):
    return n.bit_length() - 1


def remote(src, dst, send_sem, recv_sem, device):
    pltpu.make_async_remote_copy(
        src, dst, send_sem, recv_sem, device_id=device, device_id_type=MESH
    ).start()


def local(src, dst, sem):
    pltpu.make_async_copy(src, dst, sem).start()


def wait_for(ref, sem):
    pltpu.make_async_copy(ref, ref, sem).wait()


def kernel(
    nv, nt,
    p_hbm, w_hbm, b_hbm, q_hbm, cot_hbm, kv_hbm, ow_hbm,
    agg_ref, gkv_ref, gw_ref, gb_ref,
    p_ref, w_ref, b_ref, q_ref, cot_ref, kv, ow, pl_, pg, pd, px, wf, bt, bown, cgs, emb, val, st, wgt, stat_own, stat, wtr, xo, pixt,
    gs, g1, h1, g2, h2, g3, k3, k4, k5, gp, gt, gk, gx, perm2, wbp, wt_c, ps, p1, q1, p2, os_, or_, ctx, cr, spread,
    load_sem, pg_send, pg_recv, w_send, w_recv, b_send, b_recv, px_send, px_recv, wc_send, wc_recv,
    cg_send, cg_recv, st_send, st_recv, g1_send, g1_recv, g2_send, g2_recv, g3_send, g3_recv, k3_send, k3_recv, k5_send, k5_recv,
    gt_send, gt_recv, p1_send, p1_recv, p2_send, p2_recv, o_send, o_recv, c_send, c_recv,
):
    me = lax.axis_index("var")
    row = lax.axis_index("tok")
    nz = nv // 4
    core = lax.rem(me, 2)
    zed = lax.rem(me // 2, nz)
    far = me // (2 * nz)
    sib = me + 1 - 2 * core
    width = kv.shape[0]
    toks = nt * OWN
    cw = width // nz
    per = HEADS // nz
    grows = gp.shape[0]
    cp = width // (4 * nt)
    rpd = cp // nz
    scale = HEAD_DIM ** -0.5
    pending = []

    def tok_peer(o):
        return lax.rem(row + o, nt)

    def at(y, z, c):
        return (y * nz + z) * 2 + c

    def group_of(i):
        return lax.rem(i + (nt // 2) * (i // (2 * nz)), nt), i // nt

    def owner_of(r, a):
        return nt * a + lax.rem(r + (nt // 2) * (a // 2), nt)

    my_r, my_a = group_of(me)
    sender = my_r == row

    load_ow = pltpu.make_async_copy(ow_hbm, ow, load_sem.at[0])
    load_kv = pltpu.make_async_copy(kv_hbm, kv, load_sem.at[1])

    barrier = pltpu.get_barrier_semaphore()

    def greet(device):
        pl.semaphore_signal(barrier, inc=1, device_id=device, device_id_type=MESH)

    @pl.loop(0, 4)
    def _(b):
        partner = owner_of(row, b)

        @pl.when(jnp.logical_not(jnp.logical_and(partner == me, sender)))
        def _():
            greet((partner, my_r))

    @pl.loop(1, nz)
    def _(o):
        greet((at(far, lax.rem(zed + o, nz), core), row))

    @pl.loop(0, nz)
    def _(z):
        source = at(lax.rem(my_a, 2), z, my_a // 2)

        @pl.when(jnp.logical_not(jnp.logical_and(source == me, sender)))
        def _():
            greet((source, my_r))

    @pl.loop(0, nt)
    def _(o):
        greet((at(1 - far, zed, core), tok_peer(o)))

    @pl.loop(1, nt)
    def _(o):
        greet((me, tok_peer(o)))

    greet((sib, row))

    small_loads = [
        pltpu.make_async_copy(source, ref, load_sem.at[2 + k])
        for k, (source, ref) in enumerate(
            ((p_hbm, p_ref), (b_hbm, b_ref), (w_hbm, w_ref), (cot_hbm, cot_ref), (q_hbm, q_ref))
        )
    ]
    for load in small_loads:
        load.start()
    load_ow.start()
    load_kv.start()

    for load in small_loads:
        load.wait()
    for r in range(nt):
        parts = []
        for b in range(4):
            k = nt * b + (r + (nt // 2) * (b // 2)) % nt
            parts += [p_ref[v, :, k * LANES:(k + 1) * LANES].astype(F32) for v in range(2)]
        pl_[r] = jnp.concatenate(parts, axis=0).astype(BF16)
    bias = b_ref[...].astype(F32)
    bown[...] = jnp.concatenate(
        [bias[v:v + 1, k * LANES:(k + 1) * LANES] for v in range(2) for k in range(width // LANES)], axis=0
    ).astype(BF16)

    held = core * 2 + far
    mine = owner_of(row, held)
    unsent = jnp.where(mine == me, 1, 0) + jnp.where(sender, 1, 0)
    pl.semaphore_wait(barrier, 1 + (nz - 1) + nt + 4 + (nt - 1) + nt - unsent)

    local(pl_.at[row], pg.at[row], pg_recv)

    @pl.loop(1, nt)
    def _(o):
        peer = tok_peer(o)
        remote(pl_.at[peer], pg.at[row], pg_send.at[o], pg_recv, (me, peer))

    def to_partner(b, then_remote, then_local):
        partner = owner_of(row, b)
        itself = jnp.logical_and(partner == me, sender)

        @pl.when(itself)
        def _():
            then_local()

        @pl.when(jnp.logical_not(itself))
        def _():
            then_remote(partner, lax.rem(partner, 2))

    def send_weights(b):
        def away(partner, their):
            device = (partner, my_r)
            remote(w_ref.at[their], wf.at[my_a, their], w_send.at[b], w_recv.at[my_a], device)
            remote(bown, bt.at[my_a], b_send.at[b], b_recv.at[my_a], device)

        def here():
            local(w_ref.at[core], wf.at[my_a, core], w_recv.at[my_a])
            local(bown, bt.at[my_a], b_recv.at[my_a])

        to_partner(b, away, here)

    def send_pixels(b):
        to_partner(
            b,
            lambda partner, _: remote(pd.at[b], px.at[my_a], px_send.at[b], px_recv.at[my_a], (partner, my_r)),
            lambda: local(pd.at[b], px.at[my_a], px_recv.at[my_a]),
        )

    def partner_sent(b):
        def away(partner, their):
            wait_for(w_ref.at[0], w_send.at[b])
            wait_for(bown, b_send.at[b])
            wait_for(pd.at[0], px_send.at[b])

        to_partner(b, away, lambda: None)

    def first_sent():
        @pl.loop(1, nt)
        def _(o):
            wait_for(pl_.at[0], pg_send.at[o])

        pl.loop(0, 4)(partner_sent)

    pending.append(first_sent)
    pl.loop(0, 4)(send_weights)
    load_ow.wait()
    cot = cot_ref[...].astype(F32).reshape(OWN, width).astype(BF16)
    cgs[row] = dot_nt(cot, ow[...]).astype(BF16)

    lines = 16 * nt
    o_q = iota((lines, lines), 0)
    order = ones_at(
        iota((lines, lines), 1) == ((o_q >> 2) & (nt - 1)) * 16 + (o_q >> bits(4 * nt)) * 4 + (o_q & 3)
    )
    wait_for(pg, pg_recv)
    pd[...] = dot(order, pg[...].reshape(lines, LANES)).astype(BF16).reshape(4, 4 * nt, LANES)
    pl.loop(0, 4)(send_pixels)

    @pl.loop(1, nt)
    def _(o):
        remote(cgs.at[row], cgs.at[row], cg_send.at[o], cg_recv.at[o], (me, tok_peer(o)))

    def cg_sent():
        @pl.loop(1, nt)
        def _(o):
            wait_for(cgs.at[0], cg_send.at[o])

    pending.append(cg_sent)

    lane2 = iota((2 * toks, LANES), 1)
    tok2 = iota((2 * toks, LANES), 0) & (toks - 1)
    par2 = iota((2 * toks, LANES), 0) >> bits(toks)
    sel_k = iota((2 * toks, 4 * nt), 1)
    sel_r = iota((2 * toks, 4 * nt), 0)
    sel_t = sel_r & (toks - 1)
    sel = ones_at(sel_k == (sel_t >> 4) * 4 + (sel_r >> bits(toks)) * 2 + ((sel_t >> 3) & 1))
    same_lon = (tok2 & 7) == (lane2 >> 4)
    fold = ones_at(
        ((iota((LANES, LANES), 0) & 15) == (iota((LANES, LANES), 1) & 15)) & (iota((LANES, LANES), 1) < 32)
    )
    query = q_ref[...].astype(F32).reshape(1, width)
    head_of = (iota((width, LANES), 0) >> bits(HEAD_DIM)) == iota((width, LANES), 1)
    sum_heads = ones_at(head_of)
    q_cols = jnp.broadcast_to(query, (LANES, width)).T
    q_block = jnp.where(head_of, q_cols, 0.0).astype(BF16)
    spread[...] = ones_at((iota((LANES, width), 1) >> bits(HEAD_DIM)) == iota((LANES, width), 0))
    new = iota((1, width), 1)
    c_core = new >> bits(2 * nt * cp)
    c_far = (new >> bits(nt * cp)) & 1
    c_row = (new >> bits(cp)) & (nt - 1)
    c_z = (new >> bits(rpd)) & (nz - 1)
    old = ((((c_far * nz + c_z) * 2 + c_core) * nt) + c_row) * rpd + (new & (rpd - 1))
    for blk in range(width // LANES):
        lines = slice(blk * LANES, (blk + 1) * LANES)
        perm2[lines, :] = ones_at(iota((LANES, width), 0) + blk * LANES == old)

    def weights_arrived(a):
        wait_for(wf.at[a, core], w_recv.at[a])
        remote(wf.at[a, core], wf.at[a, core], wc_send.at[a], wc_recv.at[a], (sib, row))

    def wc_sent():
        @pl.loop(0, 4)
        def _(a):
            wait_for(wf.at[a, 0], wc_send.at[a])

    pending.append(wc_sent)
    load_kv.wait()
    weights_arrived(0)

    def chunk(a):
        x = dot(sel, px[a])
        x = jnp.where(same_lon, x, 0.0).astype(BF16)
        x = jnp.where((lane2 >> 4) == par2, dot(x, fold), 0.0)
        with_ones = jnp.where(lane2 == 32 + par2, 1.0, x)
        for par in range(2):
            xo[a * 2 + par] = with_ones[par * toks:(par + 1) * toks].astype(BF16)
            pixt[a * 2 + par] = with_ones[par * toks:(par + 1) * toks].T[0:48].astype(BF16)
        x = x.astype(BF16)[:, 0:32]
        biases = bt[a].astype(F32)
        w = wf[a].reshape(32, width)
        for k in range(width // LANES):
            lanes = slice(k * LANES, (k + 1) * LANES)
            e = dot(x, w[:, lanes])
            n = width // LANES
            e = e + jnp.where(par2 == 0, biases[k:k + 1], biases[n + k:n + k + 1])
            emb[:, lanes] = e.astype(BF16)
        keys = dot(emb[...], kv[:, :width]).astype(BF16)
        s = (dot(keys, q_block) * scale).T
        values = dot(emb[...], kv[:, width:]).astype(BF16)
        for par in range(2):
            mine = slice(par * toks, (par + 1) * toks)
            st[a * 2 + par] = s[0:HEADS, mine]
            val[a * 2 + par] = values[mine]

    @pl.loop(0, 4)
    def _(a):
        @pl.when(a < 3)
        def _():
            weights_arrived(a + 1)

        wait_for(px.at[a], px_recv.at[a])
        wait_for(bt.at[a], b_recv.at[a])
        wait_for(wf.at[a, 1 - core], wc_recv.at[a])
        chunk(a)

    @pl.loop(1, nt)
    def _(o):
        k = lax.rem(row - o + nt, nt)
        wait_for(cgs.at[k], cg_recv.at[o])

    cg_f = cgs[...].reshape(toks, width).astype(F32)

    @pl.loop(0, 4)
    def _(a):
        product = val[pl.ds(a * 2, 2)].astype(F32) * cg_f[None]
        high, low = split(product.reshape(2 * toks, width))
        g = (dot(high, sum_heads) + dot(low, sum_heads)).T
        for par in range(2):
            wgt[a * 2 + par] = g[0:HEADS, par * toks:(par + 1) * toks]

    s = st[...]
    wg = wgt[...]
    top = jnp.max(s, axis=0)
    e = jnp.exp(s - top[None])
    stat_own[0:16] = top
    stat_own[16:32] = jnp.sum(e, axis=0)
    stat_own[32:48] = jnp.sum(e * wg, axis=0)

    @pl.loop(1, nt)
    def _(o):
        remote(stat_own, stat.at[o], st_send.at[o], st_recv.at[o], (me, tok_peer(o)))

    def st_sent():
        @pl.loop(1, nt)
        def _(o):
            wait_for(stat_own, st_send.at[o])

    pending.append(st_sent)

    pair = jnp.concatenate(
        [wf[held].reshape(32, width).astype(F32)]
        + [jnp.concatenate([bt[held].astype(F32)[par * 8 + k:par * 8 + k + 1] for k in range(width // LANES)], axis=1)
           for par in range(2)]
        + [jnp.zeros((LANES - TAIL, width), F32)], axis=0
    ).astype(BF16)
    wbp[...] = dot(pair, perm2[...]).astype(BF16)
    wt_c[...] = wbp[...].astype(F32).T.astype(BF16)

    stat[0] = stat_own[...]

    @pl.loop(1, nt)
    def _(o):
        wait_for(stat.at[o], st_recv.at[o])

    tops = stat[:, 0:16]
    highest = jnp.max(tops, axis=0)
    factor = jnp.exp(tops - highest[None])
    norm = jnp.sum(stat[:, 16:32] * factor, axis=0)
    mean = jnp.sum(stat[:, 32:48] * factor, axis=0) / norm
    weights_f = e * (jnp.exp(top - highest) / norm)[None]
    sg = weights_f * (wg - mean[None]) * scale
    wgt[...] = sg
    turned = weights_f.reshape(8 * HEADS, toks).T
    for v in range(8):
        wtr[v] = turned[:, v * HEADS:(v + 1) * HEADS].astype(BF16)

    for t in range(4):
        a = lax.rem((1 - core) * 2 + t, 4)
        g_val = jnp.zeros((48, width), F32)
        g_key = jnp.zeros((HEADS, LANES), F32)
        for v in (2 * a, 2 * a + 1):
            w = dot(wtr[v], spread[0:HEADS, :])
            value_grad = (w * cg_f).astype(BF16)
            g_val = g_val + dot(pixt[v], value_grad)
            high, low = split(wgt[v])
            g_key = g_key + dot(high, xo[v]) + dot(low, xo[v])
        to_core, to_far = a // 2, lax.rem(a, 2)
        for z in range(nz):
            gs[to_core, to_far, z] = g_val[0:grows, z * cw:(z + 1) * cw]
            gs[to_core, to_far, z, TAIL:TAIL + per, 0:LANES] = g_key[z * per:(z + 1) * per, :]

        if t == 1:
            remote(gs.at[1 - core], g1, g1_send, g1_recv, (sib, row))

    pending.append(lambda: wait_for(g1, g1_send))
    total = jnp.zeros((toks, width), F32)
    for v in range(8):
        w = dot(wtr[v], spread[0:HEADS, :])
        total = total + w * val[v].astype(F32)
    ctx[...] = total.reshape(nt, OWN, width)
    cr[row] = ctx[row]

    @pl.loop(1, nt)
    def _(o):
        peer = tok_peer(o)
        remote(ctx.at[peer], cr.at[row], c_send.at[o], c_recv.at[o], (me, peer))

    def c_sent():
        @pl.loop(1, nt)
        def _(o):
            wait_for(ctx.at[0], c_send.at[o])

    pending.append(c_sent)

    wait_for(g1, g1_recv)
    h1[...] = gs[core] + g1[...]
    opposite = (at(1 - far, zed, core), row)
    remote(h1.at[1 - far, :, 0:SPLIT], g2, g2_send, g2_recv, opposite)
    pending.append(lambda: wait_for(g2, g2_send))

    @pl.loop(1, nz)
    def _(o):
        z = lax.rem(zed + o, nz)
        remote(h1.at[:, z, SPLIT:], k3.at[o], k3_send.at[o], k3_recv.at[o], (at(far, z, core), row))

    def k3_sent():
        @pl.loop(1, nz)
        def _(o):
            wait_for(k3.at[0], k3_send.at[o])

    pending.append(k3_sent)

    wait_for(g2, g2_recv)
    h2[...] = h1[far, :, 0:SPLIT] + g2[...]

    @pl.loop(1, nz)
    def _(o):
        z = lax.rem(zed + o, nz)
        remote(h2.at[z], g3.at[o], g3_send.at[o], g3_recv.at[o], (at(far, z, core), row))

    def g3_sent():
        @pl.loop(1, nz)
        def _(o):
            wait_for(h2.at[0], g3_send.at[o])

    pending.append(g3_sent)

    def wait_c():
        @pl.loop(1, nt)
        def _(o):
            wait_for(cr.at[lax.rem(row - o + nt, nt)], c_recv.at[o])

    g3[0] = h2[zed]
    k3[0] = h1[:, zed, SPLIT:]

    @pl.loop(1, nz)
    def _(o):
        wait_for(k3.at[o], k3_recv.at[o])

    k4[...] = jnp.sum(k3[...], axis=0)
    remote(k4.at[1 - far], k5, k5_send, k5_recv, opposite)
    pending.append(lambda: wait_for(k5, k5_send))

    @pl.loop(1, nz)
    def _(o):
        wait_for(g3.at[o], g3_recv.at[o])

    gp[0:SPLIT, :] = jnp.sum(g3[...], axis=0)
    wait_for(k5, k5_recv)
    gp[SPLIT:, :] = k4[far] + k5[...]

    def to_owner(r, then_remote, then_local):
        itself = jnp.logical_and(mine == me, r == row)

        @pl.when(itself)
        def _():
            then_local()

        @pl.when(jnp.logical_not(itself))
        def _():
            then_remote()

    @pl.loop(0, nt)
    def _(r):
        to_owner(
            r,
            lambda: remote(gp, gt.at[zed], gt_send.at[r], gt_recv, (mine, r)),
            lambda: local(gp, gt.at[zed], gt_recv),
        )

    def gt_sent():
        @pl.loop(0, nt)
        def _(r):
            to_owner(r, lambda: wait_for(gp, gt_send.at[r]), lambda: None)

    pending.append(gt_sent)

    lines = iota((grows, cw), 0)
    high, low = split(jnp.where(lines < TAIL, gp[...], 0.0))
    keys_here = jnp.concatenate([gp[TAIL:TAIL + per, 0:LANES], jnp.zeros((16 - per, LANES), F32)], axis=0)
    key_high, key_low = split(keys_here)
    half = width // 2

    def products(c):
        lines_c = pl.ds(pl.multiple_of(c * half, half), half)
        left = wt_c[lines_c, 0:grows]
        part = dot(left, high) + dot(left, low)
        right = wbp[:, lines_c]
        key_part = (dot(key_high, right) + dot(key_low, right))[0:8]
        for y in range(2):
            for r in range(nt):
                k = y * nt + r
                ps[c, y, r, 0:cp, :] = part[k * cp:(k + 1) * cp]
                ps[c, y, r, cp:, :] = jnp.zeros((8, cw), F32)
                ps[c, y, r, cp:, 0:cp] = key_part[:, k * cp:(k + 1) * cp]

    products(1 - core)
    remote(ps.at[1 - core], p1, p1_send, p1_recv, (sib, row))
    pending.append(lambda: wait_for(p1, p1_send))
    products(core)
    wait_for(p1, p1_recv)
    q1[...] = ps[core] + p1[...]

    @pl.loop(1, nt)
    def _(o):
        peer = tok_peer(o)
        remote(q1.at[far, peer], p2.at[far, row], p2_send.at[far, o], p2_recv, (me, peer))

    @pl.loop(0, nt)
    def _(o):
        peer = tok_peer(o)
        remote(
            q1.at[1 - far, peer], p2.at[far, row], p2_send.at[1 - far, o], p2_recv,
            (at(1 - far, zed, core), peer),
        )

    local(q1.at[far, row], p2.at[far, row], p2_recv)

    def p2_sent():
        @pl.loop(1, nt)
        def _(o):
            wait_for(q1.at[0, 0], p2_send.at[far, o])

        @pl.loop(0, nt)
        def _(o):
            wait_for(q1.at[0, 0], p2_send.at[1 - far, o])

    pending.append(p2_sent)

    wait_c()
    context = jnp.sum(cr[...], axis=0).astype(BF16)
    agg_ref[...] = dot(context, ow[...]).astype(BF16)

    wait_for(p2, p2_recv)
    mine_c = jnp.sum(p2[...].reshape(2 * nt, cp + 8, cw), axis=0)
    key_cols = jnp.concatenate([mine_c[cp:, 0:LANES], jnp.zeros((LANES - 8, LANES), F32)], axis=0).T
    for z in range(nz):
        os_[z, 0:rpd, :] = mine_c[z * rpd:(z + 1) * rpd]
        os_[z, rpd:, 0:LANES] = key_cols[z * rpd:(z + 1) * rpd]
    local(os_.at[zed], or_.at[zed], o_recv)

    @pl.loop(1, nz)
    def _(o):
        z = lax.rem(zed + o, nz)
        remote(os_.at[z], or_.at[zed], o_send.at[o], o_recv, (at(far, z, core), row))

    def o_sent():
        @pl.loop(1, nz)
        def _(o):
            wait_for(os_.at[0], o_send.at[o])

    pending.append(o_sent)

    wait_for(gt, gt_recv)
    gk[...] = jnp.zeros((LANES, LANES), F32)
    for z in range(nz):
        gk[z * per:(z + 1) * per, :] = gt[z, TAIL:TAIL + per, 0:LANES]
        high, low = split(gt[z])
        lanes = slice(width + z * cw, width + (z + 1) * cw)
        gx[0:grows, lanes] = high
        gx[grows:, lanes] = low
    key_high, key_low = split(gk[...].T[0:grows])
    q_rows = (spread[...].astype(F32) * query).astype(BF16)
    high, low = split(dot(key_high, q_rows) + dot(key_low, q_rows))
    gx[0:grows, :width] = high
    gx[grows:, :width] = low

    both = dot_nt(gx[...], kv[...])
    table = both[0:grows] + both[grows:]
    gw_ref[0] = table[0:16]
    gw_ref[1] = table[16:32]
    gb_ref[...] = table[32:34]

    wait_for(or_, o_recv)
    small = iota((rpd, cw), 1)
    for z in range(nz):
        lanes = slice(z * cw, (z + 1) * cw)
        gkv_ref[:, width + z * cw:width + (z + 1) * cw] = or_[z, 0:rpd, :]
        keyed = or_[z, rpd:, :]
        spread_key = jnp.zeros((rpd, cw), F32)
        for h in range(per):
            spread_key = jnp.where((small >> bits(HEAD_DIM)) == h, keyed[:, h:h + 1], spread_key)
        gkv_ref[:, lanes] = spread_key * query[:, lanes]

    for done in pending:
        done()


def copy_kernel(*refs):
    for k in range(4):
        refs[4 + k][...] = refs[k][...]


def shards(nv, nt, patches, embed_w, embed_b, query, kv_w, out_w, cotangent):
    width = kv_w.shape[0]
    rpd = width // (nv * nt)
    nz = nv // 4
    cw = width // nz
    grows = -(-(TAIL + HEADS // nz) // 8) * 8
    cp = width // (4 * nt)
    toks = nt * OWN
    vmem = pl.BlockSpec(memory_space=pltpu.VMEM)
    hbm = pl.BlockSpec(memory_space=pl.ANY)
    dma = pltpu.SemaphoreType.DMA
    f32 = lambda *shape: pltpu.VMEM(shape, F32)
    bf16 = lambda *shape: pltpu.VMEM(shape, BF16)
    outs = pl.pallas_call(
        functools.partial(kernel, nv, nt),
        out_shape=(
            jax.ShapeDtypeStruct((OWN, width), BF16),
            jax.ShapeDtypeStruct((rpd, 2 * width), F32),
            jax.ShapeDtypeStruct(embed_w.shape, F32),
            jax.ShapeDtypeStruct(embed_b.shape, F32),
        ),
        in_specs=[hbm] * 7,
        out_specs=(vmem,) * 4,
        scratch_shapes=[
            pltpu.VMEM(patches.shape, BF16),
            pltpu.VMEM(embed_w.shape, BF16),
            pltpu.VMEM(embed_b.shape, BF16),
            pltpu.VMEM(query.shape, BF16),
            pltpu.VMEM(cotangent.shape, BF16),
            bf16(width, 2 * width),
            bf16(width, width),
            bf16(nt, 16, LANES),
            bf16(nt, 16, LANES),
            bf16(4, 4 * nt, LANES),
            bf16(4, 4 * nt, LANES),
            bf16(4, 2, PIX, width),
            bf16(4, 16, LANES),
            bf16(16, LANES),
            bf16(nt, OWN, width),
            bf16(2 * toks, width),
            bf16(8, toks, width),
            f32(8, HEADS, toks),
            f32(8, HEADS, toks),
            f32(48, toks),
            f32(nt, 48, toks),
            bf16(8, toks, HEADS),
            bf16(8, toks, LANES),
            bf16(8, 48, toks),
            f32(2, 2, nz, grows, cw),
            f32(2, nz, grows, cw),
            f32(2, nz, grows, cw),
            f32(nz, SPLIT, cw),
            f32(nz, SPLIT, cw),
            f32(nz, SPLIT, cw),
            f32(nz, 2, grows - SPLIT, cw),
            f32(2, grows - SPLIT, cw),
            f32(grows - SPLIT, cw),
            f32(grows, cw),
            f32(nz, grows, cw),
            f32(LANES, LANES),
            bf16(2 * grows, 2 * width),
            bf16(width, width),
            bf16(LANES, width),
            bf16(width, LANES),
            f32(2, 2, nt, cp + 8, cw),
            f32(2, nt, cp + 8, cw),
            f32(2, nt, cp + 8, cw),
            f32(2, nt, cp + 8, cw),
            f32(nz, 2 * rpd, cw),
            f32(nz, 2 * rpd, cw),
            f32(nt, OWN, width),
            f32(nt, OWN, width),
            bf16(LANES, width),
            dma((7,)), dma((nt,)), dma, dma((4,)), dma((4,)), dma((4,)), dma((4,)), dma((4,)), dma((4,)), dma((4,)), dma((4,)),
            dma((nt,)), dma((nt,)), dma((nt,)), dma((nt,)), dma, dma, dma, dma, dma((nz,)), dma((nz,)), dma((nz,)), dma((nz,)), dma, dma,
            dma((nt,)), dma, dma, dma, dma((2, nt)), dma, dma((nz,)), dma, dma((nt,)), dma((nt,)),
        ],
        compiler_params=pltpu.CompilerParams(
            collective_id=0, has_side_effects=True, vmem_limit_bytes=56 * 1024 * 1024
        ),
        cost_estimate=pl.CostEstimate(flops=5_000_000_000, bytes_accessed=8_000_000, transcendentals=20_000),
    )(patches, embed_w, embed_b, query, cotangent, kv_w, out_w)
    aggregated, grad_kv, grad_w, grad_b = pl.pallas_call(
        copy_kernel,
        out_shape=[jax.ShapeDtypeStruct(x.shape, x.dtype) for x in outs],
        in_specs=[vmem] * 4,
        out_specs=[vmem] * 4,
    )(*outs)
    return aggregated.reshape(cotangent.shape), grad_kv, grad_w, grad_b


def solution(mesh):
    return jax.shard_map(
        functools.partial(shards, mesh.shape["var"], mesh.shape["tok"]),
        mesh=mesh,
        in_specs=(
            P("var", "tok", None),
            P("var", None, None),
            P("var", None),
            P(),
            P(),
            P(),
            P("tok", "var", None),
        ),
        out_specs=(
            P("tok", "var", None),
            P(("var", "tok"), None),
            P("var", None, None),
            P("var", None),
        ),
        check_vma=False,
    )
```

```python
import functools

import jax
import jax.numpy as jnp
from jax import lax
from jax.experimental import pallas as pl
from jax.experimental.pallas import tpu as pltpu
from jax.sharding import PartitionSpec as P

MESH = pl.DeviceIdType.MESH
F32 = jnp.float32
BF16 = jnp.bfloat16
LANES = 128
PIX = 16
OWN = 16
HEADS = 16
HEAD_DIM = 64
SPLIT = 24
TAIL = 34


def dot(a, b):
    return jnp.dot(a, b, preferred_element_type=F32)


def dot_nt(a, b):
    return lax.dot_general(a, b, (((1,), (1,)), ((), ())), preferred_element_type=F32)


def iota(shape, dim):
    return lax.broadcasted_iota(jnp.int32, shape, dim)


def ones_at(cond):
    return jnp.where(cond, 1.0, 0.0).astype(BF16)


def split(x):
    high = x.astype(BF16)
    return high, (x - high.astype(F32)).astype(BF16)


def bits(n):
    return n.bit_length() - 1


def remote(src, dst, send_sem, recv_sem, device):
    pltpu.make_async_remote_copy(
        src, dst, send_sem, recv_sem, device_id=device, device_id_type=MESH
    ).start()


def local(src, dst, sem):
    pltpu.make_async_copy(src, dst, sem).start()


def wait_for(ref, sem):
    pltpu.make_async_copy(ref, ref, sem).wait()


def kernel(
    nv, nt,
    p_hbm, w_hbm, b_hbm, q_hbm, cot_hbm, kv_hbm, ow_hbm,
    agg_ref, gkv_ref, gw_ref, gb_ref,
    p_ref, w_ref, b_ref, q_ref, cot_ref, kv, ow, pl_, pg, pd, px, wf, bt, bown, cgs, emb, val, st, wgt, stat_own, stat, wtr, xo, pixt,
    gs, g1, h1, g2, h2, g3, k3, k4, k5, gp, gt, gk, gx, perm2, wbp, wt_c, ps, p1, q1, p2, os_, or_, ctx, cr, spread,
    load_sem, pg_send, pg_recv, w_send, w_recv, b_send, b_recv, px_send, px_recv, wc_send, wc_recv,
    cg_send, cg_recv, st_send, st_recv, g1_send, g1_recv, g2_send, g2_recv, g3_send, g3_recv, k3_send, k3_recv, k5_send, k5_recv,
    gt_send, gt_recv, p1_send, p1_recv, p2_send, p2_recv, o_send, o_recv, c_send, c_recv,
):
    me = lax.axis_index("var")
    row = lax.axis_index("tok")
    nz = nv // 4
    core = lax.rem(me, 2)
    zed = lax.rem(me // 2, nz)
    far = me // (2 * nz)
    sib = me + 1 - 2 * core
    width = kv.shape[0]
    toks = nt * OWN
    cw = width // nz
    per = HEADS // nz
    grows = gp.shape[0]
    cp = width // (4 * nt)
    rpd = cp // nz
    scale = HEAD_DIM ** -0.5
    pending = []

    def tok_peer(o):
        return lax.rem(row + o, nt)

    def at(y, z, c):
        return (y * nz + z) * 2 + c

    def group_of(i):
        return lax.rem(i + (nt // 2) * (i // (2 * nz)), nt), i // nt

    def owner_of(r, a):
        return nt * a + lax.rem(r + (nt // 2) * (a // 2), nt)

    my_r, my_a = group_of(me)
    sender = my_r == row

    load_ow = pltpu.make_async_copy(ow_hbm, ow, load_sem.at[0])
    load_kv = pltpu.make_async_copy(kv_hbm, kv, load_sem.at[1])

    barrier = pltpu.get_barrier_semaphore()

    def greet(device):
        pl.semaphore_signal(barrier, inc=1, device_id=device, device_id_type=MESH)

    @pl.loop(0, 4)
    def _(b):
        partner = owner_of(row, b)

        @pl.when(jnp.logical_not(jnp.logical_and(partner == me, sender)))
        def _():
            greet((partner, my_r))

    @pl.loop(1, nz)
    def _(o):
        greet((at(far, lax.rem(zed + o, nz), core), row))

    @pl.loop(0, nz)
    def _(z):
        source = at(lax.rem(my_a, 2), z, my_a // 2)

        @pl.when(jnp.logical_not(jnp.logical_and(source == me, sender)))
        def _():
            greet((source, my_r))

    @pl.loop(0, nt)
    def _(o):
        greet((at(1 - far, zed, core), tok_peer(o)))

    @pl.loop(1, nt)
    def _(o):
        greet((me, tok_peer(o)))

    greet((sib, row))

    small_loads = [
        pltpu.make_async_copy(source, ref, load_sem.at[2 + k])
        for k, (source, ref) in enumerate(
            ((p_hbm, p_ref), (b_hbm, b_ref), (w_hbm, w_ref), (cot_hbm, cot_ref), (q_hbm, q_ref))
        )
    ]
    for load in small_loads:
        load.start()
    load_ow.start()
    load_kv.start()

    for load in small_loads:
        load.wait()
    for r in range(nt):
        parts = []
        for b in range(4):
            k = nt * b + (r + (nt // 2) * (b // 2)) % nt
            parts += [p_ref[v, :, k * LANES:(k + 1) * LANES].astype(F32) for v in range(2)]
        pl_[r] = jnp.concatenate(parts, axis=0).astype(BF16)
    bias = b_ref[...].astype(F32)
    bown[...] = jnp.concatenate(
        [bias[v:v + 1, k * LANES:(k + 1) * LANES] for v in range(2) for k in range(width // LANES)], axis=0
    ).astype(BF16)

    held = core * 2 + far
    mine = owner_of(row, held)
    unsent = jnp.where(mine == me, 1, 0) + jnp.where(sender, 1, 0)
    pl.semaphore_wait(barrier, 1 + (nz - 1) + nt + 4 + (nt - 1) + nt - unsent)

    local(pl_.at[row], pg.at[row], pg_recv)

    @pl.loop(1, nt)
    def _(o):
        peer = tok_peer(o)
        remote(pl_.at[peer], pg.at[row], pg_send.at[o], pg_recv, (me, peer))

    def to_partner(b, then_remote, then_local):
        partner = owner_of(row, b)
        itself = jnp.logical_and(partner == me, sender)

        @pl.when(itself)
        def _():
            then_local()

        @pl.when(jnp.logical_not(itself))
        def _():
            then_remote(partner, lax.rem(partner, 2))

    def send_weights(b):
        def away(partner, their):
            device = (partner, my_r)
            remote(w_ref.at[their], wf.at[my_a, their], w_send.at[b], w_recv.at[my_a], device)
            remote(bown, bt.at[my_a], b_send.at[b], b_recv.at[my_a], device)

        def here():
            local(w_ref.at[core], wf.at[my_a, core], w_recv.at[my_a])
            local(bown, bt.at[my_a], b_recv.at[my_a])

        to_partner(b, away, here)

    def send_pixels(b):
        to_partner(
            b,
            lambda partner, _: remote(pd.at[b], px.at[my_a], px_send.at[b], px_recv.at[my_a], (partner, my_r)),
            lambda: local(pd.at[b], px.at[my_a], px_recv.at[my_a]),
        )

    def partner_sent(b):
        def away(partner, their):
            wait_for(w_ref.at[0], w_send.at[b])
            wait_for(bown, b_send.at[b])
            wait_for(pd.at[0], px_send.at[b])

        to_partner(b, away, lambda: None)

    def first_sent():
        @pl.loop(1, nt)
        def _(o):
            wait_for(pl_.at[0], pg_send.at[o])

        pl.loop(0, 4)(partner_sent)

    pending.append(first_sent)
    pl.loop(0, 4)(send_weights)
    load_ow.wait()
    cot = cot_ref[...].astype(F32).reshape(OWN, width).astype(BF16)
    cgs[row] = dot_nt(cot, ow[...]).astype(BF16)

    lines = 16 * nt
    o_q = iota((lines, lines), 0)
    order = ones_at(
        iota((lines, lines), 1) == ((o_q >> 2) & (nt - 1)) * 16 + (o_q >> bits(4 * nt)) * 4 + (o_q & 3)
    )
    wait_for(pg, pg_recv)
    pd[...] = dot(order, pg[...].reshape(lines, LANES)).astype(BF16).reshape(4, 4 * nt, LANES)
    pl.loop(0, 4)(send_pixels)

    @pl.loop(1, nt)
    def _(o):
        remote(cgs.at[row], cgs.at[row], cg_send.at[o], cg_recv.at[o], (me, tok_peer(o)))

    def cg_sent():
        @pl.loop(1, nt)
        def _(o):
            wait_for(cgs.at[0], cg_send.at[o])

    pending.append(cg_sent)

    lane2 = iota((2 * toks, LANES), 1)
    tok2 = iota((2 * toks, LANES), 0) & (toks - 1)
    par2 = iota((2 * toks, LANES), 0) >> bits(toks)
    sel_k = iota((2 * toks, 4 * nt), 1)
    sel_r = iota((2 * toks, 4 * nt), 0)
    sel_t = sel_r & (toks - 1)
    sel = ones_at(sel_k == (sel_t >> 4) * 4 + (sel_r >> bits(toks)) * 2 + ((sel_t >> 3) & 1))
    same_lon = (tok2 & 7) == (lane2 >> 4)
    fold = ones_at(
        ((iota((LANES, LANES), 0) & 15) == (iota((LANES, LANES), 1) & 15)) & (iota((LANES, LANES), 1) < 32)
    )
    query = q_ref[...].astype(F32).reshape(1, width)
    head_of = (iota((width, LANES), 0) >> bits(HEAD_DIM)) == iota((width, LANES), 1)
    sum_heads = ones_at(head_of)
    q_cols = jnp.broadcast_to(query, (LANES, width)).T
    q_block = jnp.where(head_of, q_cols, 0.0).astype(BF16)
    spread[...] = ones_at((iota((LANES, width), 1) >> bits(HEAD_DIM)) == iota((LANES, width), 0))
    new = iota((1, width), 1)
    c_core = new >> bits(2 * nt * cp)
    c_far = (new >> bits(nt * cp)) & 1
    c_row = (new >> bits(cp)) & (nt - 1)
    c_z = (new >> bits(rpd)) & (nz - 1)
    old = ((((c_far * nz + c_z) * 2 + c_core) * nt) + c_row) * rpd + (new & (rpd - 1))
    for blk in range(width // LANES):
        lines = slice(blk * LANES, (blk + 1) * LANES)
        perm2[lines, :] = ones_at(iota((LANES, width), 0) + blk * LANES == old)

    def weights_arrived(a):
        wait_for(wf.at[a, core], w_recv.at[a])
        remote(wf.at[a, core], wf.at[a, core], wc_send.at[a], wc_recv.at[a], (sib, row))

    def wc_sent():
        @pl.loop(0, 4)
        def _(a):
            wait_for(wf.at[a, 0], wc_send.at[a])

    pending.append(wc_sent)
    load_kv.wait()
    weights_arrived(0)

    def chunk(a):
        x = dot(sel, px[a])
        x = jnp.where(same_lon, x, 0.0).astype(BF16)
        x = jnp.where((lane2 >> 4) == par2, dot(x, fold), 0.0)
        with_ones = jnp.where(lane2 == 32 + par2, 1.0, x)
        for par in range(2):
            xo[a * 2 + par] = with_ones[par * toks:(par + 1) * toks].astype(BF16)
            pixt[a * 2 + par] = with_ones[par * toks:(par + 1) * toks].T[0:48].astype(BF16)
        x = x.astype(BF16)[:, 0:32]
        biases = bt[a].astype(F32)
        w = wf[a].reshape(32, width)
        for k in range(width // LANES):
            lanes = slice(k * LANES, (k + 1) * LANES)
            e = dot(x, w[:, lanes])
            n = width // LANES
            e = e + jnp.where(par2 == 0, biases[k:k + 1], biases[n + k:n + k + 1])
            emb[:, lanes] = e.astype(BF16)
        keys = dot(emb[...], kv[:, :width]).astype(BF16)
        s = (dot(keys, q_block) * scale).T
        values = dot(emb[...], kv[:, width:]).astype(BF16)
        for par in range(2):
            mine = slice(par * toks, (par + 1) * toks)
            st[a * 2 + par] = s[0:HEADS, mine]
            val[a * 2 + par] = values[mine]

    @pl.loop(0, 4)
    def _(a):
        @pl.when(a < 3)
        def _():
            weights_arrived(a + 1)

        wait_for(px.at[a], px_recv.at[a])
        wait_for(bt.at[a], b_recv.at[a])
        wait_for(wf.at[a, 1 - core], wc_recv.at[a])
        chunk(a)

    @pl.loop(1, nt)
    def _(o):
        k = lax.rem(row - o + nt, nt)
        wait_for(cgs.at[k], cg_recv.at[o])

    cg_f = cgs[...].reshape(toks, width).astype(F32)

    @pl.loop(0, 4)
    def _(a):
        product = val[pl.ds(a * 2, 2)].astype(F32) * cg_f[None]
        high, low = split(product.reshape(2 * toks, width))
        g = (dot(high, sum_heads) + dot(low, sum_heads)).T
        for par in range(2):
            wgt[a * 2 + par] = g[0:HEADS, par * toks:(par + 1) * toks]

    s = st[...]
    wg = wgt[...]
    top = jnp.max(s, axis=0)
    e = jnp.exp(s - top[None])
    stat_own[0:16] = top
    stat_own[16:32] = jnp.sum(e, axis=0)
    stat_own[32:48] = jnp.sum(e * wg, axis=0)

    @pl.loop(1, nt)
    def _(o):
        remote(stat_own, stat.at[o], st_send.at[o], st_recv.at[o], (me, tok_peer(o)))

    def st_sent():
        @pl.loop(1, nt)
        def _(o):
            wait_for(stat_own, st_send.at[o])

    pending.append(st_sent)

    pair = jnp.concatenate(
        [wf[held].reshape(32, width).astype(F32)]
        + [jnp.concatenate([bt[held].astype(F32)[par * 8 + k:par * 8 + k + 1] for k in range(width // LANES)], axis=1)
           for par in range(2)]
        + [jnp.zeros((LANES - TAIL, width), F32)], axis=0
    ).astype(BF16)
    wbp[...] = dot(pair, perm2[...]).astype(BF16)
    wt_c[...] = wbp[...].astype(F32).T.astype(BF16)

    stat[0] = stat_own[...]

    @pl.loop(1, nt)
    def _(o):
        wait_for(stat.at[o], st_recv.at[o])

    tops = stat[:, 0:16]
    highest = jnp.max(tops, axis=0)
    factor = jnp.exp(tops - highest[None])
    norm = jnp.sum(stat[:, 16:32] * factor, axis=0)
    mean = jnp.sum(stat[:, 32:48] * factor, axis=0) / norm
    weights_f = e * (jnp.exp(top - highest) / norm)[None]
    sg = weights_f * (wg - mean[None]) * scale
    wgt[...] = sg
    turned = weights_f.reshape(8 * HEADS, toks).T
    for v in range(8):
        wtr[v] = turned[:, v * HEADS:(v + 1) * HEADS].astype(BF16)

    for t in range(4):
        a = lax.rem((1 - core) * 2 + t, 4)
        g_val = jnp.zeros((48, width), F32)
        g_key = jnp.zeros((HEADS, LANES), F32)
        for v in (2 * a, 2 * a + 1):
            w = dot(wtr[v], spread[0:HEADS, :])
            value_grad = (w * cg_f).astype(BF16)
            g_val = g_val + dot(pixt[v], value_grad)
            high, low = split(wgt[v])
            g_key = g_key + dot(high, xo[v]) + dot(low, xo[v])
        to_core, to_far = a // 2, lax.rem(a, 2)
        for z in range(nz):
            gs[to_core, to_far, z] = g_val[0:grows, z * cw:(z + 1) * cw]
            gs[to_core, to_far, z, TAIL:TAIL + per, 0:LANES] = g_key[z * per:(z + 1) * per, :]

        if t == 1:
            remote(gs.at[1 - core], g1, g1_send, g1_recv, (sib, row))

    pending.append(lambda: wait_for(g1, g1_send))
    wait_for(g1, g1_recv)
    h1[...] = gs[core] + g1[...]
    opposite = (at(1 - far, zed, core), row)
    remote(h1.at[1 - far, :, 0:SPLIT], g2, g2_send, g2_recv, opposite)
    pending.append(lambda: wait_for(g2, g2_send))

    @pl.loop(1, nz)
    def _(o):
        z = lax.rem(zed + o, nz)
        remote(h1.at[:, z, SPLIT:], k3.at[o], k3_send.at[o], k3_recv.at[o], (at(far, z, core), row))

    def k3_sent():
        @pl.loop(1, nz)
        def _(o):
            wait_for(k3.at[0], k3_send.at[o])

    pending.append(k3_sent)

    total = jnp.zeros((toks, width), F32)
    for v in range(8):
        w = dot(wtr[v], spread[0:HEADS, :])
        total = total + w * val[v].astype(F32)
    ctx[...] = total.reshape(nt, OWN, width)
    cr[row] = ctx[row]

    wait_for(g2, g2_recv)
    h2[...] = h1[far, :, 0:SPLIT] + g2[...]

    @pl.loop(1, nz)
    def _(o):
        z = lax.rem(zed + o, nz)
        remote(h2.at[z], g3.at[o], g3_send.at[o], g3_recv.at[o], (at(far, z, core), row))

    def g3_sent():
        @pl.loop(1, nz)
        def _(o):
            wait_for(h2.at[0], g3_send.at[o])

    pending.append(g3_sent)

    @pl.loop(1, nt)
    def _(o):
        peer = tok_peer(o)
        remote(ctx.at[peer], cr.at[row], c_send.at[o], c_recv.at[o], (me, peer))

    def c_sent():
        @pl.loop(1, nt)
        def _(o):
            wait_for(ctx.at[0], c_send.at[o])

    pending.append(c_sent)

    def wait_c():
        @pl.loop(1, nt)
        def _(o):
            wait_for(cr.at[lax.rem(row - o + nt, nt)], c_recv.at[o])

    g3[0] = h2[zed]
    k3[0] = h1[:, zed, SPLIT:]

    @pl.loop(1, nz)
    def _(o):
        wait_for(k3.at[o], k3_recv.at[o])

    k4[...] = jnp.sum(k3[...], axis=0)
    remote(k4.at[1 - far], k5, k5_send, k5_recv, opposite)
    pending.append(lambda: wait_for(k5, k5_send))

    @pl.loop(1, nz)
    def _(o):
        wait_for(g3.at[o], g3_recv.at[o])

    gp[0:SPLIT, :] = jnp.sum(g3[...], axis=0)
    wait_for(k5, k5_recv)
    gp[SPLIT:, :] = k4[far] + k5[...]

    def to_owner(r, then_remote, then_local):
        itself = jnp.logical_and(mine == me, r == row)

        @pl.when(itself)
        def _():
            then_local()

        @pl.when(jnp.logical_not(itself))
        def _():
            then_remote()

    @pl.loop(0, nt)
    def _(r):
        to_owner(
            r,
            lambda: remote(gp, gt.at[zed], gt_send.at[r], gt_recv, (mine, r)),
            lambda: local(gp, gt.at[zed], gt_recv),
        )

    def gt_sent():
        @pl.loop(0, nt)
        def _(r):
            to_owner(r, lambda: wait_for(gp, gt_send.at[r]), lambda: None)

    pending.append(gt_sent)

    lines = iota((grows, cw), 0)
    high, low = split(jnp.where(lines < TAIL, gp[...], 0.0))
    keys_here = jnp.concatenate([gp[TAIL:TAIL + per, 0:LANES], jnp.zeros((16 - per, LANES), F32)], axis=0)
    key_high, key_low = split(keys_here)
    half = width // 2

    def products(c):
        lines_c = pl.ds(pl.multiple_of(c * half, half), half)
        left = wt_c[lines_c, 0:grows]
        part = dot(left, high) + dot(left, low)
        right = wbp[:, lines_c]
        key_part = (dot(key_high, right) + dot(key_low, right))[0:8]
        for y in range(2):
            for r in range(nt):
                k = y * nt + r
                ps[c, y, r, 0:cp, :] = part[k * cp:(k + 1) * cp]
                ps[c, y, r, cp:, :] = jnp.zeros((8, cw), F32)
                ps[c, y, r, cp:, 0:cp] = key_part[:, k * cp:(k + 1) * cp]

    products(1 - core)
    remote(ps.at[1 - core], p1, p1_send, p1_recv, (sib, row))
    pending.append(lambda: wait_for(p1, p1_send))
    products(core)
    wait_for(p1, p1_recv)
    q1[...] = ps[core] + p1[...]

    @pl.loop(1, nt)
    def _(o):
        peer = tok_peer(o)
        remote(q1.at[far, peer], p2.at[far, row], p2_send.at[far, o], p2_recv, (me, peer))

    @pl.loop(0, nt)
    def _(o):
        peer = tok_peer(o)
        remote(
            q1.at[1 - far, peer], p2.at[far, row], p2_send.at[1 - far, o], p2_recv,
            (at(1 - far, zed, core), peer),
        )

    local(q1.at[far, row], p2.at[far, row], p2_recv)

    def p2_sent():
        @pl.loop(1, nt)
        def _(o):
            wait_for(q1.at[0, 0], p2_send.at[far, o])

        @pl.loop(0, nt)
        def _(o):
            wait_for(q1.at[0, 0], p2_send.at[1 - far, o])

    pending.append(p2_sent)

    wait_c()
    context = jnp.sum(cr[...], axis=0).astype(BF16)
    agg_ref[...] = dot(context, ow[...]).astype(BF16)

    wait_for(p2, p2_recv)
    mine_c = jnp.sum(p2[...].reshape(2 * nt, cp + 8, cw), axis=0)
    key_cols = jnp.concatenate([mine_c[cp:, 0:LANES], jnp.zeros((LANES - 8, LANES), F32)], axis=0).T
    for z in range(nz):
        os_[z, 0:rpd, :] = mine_c[z * rpd:(z + 1) * rpd]
        os_[z, rpd:, 0:LANES] = key_cols[z * rpd:(z + 1) * rpd]
    local(os_.at[zed], or_.at[zed], o_recv)

    @pl.loop(1, nz)
    def _(o):
        z = lax.rem(zed + o, nz)
        remote(os_.at[z], or_.at[zed], o_send.at[o], o_recv, (at(far, z, core), row))

    def o_sent():
        @pl.loop(1, nz)
        def _(o):
            wait_for(os_.at[0], o_send.at[o])

    pending.append(o_sent)

    wait_for(gt, gt_recv)
    gk[...] = jnp.zeros((LANES, LANES), F32)
    for z in range(nz):
        gk[z * per:(z + 1) * per, :] = gt[z, TAIL:TAIL + per, 0:LANES]
        high, low = split(gt[z])
        lanes = slice(width + z * cw, width + (z + 1) * cw)
        gx[0:grows, lanes] = high
        gx[grows:, lanes] = low
    key_high, key_low = split(gk[...].T[0:grows])
    q_rows = (spread[...].astype(F32) * query).astype(BF16)
    high, low = split(dot(key_high, q_rows) + dot(key_low, q_rows))
    gx[0:grows, :width] = high
    gx[grows:, :width] = low

    both = dot_nt(gx[...], kv[...])
    table = both[0:grows] + both[grows:]
    gw_ref[0] = table[0:16]
    gw_ref[1] = table[16:32]
    gb_ref[...] = table[32:34]

    wait_for(or_, o_recv)
    small = iota((rpd, cw), 1)
    for z in range(nz):
        lanes = slice(z * cw, (z + 1) * cw)
        gkv_ref[:, width + z * cw:width + (z + 1) * cw] = or_[z, 0:rpd, :]
        keyed = or_[z, rpd:, :]
        spread_key = jnp.zeros((rpd, cw), F32)
        for h in range(per):
            spread_key = jnp.where((small >> bits(HEAD_DIM)) == h, keyed[:, h:h + 1], spread_key)
        gkv_ref[:, lanes] = spread_key * query[:, lanes]

    for done in pending:
        done()


def copy_kernel(*refs):
    for k in range(4):
        refs[4 + k][...] = refs[k][...]


def shards(nv, nt, patches, embed_w, embed_b, query, kv_w, out_w, cotangent):
    width = kv_w.shape[0]
    rpd = width // (nv * nt)
    nz = nv // 4
    cw = width // nz
    grows = -(-(TAIL + HEADS // nz) // 8) * 8
    cp = width // (4 * nt)
    toks = nt * OWN
    vmem = pl.BlockSpec(memory_space=pltpu.VMEM)
    hbm = pl.BlockSpec(memory_space=pl.ANY)
    dma = pltpu.SemaphoreType.DMA
    f32 = lambda *shape: pltpu.VMEM(shape, F32)
    bf16 = lambda *shape: pltpu.VMEM(shape, BF16)
    outs = pl.pallas_call(
        functools.partial(kernel, nv, nt),
        out_shape=(
            jax.ShapeDtypeStruct((OWN, width), BF16),
            jax.ShapeDtypeStruct((rpd, 2 * width), F32),
            jax.ShapeDtypeStruct(embed_w.shape, F32),
            jax.ShapeDtypeStruct(embed_b.shape, F32),
        ),
        in_specs=[hbm] * 7,
        out_specs=(vmem,) * 4,
        scratch_shapes=[
            pltpu.VMEM(patches.shape, BF16),
            pltpu.VMEM(embed_w.shape, BF16),
            pltpu.VMEM(embed_b.shape, BF16),
            pltpu.VMEM(query.shape, BF16),
            pltpu.VMEM(cotangent.shape, BF16),
            bf16(width, 2 * width),
            bf16(width, width),
            bf16(nt, 16, LANES),
            bf16(nt, 16, LANES),
            bf16(4, 4 * nt, LANES),
            bf16(4, 4 * nt, LANES),
            bf16(4, 2, PIX, width),
            bf16(4, 16, LANES),
            bf16(16, LANES),
            bf16(nt, OWN, width),
            bf16(2 * toks, width),
            bf16(8, toks, width),
            f32(8, HEADS, toks),
            f32(8, HEADS, toks),
            f32(48, toks),
            f32(nt, 48, toks),
            bf16(8, toks, HEADS),
            bf16(8, toks, LANES),
            bf16(8, 48, toks),
            f32(2, 2, nz, grows, cw),
            f32(2, nz, grows, cw),
            f32(2, nz, grows, cw),
            f32(nz, SPLIT, cw),
            f32(nz, SPLIT, cw),
            f32(nz, SPLIT, cw),
            f32(nz, 2, grows - SPLIT, cw),
            f32(2, grows - SPLIT, cw),
            f32(grows - SPLIT, cw),
            f32(grows, cw),
            f32(nz, grows, cw),
            f32(LANES, LANES),
            bf16(2 * grows, 2 * width),
            bf16(width, width),
            bf16(LANES, width),
            bf16(width, LANES),
            f32(2, 2, nt, cp + 8, cw),
            f32(2, nt, cp + 8, cw),
            f32(2, nt, cp + 8, cw),
            f32(2, nt, cp + 8, cw),
            f32(nz, 2 * rpd, cw),
            f32(nz, 2 * rpd, cw),
            f32(nt, OWN, width),
            f32(nt, OWN, width),
            bf16(LANES, width),
            dma((7,)), dma((nt,)), dma, dma((4,)), dma((4,)), dma((4,)), dma((4,)), dma((4,)), dma((4,)), dma((4,)), dma((4,)),
            dma((nt,)), dma((nt,)), dma((nt,)), dma((nt,)), dma, dma, dma, dma, dma((nz,)), dma((nz,)), dma((nz,)), dma((nz,)), dma, dma,
            dma((nt,)), dma, dma, dma, dma((2, nt)), dma, dma((nz,)), dma, dma((nt,)), dma((nt,)),
        ],
        compiler_params=pltpu.CompilerParams(
            collective_id=0, has_side_effects=True, vmem_limit_bytes=56 * 1024 * 1024
        ),
        cost_estimate=pl.CostEstimate(flops=5_000_000_000, bytes_accessed=8_000_000, transcendentals=20_000),
    )(patches, embed_w, embed_b, query, cotangent, kv_w, out_w)
    aggregated, grad_kv, grad_w, grad_b = pl.pallas_call(
        copy_kernel,
        out_shape=[jax.ShapeDtypeStruct(x.shape, x.dtype) for x in outs],
        in_specs=[vmem] * 4,
        out_specs=[vmem] * 4,
    )(*outs)
    return aggregated.reshape(cotangent.shape), grad_kv, grad_w, grad_b


def solution(mesh):
    return jax.shard_map(
        functools.partial(shards, mesh.shape["var"], mesh.shape["tok"]),
        mesh=mesh,
        in_specs=(
            P("var", "tok", None),
            P("var", None, None),
            P("var", None),
            P(),
            P(),
            P(),
            P("tok", "var", None),
        ),
        out_specs=(
            P("tok", "var", None),
            P(("var", "tok"), None),
            P("var", None, None),
            P("var", None),
        ),
        check_vma=False,
    )
```

```python
import functools

import jax
import jax.numpy as jnp
from jax import lax
from jax.experimental import pallas as pl
from jax.experimental.pallas import tpu as pltpu
from jax.sharding import PartitionSpec as P

MESH = pl.DeviceIdType.MESH
F32 = jnp.float32
BF16 = jnp.bfloat16
LANES = 128
PIX = 16
OWN = 16
HEADS = 16
HEAD_DIM = 64
SPLIT = 24
TAIL = 34


def dot(a, b):
    return jnp.dot(a, b, preferred_element_type=F32)


def dot_nt(a, b):
    return lax.dot_general(a, b, (((1,), (1,)), ((), ())), preferred_element_type=F32)


def iota(shape, dim):
    return lax.broadcasted_iota(jnp.int32, shape, dim)


def ones_at(cond):
    return jnp.where(cond, 1.0, 0.0).astype(BF16)


def split(x):
    high = x.astype(BF16)
    return high, (x - high.astype(F32)).astype(BF16)


def bits(n):
    return n.bit_length() - 1


def remote(src, dst, send_sem, recv_sem, device):
    pltpu.make_async_remote_copy(
        src, dst, send_sem, recv_sem, device_id=device, device_id_type=MESH
    ).start()


def local(src, dst, sem):
    pltpu.make_async_copy(src, dst, sem).start()


def wait_for(ref, sem):
    pltpu.make_async_copy(ref, ref, sem).wait()


def kernel(
    nv, nt,
    p_hbm, w_hbm, b_hbm, q_hbm, cot_hbm, kv_hbm, ow_hbm,
    agg_ref, gkv_ref, gw_ref, gb_ref,
    p_ref, w_ref, b_ref, q_ref, cot_ref, kv, ow, pl_, pg, pd, px, wf, bt, bown, cgs, emb, val, st, wgt, stat_own, stat, wtr, xo, pixt,
    gs, g1, h1, g2, h2, g3, k3, k4, k5, gp, gt, gk, gx, perm2, wbp, wt_c, ps, p1, q1, p2, os_, or_, ctx, cr, spread,
    load_sem, pg_send, pg_recv, w_send, w_recv, b_send, b_recv, px_send, px_recv, wc_send, wc_recv,
    cg_send, cg_recv, st_send, st_recv, g1_send, g1_recv, g2_send, g2_recv, g3_send, g3_recv, k3_send, k3_recv, k5_send, k5_recv,
    gt_send, gt_recv, p1_send, p1_recv, p2_send, p2_recv, o_send, o_recv, c_send, c_recv,
):
    me = lax.axis_index("var")
    row = lax.axis_index("tok")
    nz = nv // 4
    core = lax.rem(me, 2)
    zed = lax.rem(me // 2, nz)
    far = me // (2 * nz)
    sib = me + 1 - 2 * core
    width = kv.shape[0]
    toks = nt * OWN
    cw = width // nz
    per = HEADS // nz
    grows = gp.shape[0]
    cp = width // (4 * nt)
    rpd = cp // nz
    scale = HEAD_DIM ** -0.5
    pending = []

    def tok_peer(o):
        return lax.rem(row + o, nt)

    def at(y, z, c):
        return (y * nz + z) * 2 + c

    def group_of(i):
        return lax.rem(i + (nt // 2) * (i // (2 * nz)), nt), i // nt

    def owner_of(r, a):
        return nt * a + lax.rem(r + (nt // 2) * (a // 2), nt)

    my_r, my_a = group_of(me)
    sender = my_r == row

    load_ow = pltpu.make_async_copy(ow_hbm, ow, load_sem.at[0])
    load_kv = pltpu.make_async_copy(kv_hbm, kv, load_sem.at[1])

    barrier = pltpu.get_barrier_semaphore()

    def greet(device):
        pl.semaphore_signal(barrier, inc=1, device_id=device, device_id_type=MESH)

    @pl.loop(0, 4)
    def _(b):
        partner = owner_of(row, b)

        @pl.when(jnp.logical_not(jnp.logical_and(partner == me, sender)))
        def _():
            greet((partner, my_r))

    @pl.loop(1, nz)
    def _(o):
        greet((at(far, lax.rem(zed + o, nz), core), row))

    @pl.loop(0, nz)
    def _(z):
        source = at(lax.rem(my_a, 2), z, my_a // 2)

        @pl.when(jnp.logical_not(jnp.logical_and(source == me, sender)))
        def _():
            greet((source, my_r))

    @pl.loop(0, nt)
    def _(o):
        greet((at(1 - far, zed, core), tok_peer(o)))

    @pl.loop(1, nt)
    def _(o):
        greet((me, tok_peer(o)))

    greet((sib, row))

    small_loads = [
        pltpu.make_async_copy(source, ref, load_sem.at[2 + k])
        for k, (source, ref) in enumerate(
            ((p_hbm, p_ref), (b_hbm, b_ref), (w_hbm, w_ref), (cot_hbm, cot_ref), (q_hbm, q_ref))
        )
    ]
    for load in small_loads:
        load.start()
    load_ow.start()
    load_kv.start()

    for load in small_loads:
        load.wait()
    for r in range(nt):
        parts = []
        for b in range(4):
            k = nt * b + (r + (nt // 2) * (b // 2)) % nt
            parts += [p_ref[v, :, k * LANES:(k + 1) * LANES].astype(F32) for v in range(2)]
        pl_[r] = jnp.concatenate(parts, axis=0).astype(BF16)
    bias = b_ref[...].astype(F32)
    bown[...] = jnp.concatenate(
        [bias[v:v + 1, k * LANES:(k + 1) * LANES] for v in range(2) for k in range(width // LANES)], axis=0
    ).astype(BF16)

    held = core * 2 + far
    mine = owner_of(row, held)
    unsent = jnp.where(mine == me, 1, 0) + jnp.where(sender, 1, 0)
    pl.semaphore_wait(barrier, 1 + (nz - 1) + nt + 4 + (nt - 1) + nt - unsent)

    local(pl_.at[row], pg.at[row], pg_recv)

    @pl.loop(1, nt)
    def _(o):
        peer = tok_peer(o)
        remote(pl_.at[peer], pg.at[row], pg_send.at[o], pg_recv, (me, peer))

    def to_partner(b, then_remote, then_local):
        partner = owner_of(row, b)
        itself = jnp.logical_and(partner == me, sender)

        @pl.when(itself)
        def _():
            then_local()

        @pl.when(jnp.logical_not(itself))
        def _():
            then_remote(partner, lax.rem(partner, 2))

    def send_weights(b):
        def away(partner, their):
            device = (partner, my_r)
            remote(w_ref.at[their], wf.at[my_a, their], w_send.at[b], w_recv.at[my_a], device)
            remote(bown, bt.at[my_a], b_send.at[b], b_recv.at[my_a], device)

        def here():
            local(w_ref.at[core], wf.at[my_a, core], w_recv.at[my_a])
            local(bown, bt.at[my_a], b_recv.at[my_a])

        to_partner(b, away, here)

    def send_pixels(b):
        to_partner(
            b,
            lambda partner, _: remote(pd.at[b], px.at[my_a], px_send.at[b], px_recv.at[my_a], (partner, my_r)),
            lambda: local(pd.at[b], px.at[my_a], px_recv.at[my_a]),
        )

    def partner_sent(b):
        def away(partner, their):
            wait_for(w_ref.at[0], w_send.at[b])
            wait_for(bown, b_send.at[b])
            wait_for(pd.at[0], px_send.at[b])

        to_partner(b, away, lambda: None)

    def first_sent():
        @pl.loop(1, nt)
        def _(o):
            wait_for(pl_.at[0], pg_send.at[o])

        pl.loop(0, 4)(partner_sent)

    pending.append(first_sent)
    pl.loop(0, 4)(send_weights)
    lines = 16 * nt
    o_q = iota((lines, lines), 0)
    order = ones_at(
        iota((lines, lines), 1) == ((o_q >> 2) & (nt - 1)) * 16 + (o_q >> bits(4 * nt)) * 4 + (o_q & 3)
    )
    wait_for(pg, pg_recv)
    pd[...] = dot(order, pg[...].reshape(lines, LANES)).astype(BF16).reshape(4, 4 * nt, LANES)
    pl.loop(0, 4)(send_pixels)

    load_ow.wait()
    cot = cot_ref[...].astype(F32).reshape(OWN, width).astype(BF16)
    cgs[row] = dot_nt(cot, ow[...]).astype(BF16)

    @pl.loop(1, nt)
    def _(o):
        remote(cgs.at[row], cgs.at[row], cg_send.at[o], cg_recv.at[o], (me, tok_peer(o)))

    def cg_sent():
        @pl.loop(1, nt)
        def _(o):
            wait_for(cgs.at[0], cg_send.at[o])

    pending.append(cg_sent)

    lane2 = iota((2 * toks, LANES), 1)
    tok2 = iota((2 * toks, LANES), 0) & (toks - 1)
    par2 = iota((2 * toks, LANES), 0) >> bits(toks)
    sel_k = iota((2 * toks, 4 * nt), 1)
    sel_r = iota((2 * toks, 4 * nt), 0)
    sel_t = sel_r & (toks - 1)
    sel = ones_at(sel_k == (sel_t >> 4) * 4 + (sel_r >> bits(toks)) * 2 + ((sel_t >> 3) & 1))
    same_lon = (tok2 & 7) == (lane2 >> 4)
    fold = ones_at(
        ((iota((LANES, LANES), 0) & 15) == (iota((LANES, LANES), 1) & 15)) & (iota((LANES, LANES), 1) < 32)
    )
    query = q_ref[...].astype(F32).reshape(1, width)
    head_of = (iota((width, LANES), 0) >> bits(HEAD_DIM)) == iota((width, LANES), 1)
    sum_heads = ones_at(head_of)
    q_cols = jnp.broadcast_to(query, (LANES, width)).T
    q_block = jnp.where(head_of, q_cols, 0.0).astype(BF16)
    spread[...] = ones_at((iota((LANES, width), 1) >> bits(HEAD_DIM)) == iota((LANES, width), 0))
    new = iota((1, width), 1)
    c_core = new >> bits(2 * nt * cp)
    c_far = (new >> bits(nt * cp)) & 1
    c_row = (new >> bits(cp)) & (nt - 1)
    c_z = (new >> bits(rpd)) & (nz - 1)
    old = ((((c_far * nz + c_z) * 2 + c_core) * nt) + c_row) * rpd + (new & (rpd - 1))
    for blk in range(width // LANES):
        lines = slice(blk * LANES, (blk + 1) * LANES)
        perm2[lines, :] = ones_at(iota((LANES, width), 0) + blk * LANES == old)

    def weights_arrived(a):
        wait_for(wf.at[a, core], w_recv.at[a])
        remote(wf.at[a, core], wf.at[a, core], wc_send.at[a], wc_recv.at[a], (sib, row))

    def wc_sent():
        @pl.loop(0, 4)
        def _(a):
            wait_for(wf.at[a, 0], wc_send.at[a])

    pending.append(wc_sent)
    load_kv.wait()
    weights_arrived(0)

    def chunk(a):
        x = dot(sel, px[a])
        x = jnp.where(same_lon, x, 0.0).astype(BF16)
        x = jnp.where((lane2 >> 4) == par2, dot(x, fold), 0.0)
        with_ones = jnp.where(lane2 == 32 + par2, 1.0, x)
        for par in range(2):
            xo[a * 2 + par] = with_ones[par * toks:(par + 1) * toks].astype(BF16)
            pixt[a * 2 + par] = with_ones[par * toks:(par + 1) * toks].T[0:48].astype(BF16)
        x = x.astype(BF16)[:, 0:32]
        biases = bt[a].astype(F32)
        w = wf[a].reshape(32, width)
        for k in range(width // LANES):
            lanes = slice(k * LANES, (k + 1) * LANES)
            e = dot(x, w[:, lanes])
            n = width // LANES
            e = e + jnp.where(par2 == 0, biases[k:k + 1], biases[n + k:n + k + 1])
            emb[:, lanes] = e.astype(BF16)
        keys = dot(emb[...], kv[:, :width]).astype(BF16)
        s = (dot(keys, q_block) * scale).T
        values = dot(emb[...], kv[:, width:]).astype(BF16)
        for par in range(2):
            mine = slice(par * toks, (par + 1) * toks)
            st[a * 2 + par] = s[0:HEADS, mine]
            val[a * 2 + par] = values[mine]

    @pl.loop(0, 4)
    def _(a):
        @pl.when(a < 3)
        def _():
            weights_arrived(a + 1)

        wait_for(px.at[a], px_recv.at[a])
        wait_for(bt.at[a], b_recv.at[a])
        wait_for(wf.at[a, 1 - core], wc_recv.at[a])
        chunk(a)

    @pl.loop(1, nt)
    def _(o):
        k = lax.rem(row - o + nt, nt)
        wait_for(cgs.at[k], cg_recv.at[o])

    cg_f = cgs[...].reshape(toks, width).astype(F32)

    @pl.loop(0, 4)
    def _(a):
        product = val[pl.ds(a * 2, 2)].astype(F32) * cg_f[None]
        high, low = split(product.reshape(2 * toks, width))
        g = (dot(high, sum_heads) + dot(low, sum_heads)).T
        for par in range(2):
            wgt[a * 2 + par] = g[0:HEADS, par * toks:(par + 1) * toks]

    s = st[...]
    wg = wgt[...]
    top = jnp.max(s, axis=0)
    e = jnp.exp(s - top[None])
    stat_own[0:16] = top
    stat_own[16:32] = jnp.sum(e, axis=0)
    stat_own[32:48] = jnp.sum(e * wg, axis=0)

    @pl.loop(1, nt)
    def _(o):
        remote(stat_own, stat.at[o], st_send.at[o], st_recv.at[o], (me, tok_peer(o)))

    def st_sent():
        @pl.loop(1, nt)
        def _(o):
            wait_for(stat_own, st_send.at[o])

    pending.append(st_sent)

    pair = jnp.concatenate(
        [wf[held].reshape(32, width).astype(F32)]
        + [jnp.concatenate([bt[held].astype(F32)[par * 8 + k:par * 8 + k + 1] for k in range(width // LANES)], axis=1)
           for par in range(2)]
        + [jnp.zeros((LANES - TAIL, width), F32)], axis=0
    ).astype(BF16)
    wbp[...] = dot(pair, perm2[...]).astype(BF16)
    wt_c[...] = wbp[...].astype(F32).T.astype(BF16)

    stat[0] = stat_own[...]

    @pl.loop(1, nt)
    def _(o):
        wait_for(stat.at[o], st_recv.at[o])

    tops = stat[:, 0:16]
    highest = jnp.max(tops, axis=0)
    factor = jnp.exp(tops - highest[None])
    norm = jnp.sum(stat[:, 16:32] * factor, axis=0)
    mean = jnp.sum(stat[:, 32:48] * factor, axis=0) / norm
    weights_f = e * (jnp.exp(top - highest) / norm)[None]
    sg = weights_f * (wg - mean[None]) * scale
    wgt[...] = sg
    turned = weights_f.reshape(8 * HEADS, toks).T
    for v in range(8):
        wtr[v] = turned[:, v * HEADS:(v + 1) * HEADS].astype(BF16)

    for t in range(4):
        a = lax.rem((1 - core) * 2 + t, 4)
        g_val = jnp.zeros((48, width), F32)
        g_key = jnp.zeros((HEADS, LANES), F32)
        for v in (2 * a, 2 * a + 1):
            w = dot(wtr[v], spread[0:HEADS, :])
            value_grad = (w * cg_f).astype(BF16)
            g_val = g_val + dot(pixt[v], value_grad)
            high, low = split(wgt[v])
            g_key = g_key + dot(high, xo[v]) + dot(low, xo[v])
        to_core, to_far = a // 2, lax.rem(a, 2)
        for z in range(nz):
            gs[to_core, to_far, z] = g_val[0:grows, z * cw:(z + 1) * cw]
            gs[to_core, to_far, z, TAIL:TAIL + per, 0:LANES] = g_key[z * per:(z + 1) * per, :]

        if t == 1:
            remote(gs.at[1 - core], g1, g1_send, g1_recv, (sib, row))

    pending.append(lambda: wait_for(g1, g1_send))
    wait_for(g1, g1_recv)
    h1[...] = gs[core] + g1[...]
    opposite = (at(1 - far, zed, core), row)
    remote(h1.at[1 - far, :, 0:SPLIT], g2, g2_send, g2_recv, opposite)
    pending.append(lambda: wait_for(g2, g2_send))

    @pl.loop(1, nz)
    def _(o):
        z = lax.rem(zed + o, nz)
        remote(h1.at[:, z, SPLIT:], k3.at[o], k3_send.at[o], k3_recv.at[o], (at(far, z, core), row))

    def k3_sent():
        @pl.loop(1, nz)
        def _(o):
            wait_for(k3.at[0], k3_send.at[o])

    pending.append(k3_sent)

    total = jnp.zeros((toks, width), F32)
    for v in range(8):
        w = dot(wtr[v], spread[0:HEADS, :])
        total = total + w * val[v].astype(F32)
    ctx[...] = total.reshape(nt, OWN, width)
    cr[row] = ctx[row]

    wait_for(g2, g2_recv)
    h2[...] = h1[far, :, 0:SPLIT] + g2[...]

    @pl.loop(1, nz)
    def _(o):
        z = lax.rem(zed + o, nz)
        remote(h2.at[z], g3.at[o], g3_send.at[o], g3_recv.at[o], (at(far, z, core), row))

    def g3_sent():
        @pl.loop(1, nz)
        def _(o):
            wait_for(h2.at[0], g3_send.at[o])

    pending.append(g3_sent)

    @pl.loop(1, nt)
    def _(o):
        peer = tok_peer(o)
        remote(ctx.at[peer], cr.at[row], c_send.at[o], c_recv.at[o], (me, peer))

    def c_sent():
        @pl.loop(1, nt)
        def _(o):
            wait_for(ctx.at[0], c_send.at[o])

    pending.append(c_sent)

    def wait_c():
        @pl.loop(1, nt)
        def _(o):
            wait_for(cr.at[lax.rem(row - o + nt, nt)], c_recv.at[o])

    g3[0] = h2[zed]
    k3[0] = h1[:, zed, SPLIT:]

    @pl.loop(1, nz)
    def _(o):
        wait_for(k3.at[o], k3_recv.at[o])

    k4[...] = jnp.sum(k3[...], axis=0)
    remote(k4.at[1 - far], k5, k5_send, k5_recv, opposite)
    pending.append(lambda: wait_for(k5, k5_send))

    @pl.loop(1, nz)
    def _(o):
        wait_for(g3.at[o], g3_recv.at[o])

    gp[0:SPLIT, :] = jnp.sum(g3[...], axis=0)
    wait_for(k5, k5_recv)
    gp[SPLIT:, :] = k4[far] + k5[...]

    def to_owner(r, then_remote, then_local):
        itself = jnp.logical_and(mine == me, r == row)

        @pl.when(itself)
        def _():
            then_local()

        @pl.when(jnp.logical_not(itself))
        def _():
            then_remote()

    @pl.loop(0, nt)
    def _(r):
        to_owner(
            r,
            lambda: remote(gp, gt.at[zed], gt_send.at[r], gt_recv, (mine, r)),
            lambda: local(gp, gt.at[zed], gt_recv),
        )

    def gt_sent():
        @pl.loop(0, nt)
        def _(r):
            to_owner(r, lambda: wait_for(gp, gt_send.at[r]), lambda: None)

    pending.append(gt_sent)

    lines = iota((grows, cw), 0)
    high, low = split(jnp.where(lines < TAIL, gp[...], 0.0))
    keys_here = jnp.concatenate([gp[TAIL:TAIL + per, 0:LANES], jnp.zeros((16 - per, LANES), F32)], axis=0)
    key_high, key_low = split(keys_here)
    half = width // 2

    def products(c):
        lines_c = pl.ds(pl.multiple_of(c * half, half), half)
        left = wt_c[lines_c, 0:grows]
        part = dot(left, high) + dot(left, low)
        right = wbp[:, lines_c]
        key_part = (dot(key_high, right) + dot(key_low, right))[0:8]
        for y in range(2):
            for r in range(nt):
                k = y * nt + r
                ps[c, y, r, 0:cp, :] = part[k * cp:(k + 1) * cp]
                ps[c, y, r, cp:, :] = jnp.zeros((8, cw), F32)
                ps[c, y, r, cp:, 0:cp] = key_part[:, k * cp:(k + 1) * cp]

    products(1 - core)
    remote(ps.at[1 - core], p1, p1_send, p1_recv, (sib, row))
    pending.append(lambda: wait_for(p1, p1_send))
    products(core)
    wait_for(p1, p1_recv)
    q1[...] = ps[core] + p1[...]

    @pl.loop(1, nt)
    def _(o):
        peer = tok_peer(o)
        remote(q1.at[far, peer], p2.at[far, row], p2_send.at[far, o], p2_recv, (me, peer))

    @pl.loop(0, nt)
    def _(o):
        peer = tok_peer(o)
        remote(
            q1.at[1 - far, peer], p2.at[far, row], p2_send.at[1 - far, o], p2_recv,
            (at(1 - far, zed, core), peer),
        )

    local(q1.at[far, row], p2.at[far, row], p2_recv)

    def p2_sent():
        @pl.loop(1, nt)
        def _(o):
            wait_for(q1.at[0, 0], p2_send.at[far, o])

        @pl.loop(0, nt)
        def _(o):
            wait_for(q1.at[0, 0], p2_send.at[1 - far, o])

    pending.append(p2_sent)

    wait_c()
    context = jnp.sum(cr[...], axis=0).astype(BF16)
    agg_ref[...] = dot(context, ow[...]).astype(BF16)

    wait_for(p2, p2_recv)
    mine_c = jnp.sum(p2[...].reshape(2 * nt, cp + 8, cw), axis=0)
    key_cols = jnp.concatenate([mine_c[cp:, 0:LANES], jnp.zeros((LANES - 8, LANES), F32)], axis=0).T
    for z in range(nz):
        os_[z, 0:rpd, :] = mine_c[z * rpd:(z + 1) * rpd]
        os_[z, rpd:, 0:LANES] = key_cols[z * rpd:(z + 1) * rpd]
    local(os_.at[zed], or_.at[zed], o_recv)

    @pl.loop(1, nz)
    def _(o):
        z = lax.rem(zed + o, nz)
        remote(os_.at[z], or_.at[zed], o_send.at[o], o_recv, (at(far, z, core), row))

    def o_sent():
        @pl.loop(1, nz)
        def _(o):
            wait_for(os_.at[0], o_send.at[o])

    pending.append(o_sent)

    wait_for(gt, gt_recv)
    gk[...] = jnp.zeros((LANES, LANES), F32)
    for z in range(nz):
        gk[z * per:(z + 1) * per, :] = gt[z, TAIL:TAIL + per, 0:LANES]
        high, low = split(gt[z])
        lanes = slice(width + z * cw, width + (z + 1) * cw)
        gx[0:grows, lanes] = high
        gx[grows:, lanes] = low
    key_high, key_low = split(gk[...].T[0:grows])
    q_rows = (spread[...].astype(F32) * query).astype(BF16)
    high, low = split(dot(key_high, q_rows) + dot(key_low, q_rows))
    gx[0:grows, :width] = high
    gx[grows:, :width] = low

    both = dot_nt(gx[...], kv[...])
    table = both[0:grows] + both[grows:]
    gw_ref[0] = table[0:16]
    gw_ref[1] = table[16:32]
    gb_ref[...] = table[32:34]

    wait_for(or_, o_recv)
    small = iota((rpd, cw), 1)
    for z in range(nz):
        lanes = slice(z * cw, (z + 1) * cw)
        gkv_ref[:, width + z * cw:width + (z + 1) * cw] = or_[z, 0:rpd, :]
        keyed = or_[z, rpd:, :]
        spread_key = jnp.zeros((rpd, cw), F32)
        for h in range(per):
            spread_key = jnp.where((small >> bits(HEAD_DIM)) == h, keyed[:, h:h + 1], spread_key)
        gkv_ref[:, lanes] = spread_key * query[:, lanes]

    for done in pending:
        done()


def copy_kernel(*refs):
    for k in range(4):
        refs[4 + k][...] = refs[k][...]


def shards(nv, nt, patches, embed_w, embed_b, query, kv_w, out_w, cotangent):
    width = kv_w.shape[0]
    rpd = width // (nv * nt)
    nz = nv // 4
    cw = width // nz
    grows = -(-(TAIL + HEADS // nz) // 8) * 8
    cp = width // (4 * nt)
    toks = nt * OWN
    vmem = pl.BlockSpec(memory_space=pltpu.VMEM)
    hbm = pl.BlockSpec(memory_space=pl.ANY)
    dma = pltpu.SemaphoreType.DMA
    f32 = lambda *shape: pltpu.VMEM(shape, F32)
    bf16 = lambda *shape: pltpu.VMEM(shape, BF16)
    outs = pl.pallas_call(
        functools.partial(kernel, nv, nt),
        out_shape=(
            jax.ShapeDtypeStruct((OWN, width), BF16),
            jax.ShapeDtypeStruct((rpd, 2 * width), F32),
            jax.ShapeDtypeStruct(embed_w.shape, F32),
            jax.ShapeDtypeStruct(embed_b.shape, F32),
        ),
        in_specs=[hbm] * 7,
        out_specs=(vmem,) * 4,
        scratch_shapes=[
            pltpu.VMEM(patches.shape, BF16),
            pltpu.VMEM(embed_w.shape, BF16),
            pltpu.VMEM(embed_b.shape, BF16),
            pltpu.VMEM(query.shape, BF16),
            pltpu.VMEM(cotangent.shape, BF16),
            bf16(width, 2 * width),
            bf16(width, width),
            bf16(nt, 16, LANES),
            bf16(nt, 16, LANES),
            bf16(4, 4 * nt, LANES),
            bf16(4, 4 * nt, LANES),
            bf16(4, 2, PIX, width),
            bf16(4, 16, LANES),
            bf16(16, LANES),
            bf16(nt, OWN, width),
            bf16(2 * toks, width),
            bf16(8, toks, width),
            f32(8, HEADS, toks),
            f32(8, HEADS, toks),
            f32(48, toks),
            f32(nt, 48, toks),
            bf16(8, toks, HEADS),
            bf16(8, toks, LANES),
            bf16(8, 48, toks),
            f32(2, 2, nz, grows, cw),
            f32(2, nz, grows, cw),
            f32(2, nz, grows, cw),
            f32(nz, SPLIT, cw),
            f32(nz, SPLIT, cw),
            f32(nz, SPLIT, cw),
            f32(nz, 2, grows - SPLIT, cw),
            f32(2, grows - SPLIT, cw),
            f32(grows - SPLIT, cw),
            f32(grows, cw),
            f32(nz, grows, cw),
            f32(LANES, LANES),
            bf16(2 * grows, 2 * width),
            bf16(width, width),
            bf16(LANES, width),
            bf16(width, LANES),
            f32(2, 2, nt, cp + 8, cw),
            f32(2, nt, cp + 8, cw),
            f32(2, nt, cp + 8, cw),
            f32(2, nt, cp + 8, cw),
            f32(nz, 2 * rpd, cw),
            f32(nz, 2 * rpd, cw),
            f32(nt, OWN, width),
            f32(nt, OWN, width),
            bf16(LANES, width),
            dma((7,)), dma((nt,)), dma, dma((4,)), dma((4,)), dma((4,)), dma((4,)), dma((4,)), dma((4,)), dma((4,)), dma((4,)),
            dma((nt,)), dma((nt,)), dma((nt,)), dma((nt,)), dma, dma, dma, dma, dma((nz,)), dma((nz,)), dma((nz,)), dma((nz,)), dma, dma,
            dma((nt,)), dma, dma, dma, dma((2, nt)), dma, dma((nz,)), dma, dma((nt,)), dma((nt,)),
        ],
        compiler_params=pltpu.CompilerParams(
            collective_id=0, has_side_effects=True, vmem_limit_bytes=56 * 1024 * 1024
        ),
        cost_estimate=pl.CostEstimate(flops=5_000_000_000, bytes_accessed=8_000_000, transcendentals=20_000),
    )(patches, embed_w, embed_b, query, cotangent, kv_w, out_w)
    aggregated, grad_kv, grad_w, grad_b = pl.pallas_call(
        copy_kernel,
        out_shape=[jax.ShapeDtypeStruct(x.shape, x.dtype) for x in outs],
        in_specs=[vmem] * 4,
        out_specs=[vmem] * 4,
    )(*outs)
    return aggregated.reshape(cotangent.shape), grad_kv, grad_w, grad_b


def solution(mesh):
    return jax.shard_map(
        functools.partial(shards, mesh.shape["var"], mesh.shape["tok"]),
        mesh=mesh,
        in_specs=(
            P("var", "tok", None),
            P("var", None, None),
            P("var", None),
            P(),
            P(),
            P(),
            P("tok", "var", None),
        ),
        out_specs=(
            P("tok", "var", None),
            P(("var", "tok"), None),
            P("var", None, None),
            P("var", None),
        ),
        check_vma=False,
    )
```
